256 devices in a mesh: fsdp: 64 (over x, z, y_lo), tile: 4 (over y_hi, core).
Axes of the slice: x: 4, y: 4 (y_hi: 2, y_lo: 2; y = y_hi * 2 + y_lo), z: 8, core: 2. Of those that a mesh axis runs over, the one named last changes fastest.
Arguments:
- tokens: bfloat16 [65536, 1536], P('fsdp', 'tile'), may hold values from -6 to 6
- ln_gain: float32 [1536], replicated, may hold values from 0.25 to 1.75
- w_up: bfloat16 [1536, 6144], P('fsdp', 'tile'), may hold values from -0.15625 to 0.15625
- w_down: bfloat16 [6144, 1536], P('tile', 'fsdp'), may hold values from -0.078125 to 0.078125
- w_flux_in: bfloat16 [1536, 768], P('tile'), may hold values from -0.15625 to 0.15625
- w_flux_out: bfloat16 [768, 128], replicated, may hold values from -0.21875 to 0.21875
- ocean_state: bfloat16 [2048, 128, 256], P('fsdp', 'tile'), may hold values from -6 to 6
- land_mask: int32 [2048, 128], P('fsdp', 'tile'), may hold values from 0 to 1, as said below
- column_map: int32 [2048, 128], P('fsdp', 'tile'), may hold values from 0 to 65535, as said below
- w_couple: bfloat16 [128, 256], replicated, may hold values from -0.5 to 0.5
- dw_kernel: float32 [2, 7, 7, 256], replicated, may hold values from -0.875 to 0.875
- ocean_gain: float32 [2, 256], replicated, may hold values from 0.25 to 1.75
- w_pw1: bfloat16 [2, 256, 1024], replicated, may hold values from -0.375 to 0.375
- w_pw2: bfloat16 [2, 1024, 256], replicated, may hold values from -0.1875 to 0.1875
Outputs:
- atm_out: bfloat16 [65536, 1536], P('fsdp', 'tile')
- ocean_out: bfloat16 [2048, 128, 256], P('fsdp', 'tile')
The draws below stay inside these ranges and needn't reach their ends.
Inputs may be any that keep to these rules, and one draw needn't show every extreme that they name: `land_mask`: 0 or 1; land comes in regions of 8 x 8 cells whose ocean share varies. `column_map`: the column in grid row x names a token between (x // 32) * 1024 - 256 and (x // 32 + 1) * 1024 + 255.
All inputs are finite; a program needn't handle non-finite values.
Results may differ from the reference program's by a relative error of at most 0.014.
Values may be sent and summed in bfloat16 or wider, within the bound.
A program may use at most 128 MiB of HBM per device.

```python
import jax
import jax.numpy as jnp
from jax import lax

D = 1536
FF = 6144
FH = 768
FLX = 128
OC = 256
OH = 1024
KS = 7
BLOCKS = 2
TOK_DEV = 1024
OX = 32
RIM = 256
TOKENS = 65536
NOX = 2048
NOY = 128
N_FSDP = 64


def draw_land_mask(key, part):
    first, second = jax.random.split(jax.random.fold_in(key, 11))
    patch_rows = NOX // 8 + 1
    patch_cols = NOY // 8 + 1
    levels = jax.random.randint(first, (patch_rows, patch_cols), 2, 11)
    levels = jnp.repeat(jnp.repeat(levels, 8, axis=0), 8, axis=1)[:NOX, :NOY]
    cells = jax.random.randint(second, (NOX, NOY), 0, 10)
    return (cells < levels).astype(jnp.int32)


def draw_column_map(key, part):
    offsets = jax.random.randint(jax.random.fold_in(key, 23), (NOX, NOY), 0, TOK_DEV + 2 * RIM)
    band = jnp.arange(NOX, dtype=jnp.int32) // OX
    start = band * TOK_DEV - RIM
    return jnp.clip(start[:, None] + offsets, 0, TOKENS - 1).astype(jnp.int32)


def shard_levels(stream_key, extent, cuts, low, top_value):
    def one(axis_at, blocks):
        draws = jax.random.uniform(jax.random.fold_in(jax.random.fold_in(stream_key, 6), axis_at), (blocks,), jnp.float32, low / len(cuts), top_value / len(cuts))
        return jnp.repeat(jnp.exp(draws), extent[axis_at] // blocks).reshape((-1,) + (1,) * (len(extent) - axis_at - 1))

    level = one(*cuts[0])
    for cut in cuts[1:]:
        level = level * one(*cut)
    return level


def gaussian(stream_key, dims, scale, reach, shards=(), kind=jnp.bfloat16):
    level = shard_levels(stream_key, dims, shards, -0.22, 0.18) if shards else 1.0
    result = jax.random.normal(stream_key, dims, jnp.float32) * scale * level
    return jnp.minimum(jnp.maximum(result, -reach), reach).astype(kind)


def setup_inputs(seed: int = 0) -> dict:
    seeds = jax.random.split(jax.random.key(seed), 15)
    return {
        "tokens": gaussian(seeds[0], (TOKENS, D), 1.0, 6.0, ((0, 64), (1, 4))),
        "ln_gain": jnp.clip(1.0 + 0.15 * jax.random.normal(seeds[1], (D,), jnp.float32), 0.25, 1.75),
        "w_up": gaussian(seeds[2], (D, FF), D ** -0.5, 0.15625, ((0, 64), (1, 4))),
        "w_down": gaussian(seeds[3], (FF, D), FF ** -0.5, 0.078125, ((0, 4), (1, 64))),
        "w_flux_in": gaussian(seeds[4], (D, FH), D ** -0.5, 0.15625, ((0, 4),)),
        "w_flux_out": gaussian(seeds[5], (FH, FLX), FH ** -0.5, 0.21875),
        "ocean_state": gaussian(seeds[6], (NOX, NOY, OC), 1.0, 6.0, ((0, 64), (1, 4))),
        "land_mask": draw_land_mask(jax.random.fold_in(seeds[14], 71), 0),
        "column_map": draw_column_map(jax.random.fold_in(seeds[14], 71), 0),
        "w_couple": gaussian(seeds[9], (FLX, OC), FLX ** -0.5, 0.5),
        "dw_kernel": gaussian(seeds[10], (BLOCKS, KS, KS, OC), (KS * KS) ** -0.5, 0.875, (), jnp.float32),
        "ocean_gain": jnp.clip(1.0 + 0.15 * jax.random.normal(seeds[11], (BLOCKS, OC), jnp.float32), 0.25, 1.75),
        "w_pw1": gaussian(seeds[12], (BLOCKS, OC, OH), OC ** -0.5, 0.375),
        "w_pw2": gaussian(seeds[13], (BLOCKS, OH, OC), OH ** -0.5, 0.1875),
    }


def layer_norm(values, gain):
    center = values - lax.optimization_barrier(jnp.mean(values, axis=-1, keepdims=True))
    spread = lax.optimization_barrier(jnp.mean(center * center, axis=-1, keepdims=True))
    return center * lax.rsqrt(spread + 1e-06) * gain

def conv_block(padded, region_mask, kernel, gain, w_one, w_two):
    rows = padded.shape[0] - 6
    cols = padded.shape[1] - 6
    chans = padded.shape[2]
    total = jnp.zeros((rows, cols, chans), jnp.float32)
    for first in range(7):
        for second in range(7):
            total = total + padded[first:first + rows, second:second + cols].astype(jnp.float32) * kernel[first, second]
    pnorm = layer_norm(total, gain).astype(jnp.bfloat16).reshape(rows * cols, chans)
    inner = jax.nn.gelu(jnp.dot(pnorm, w_one, preferred_element_type=jnp.float32), approximate=True).astype(jnp.bfloat16)
    lowered = jnp.dot(inner, w_two, preferred_element_type=jnp.float32).reshape(rows, cols, chans)
    before = padded[3:3 + rows, 3:3 + cols].astype(jnp.float32)
    return (region_mask[..., None] * (before + lowered)).astype(jnp.bfloat16)

def reference(tokens, ln_gain, w_up, w_down, w_flux_in, w_flux_out, ocean_state, land_mask, column_map, w_couple, dw_kernel, ocean_gain, w_pw1, w_pw2):
    bands = tokens.reshape(N_FSDP, TOK_DEV, D)

    def one_band(band):
        normed = layer_norm(band.astype(jnp.float32), ln_gain).astype(jnp.bfloat16)
        hidden = jax.nn.gelu(jnp.dot(normed, w_up, preferred_element_type=jnp.float32), approximate=True).astype(jnp.bfloat16)
        atm_band = (band.astype(jnp.float32) + jnp.dot(hidden, w_down, preferred_element_type=jnp.float32)).astype(jnp.bfloat16)
        flux_hidden = jax.nn.gelu(jnp.dot(atm_band, w_flux_in, preferred_element_type=jnp.float32), approximate=True).astype(jnp.bfloat16)
        fluxes = jnp.dot(flux_hidden, w_flux_out, preferred_element_type=jnp.float32).astype(jnp.bfloat16)
        return (atm_band, fluxes)
    atm_bands, flux_bands = lax.map(one_band, bands)
    atm_out = atm_bands.reshape(TOKENS, D)
    fluxes = flux_bands.reshape(TOKENS, FLX)
    mask = land_mask.astype(jnp.float32)
    picked = jnp.take(fluxes, column_map.reshape(-1).astype(jnp.int32), axis=0)
    forcing = jnp.dot(picked, w_couple, preferred_element_type=jnp.float32).reshape(NOX, NOY, OC)
    state = (mask[..., None] * (ocean_state.astype(jnp.float32) + forcing)).astype(jnp.bfloat16)
    for block in range(BLOCKS):
        padded = jnp.pad(state, ((3, 3), (3, 3), (0, 0)))
        state = conv_block(padded, mask, dw_kernel[block], ocean_gain[block], w_pw1[block], w_pw2[block])
    return (atm_out, state)
```

```python
import functools

import jax
import jax.numpy as jnp
from jax import lax
from jax.experimental import pallas as pl
from jax.experimental.pallas import tpu as pltpu
from jax.sharding import PartitionSpec as P

MESH = pl.DeviceIdType.MESH
BF = jnp.bfloat16
F32 = jnp.float32
EPS = 1e-06
XS = 4
ZS = 8


def nt_dot(lhs, rhs):
    return lax.dot_general(lhs, rhs, (((1,), (1,)), ((), ())), preferred_element_type=F32)


def atmosphere_kernel(
    xs, zs,
    tok_ref, gain_ref, up_ref, down_ref, wfi_ref, wfo_ref,
    atm_ref, win_ref,
    yb, gw, tk, nm, hd, fi, sb, rb, acc, at, ao, wn,
    y_send, y_recv, ring_send, ring_recv, tok_send, tok_recv, fi_send, fi_recv,
    rs_send, rs_recv, at_send, at_recv, fx_send, fx_recv, rim_send, rim_recv,
):
    f = lax.axis_index("fsdp")
    t = lax.axis_index("tile")
    n_f = 2 * xs * zs
    x, z, yl = f // (2 * zs), (f // 2) % zs, f % 2
    yh, c = t // 2, t % 2
    yp = f + 1 - 2 * yl
    x_right = (f + 2 * zs) % n_f
    x_left = (f - 2 * zs + n_f) % n_f
    z_right = x * 2 * zs + ((z + 1) % zs) * 2 + yl
    z_left = x * 2 * zs + ((z + zs - 1) % zs) * 2 + yl
    f_next, f_prev = (f + 1) % n_f, (f + n_f - 1) % n_f
    t_core = yh * 2 + (1 - c)
    t_far = (1 - yh) * 2 + c
    t_diag = (1 - yh) * 2 + (1 - c)
    rows = tok_ref.shape[0]
    quarter = rows // 4
    feat = tok_ref.shape[1]
    width = gw.shape[-1]
    d_model = 4 * feat

    barrier = pltpu.get_barrier_semaphore()
    for other in (yp, x_right, x_left, z_right, z_left):
        pl.semaphore_signal(barrier, inc=1, device_id=(other, t), device_id_type=MESH)
    for other in (t_core, t_far, t_diag):
        pl.semaphore_signal(barrier, inc=1, device_id=(f, other), device_id_type=MESH)
    pl.semaphore_signal(barrier, inc=1, device_id=(f_prev, 3), device_id_type=MESH)
    pl.semaphore_signal(barrier, inc=1, device_id=(f_next, 0), device_id_type=MESH)
    edge = jnp.where(jnp.logical_or(t == 0, t == 3), 4, 0)
    pl.semaphore_wait(barrier, 8 + edge)

    def remote(src, dst, send, recv, device):
        return pltpu.make_async_remote_copy(
            src_ref=src, dst_ref=dst, send_sem=send, recv_sem=recv,
            device_id=device, device_id_type=MESH,
        )

    y_copies = [
        remote(ref, yb.at[w], y_send.at[w], y_recv.at[w], (yp, t))
        for w, ref in enumerate((up_ref, down_ref))
    ]
    for copy in y_copies:
        copy.start()
    shared = []
    for src, dst, send, recv in ((tok_ref, tk, tok_send, tok_recv), (wfi_ref, fi, fi_send, fi_recv)):
        far = remote(src, dst.at[t], send.at[1], recv.at[1], (f, t_far))
        near = remote(src, dst.at[t], send.at[0], recv.at[0], (f, t_core))
        relay = remote(dst.at[t_far], dst.at[t_far], send.at[2], recv.at[2], (f, t_core))
        shared.append((near, far, relay))
    for near, far, relay in shared:
        far.start()
        near.start()

    def ring_round(w, stream, stage, s):
        on_x = (stream == 0) == (stage == 0)
        n = xs if on_x else zs
        here = x if on_x else z
        last = s == n // 2 - 1
        copies = []
        for way in (0, 1):
            chunk = (here - s + n) % n if way == 0 else (here + s) % n
            if last:
                pieces = 2 * stream + way
            else:
                pieces = pl.ds(2 * stream, 2)
            if stage == 0:
                part = gw.at[w, pieces, chunk, z] if on_x else gw.at[w, pieces, x, chunk]
            else:
                part = gw.at[w, pieces, chunk] if on_x else gw.at[w, pieces, :, chunk]
            if on_x:
                target = x_right if way == 0 else x_left
            else:
                target = z_right if way == 0 else z_left
            at_sem = (((w * 2 + stream) * 2 + stage) * 4 + s) * 2 + way
            copies.append(
                remote(part, part, ring_send.at[at_sem], ring_recv.at[at_sem], (target, t))
            )
        return copies

    done = []

    def start(copies):
        for copy in copies:
            copy.start()
        done.extend(copies)
        return copies

    def arrive(copies):
        for copy in copies:
            copy.wait_recv()

    for w, ref in enumerate((up_ref, down_ref)):
        y_copies[w].wait_recv()
        for p in range(4):
            mine = ref[:, p * width : (p + 1) * width].astype(F32)
            other = yb[w, :, p * width : (p + 1) * width].astype(F32)
            first = jnp.where(yl == 0, mine, other)
            second = jnp.where(yl == 0, other, mine)
            gw[w, p, x, z] = jnp.concatenate([first, second], axis=0).astype(BF)
        if w == 0:
            up_small = [start(ring_round(0, b, 0, 0)) for b in (0, 1)]
    down_small = [start(ring_round(1, b, 0, 0)) for b in (0, 1)]
    tk[t] = tok_ref[...]
    fi[t] = wfi_ref[...]

    sizes = (xs // 2, zs // 2)
    for s in range(1, max(sizes)):
        for w, small in ((0, up_small), (1, down_small)):
            for b in (0, 1):
                if s < sizes[b]:
                    arrive(small[b])
                    small[b] = start(ring_round(w, b, 0, s))
    arrive(up_small[0])
    up_a = start(ring_round(0, 0, 1, 0))
    arrive(up_small[1])
    up_b = start(ring_round(0, 1, 1, 0))
    arrive(down_small[0])
    down_a = start(ring_round(1, 0, 1, 0))
    arrive(down_small[1])
    down_b = start(ring_round(1, 1, 1, 0))

    for near, far, relay in shared:
        far.wait_recv()
        relay.start()

    arrive(up_a)
    up_a = start(ring_round(0, 0, 1, 1)) if zs // 2 > 1 else []
    arrive(up_b)
    up_b = start(ring_round(0, 1, 1, 1)) if xs // 2 > 1 else []
    arrive(down_a)
    down_a = start(ring_round(1, 0, 1, 1)) if zs // 2 > 1 else []

    shared[0][0].wait_recv()
    shared[0][2].wait_recv()
    step = min(32, quarter)

    @pl.loop(0, rows // step)
    def _(i):
        span = pl.ds(pl.multiple_of(i * step, step), step)
        values = [tk[q, span, :].astype(F32) for q in range(4)]
        mean = sum(jnp.sum(v, axis=-1, keepdims=True) for v in values) / d_model
        centers = [v - mean for v in values]
        spread = sum(jnp.sum(v * v, axis=-1, keepdims=True) for v in centers) / d_model
        inverse = lax.rsqrt(spread + EPS)
        for q in range(4):
            gain = gain_ref[:, q * feat : (q + 1) * feat]
            nm[span, q * feat : (q + 1) * feat] = (centers[q] * inverse * gain).astype(BF)

    for s in range(2, zs // 2):
        arrive(up_a)
        up_a = start(ring_round(0, 0, 1, s))
        if s == 2:
            arrive(down_b)
            down_b = start(ring_round(1, 1, 1, 1)) if xs // 2 > 1 else []
        arrive(down_a)
        down_a = start(ring_round(1, 0, 1, s))
    if zs // 2 <= 2 and xs // 2 > 1:
        arrive(down_b)
        down_b = start(ring_round(1, 1, 1, 1))
    arrive(up_b)
    arrive(up_a)

    @pl.loop(0, 8)
    def _(i):
        half, block = i // 4, i % 4
        span = pl.ds(pl.multiple_of(block * quarter, quarter), quarter)
        rhs = jnp.concatenate(
            [gw[0, half * 2 + k].reshape(d_model, width) for k in (0, 1)], axis=1
        )
        pre = jnp.dot(nm[span, :], rhs, preferred_element_type=F32)
        hd[half, span, :] = jax.nn.gelu(pre, approximate=True).astype(BF)

    arrive(down_b)
    arrive(down_a)

    def partial(block, half):
        span = pl.ds(pl.multiple_of(block * quarter, quarter), quarter)
        lhs = jnp.concatenate([hd[0, span, :], hd[1, span, :]], axis=1)
        part = pl.ds(half * (xs // 2), xs // 2)
        rhs = jnp.concatenate(
            [gw[1, p, part].reshape(d_model // 2, width) for p in range(4)], axis=1
        )
        return nt_dot(lhs, rhs)

    def sums(k, half, target):
        return remote(
            sb.at[k, half], rb.at[k, half], rs_send.at[2 * k + half], rs_recv.at[2 * k + half],
            (f, target),
        )

    to_core = [sums(0, half, t_core) for half in (0, 1)]
    to_far = [sums(1, half, t_far) for half in (0, 1)]
    to_core2 = [sums(2, half, t_core) for half in (0, 1)]

    for half in (0, 1):
        sb[0, half] = partial(t_diag, half).astype(BF)
        to_core[half].start()
    for half in (0, 1):
        acc[half] = partial(t_far, half)
        to_core[half].wait_recv()
        sb[1, half] = (acc[half] + rb[0, half].astype(F32)).astype(BF)
        to_far[half].start()
    for half in (0, 1):
        sb[2, half] = partial(t_core, half).astype(BF)
        to_core2[half].start()
    for half in (0, 1):
        acc[half] = partial(t, half)
    mine = pl.ds(pl.multiple_of(t * quarter, quarter), quarter)
    for half in (0, 1):
        to_core2[half].wait_recv()
        to_far[half].wait_recv()
        for k in (0, 1):
            q = 2 * half + k
            cols = slice(k * feat, (k + 1) * feat)
            delta = acc[half, :, cols] + rb[2, half, :, cols].astype(F32) + rb[1, half, :, cols].astype(F32)
            at[q] = (tk[q, mine, :].astype(F32) + delta).astype(BF)

    at_copies = []
    for k in range(1, 4):
        q = (t + k) % 4
        at_copies.append(remote(at.at[q], ao.at[t], at_send.at[k - 1], at_recv.at[k - 1], (f, q)))
        at_copies[-1].start()
    ao[t] = at[t]

    shared[1][0].wait_recv()
    shared[1][2].wait_recv()
    pre = jnp.dot(
        jnp.concatenate([at[q] for q in range(4)], axis=1),
        fi[...].reshape(d_model, fi.shape[-1]),
        preferred_element_type=F32,
    )
    flux_hidden = jax.nn.gelu(pre, approximate=True).astype(BF)
    wn[1 + t] = jnp.dot(flux_hidden, wfo_ref[...], preferred_element_type=F32).astype(BF)
    fx_copies = []
    for k in range(1, 4):
        fx_copies.append(
            remote(wn.at[1 + t], wn.at[1 + t], fx_send.at[k - 1], fx_recv.at[k - 1], (f, (t + k) % 4))
        )
        fx_copies[-1].start()

    def rim(slot, source, target):
        return [
            remote(wn.at[source], wn.at[slot], rim_send.at[q], rim_recv.at[slot // 5], (target, q))
            for q in range(4)
        ]

    low = rim(0, 4, f_next)
    high = rim(5, 1, f_prev)

    @pl.when(t == 3)
    def _():
        for copy in low:
            copy.start()

    @pl.when(t == 0)
    def _():
        for copy in high:
            copy.start()

    for copy in at_copies:
        copy.wait_recv()
    for q in range(4):
        atm_ref[pl.ds(q * quarter, quarter), :] = ao[q]
    for copy in fx_copies:
        copy.wait_recv()
    low[0].wait_recv()
    high[0].wait_recv()
    win_ref[...] = wn[...]

    @pl.when(t == 3)
    def _():
        for copy in low:
            copy.wait_send()

    @pl.when(t == 0)
    def _():
        for copy in high:
            copy.wait_send()

    for copy in y_copies + done + at_copies + fx_copies + to_core + to_far + to_core2:
        copy.wait_send()
    for trio in shared:
        for copy in trio:
            copy.wait_send()


def atmosphere(xs, zs, tokens, ln_gain, w_up, w_down, w_flux_in, w_flux_out):
    rows, feat = tokens.shape
    d_model = 4 * feat
    shard, hidden = w_up.shape
    width = hidden // 4
    fh, flx = w_flux_out.shape
    quarter = rows // 4
    dma = pltpu.SemaphoreType.DMA
    vm = pl.BlockSpec(memory_space=pltpu.VMEM)
    return pl.pallas_call(
        functools.partial(atmosphere_kernel, xs, zs),
        out_shape=(
            jax.ShapeDtypeStruct((rows, feat), BF),
            jax.ShapeDtypeStruct((6, quarter, flx), BF),
        ),
        in_specs=[vm] * 6,
        out_specs=(vm, vm),
        scratch_shapes=[
            pltpu.VMEM((2, shard, hidden), BF),
            pltpu.VMEM((2, 4, xs, zs, 2 * shard, width), BF),
            pltpu.VMEM((4, rows, feat), BF),
            pltpu.VMEM((rows, d_model), BF),
            pltpu.VMEM((2, rows, hidden // 2), BF),
            pltpu.VMEM((4, feat, fh), BF),
            pltpu.VMEM((3, 2, quarter, d_model // 2), BF),
            pltpu.VMEM((3, 2, quarter, d_model // 2), BF),
            pltpu.VMEM((2, quarter, d_model // 2), F32),
            pltpu.VMEM((4, quarter, feat), BF),
            pltpu.VMEM((4, quarter, feat), BF),
            pltpu.VMEM((6, quarter, flx), BF),
            dma((2,)), dma((2,)), dma((64,)), dma((64,)),
            dma((3,)), dma((3,)), dma((3,)), dma((3,)),
            dma((6,)), dma((6,)), dma((3,)), dma((3,)),
            dma((3,)), dma((3,)), dma((4,)), dma((2,)),
        ],
        compiler_params=pltpu.CompilerParams(
            collective_id=0, has_side_effects=True, vmem_limit_bytes=58 * 1024 * 1024
        ),
        name="atmosphere",
    )(tokens, ln_gain.reshape(1, d_model), w_up, w_down.T, w_flux_in, w_flux_out)


def with_halo(block, sides, width):
    for axis, dim in sides:
        count = lax.axis_size(axis)
        forward = [(i, i + 1) for i in range(count - 1)]
        backward = [(target, source) for source, target in forward]
        low = lax.ppermute(
            lax.slice_in_dim(block, block.shape[dim] - width, None, axis=dim), axis, forward
        )
        high = lax.ppermute(lax.slice_in_dim(block, 0, width, axis=dim), axis, backward)
        block = jnp.concatenate([low, block, high], axis=dim)
    return block


def layer_norm(values, gain):
    center = values - jnp.mean(values, axis=-1, keepdims=True)
    spread = jnp.mean(center * center, axis=-1, keepdims=True)
    return center * lax.rsqrt(spread + EPS) * gain


def conv_block(padded, region_mask, kernel, gain, w_one, w_two):
    rows = padded.shape[0] - 6
    cols = padded.shape[1] - 6
    chans = padded.shape[2]
    total = jnp.zeros((rows, cols, chans), jnp.float32)
    for first in range(7):
        for second in range(7):
            total = (
                total
                + padded[first : first + rows, second : second + cols].astype(jnp.float32)
                * kernel[first, second]
            )
    pnorm = layer_norm(total, gain).astype(jnp.bfloat16).reshape(rows * cols, chans)
    inner = jax.nn.gelu(
        jnp.dot(pnorm, w_one, preferred_element_type=jnp.float32), approximate=True
    ).astype(jnp.bfloat16)
    lowered = jnp.dot(inner, w_two, preferred_element_type=jnp.float32).reshape(rows, cols, chans)
    before = padded[3 : 3 + rows, 3 : 3 + cols].astype(jnp.float32)
    return (region_mask[..., None] * (before + lowered)).astype(jnp.bfloat16)


def body(
    tokens,
    ln_gain,
    w_up,
    w_down,
    w_flux_in,
    w_flux_out,
    ocean_state,
    land_mask,
    column_map,
    w_couple,
    dw_kernel,
    ocean_gain,
    w_pw1,
    w_pw2,
):
    band_rows = tokens.shape[0]
    rim_rows = band_rows // 4
    atm_out, window = atmosphere(XS, ZS, tokens, ln_gain, w_up, w_down, w_flux_in, w_flux_out)
    window = window.reshape(6 * rim_rows, window.shape[-1])
    band = lax.axis_index("fsdp")
    local_index = (column_map - (band * band_rows - rim_rows)).reshape(-1)
    picked = jnp.take(window, local_index, axis=0)
    grid_rows = ocean_state.shape[0]
    grid_cols = ocean_state.shape[1]
    chans = ocean_state.shape[2]
    forcing = jnp.dot(picked, w_couple, preferred_element_type=jnp.float32).reshape(
        grid_rows, grid_cols, chans
    )
    mask = land_mask.astype(jnp.float32)
    state = (mask[..., None] * (ocean_state.astype(jnp.float32) + forcing)).astype(jnp.bfloat16)
    count = dw_kernel.shape[0]
    for block in range(count):
        padded = with_halo(state, (("fsdp", 0), ("tile", 1)), 3)
        state = conv_block(
            padded, mask, dw_kernel[block], ocean_gain[block], w_pw1[block], w_pw2[block]
        )
    return (atm_out, state)


def solution(mesh):
    placed = (
        P("fsdp", "tile"),
        P(),
        P("fsdp", "tile"),
        P("tile", "fsdp"),
        P("tile", None),
        P(),
        P("fsdp", "tile", None),
        P("fsdp", "tile"),
        P("fsdp", "tile"),
        P(),
        P(),
        P(),
        P(),
        P(),
    )
    return jax.shard_map(
        body,
        mesh=mesh,
        in_specs=placed,
        out_specs=(P("fsdp", "tile"), P("fsdp", "tile", None)),
        check_vma=False,
    )
```

```python
import functools

import jax
import jax.numpy as jnp
from jax import lax
from jax.experimental import pallas as pl
from jax.experimental.pallas import tpu as pltpu
from jax.sharding import PartitionSpec as P
import numpy as np

MESH = pl.DeviceIdType.MESH
BF = jnp.bfloat16
F32 = jnp.float32
EPS = 1e-06
XS = 4
ZS = 8


def nt_dot(lhs, rhs):
    return lax.dot_general(lhs, rhs, (((1,), (1,)), ((), ())), preferred_element_type=F32)


def ocean_prepare(first, mask_ref, map_ref, taps_ref, mk, oh, wb):
    grid_rows, grid_cols = map_ref.shape
    tiles = oh.shape[1] // 128

    @pl.loop(0, grid_rows)
    def _(r):
        square = (grid_cols, grid_cols)
        eye = (
            lax.broadcasted_iota(jnp.int32, square, 0) == lax.broadcasted_iota(jnp.int32, square, 1)
        ).astype(F32)
        ones = jnp.ones((grid_cols, 128), BF)

        def upright(line):
            return jnp.dot((eye * line).astype(BF), ones, preferred_element_type=F32)

        index = map_ref[pl.ds(r, 1), :] - first
        high = upright((index >> 5).astype(F32))
        low = upright((index & 31).astype(F32))
        index_up = high * 32.0 + low
        span = pl.ds(pl.multiple_of(r * grid_cols, grid_cols), grid_cols)
        mk[span, :] = upright(mask_ref[pl.ds(r, 1), :].astype(F32))
        lane = lax.broadcasted_iota(jnp.int32, (grid_cols, 128), 1).astype(F32)
        for k in range(tiles):
            oh[span, k * 128 : (k + 1) * 128] = jnp.where(
                index_up == lane + 128.0 * k, 1.0, 0.0
            ).astype(BF)

    for k in range(taps_ref.shape[0]):
        for a in range(7):
            for b in range(7):
                wb[k, a, b] = jnp.broadcast_to(taps_ref[k, a, b : b + 1, :], wb.shape[3:])


def ocean(
    f, t, n_f, f_prev, f_next, remote, wn, sea_ref, couple_ref, sgain_ref, one_ref, two_ref,
    pick_ref, place_ref, out_ref, mk, oh, wb, st, pd, sh, cv, pk, rw, rn, halo_send, halo_recv,
):
    grid_rows, grid_cols, chans = sea_ref.shape
    cells = 8 * grid_cols
    wide = pd.shape[1]
    t_next, t_prev = (t + 1) % 4, (t + 3) % 4
    edge = 3 * grid_cols

    def masked(span, values):
        return (jnp.concatenate([mk[span, :]] * (chans // 128), axis=1) * values).astype(BF)

    def keep(k, i, span, values):
        st[k, span, :] = values
        pd[pl.ds(3 + i * 8, 8), 8 : 8 + grid_cols, :] = values.astype(F32).reshape(
            8, grid_cols, chans
        )

    @pl.loop(0, grid_rows // 8)
    def _(i):
        span = pl.ds(pl.multiple_of(i * cells, cells), cells)
        picked = jnp.dot(
            oh[span, :], wn[...].reshape(oh.shape[1], wn.shape[2]), preferred_element_type=F32
        ).astype(BF)
        forcing = jnp.dot(picked, couple_ref[...], preferred_element_type=F32)
        before = sea_ref[pl.ds(i * 8, 8)].reshape(cells, chans).astype(F32)
        keep(0, i, span, masked(span, before + forcing))

    for k in range(2):
        pk[k] = jnp.dot(pick_ref[...], st[k], preferred_element_type=F32).astype(BF)
        last = grid_rows * grid_cols - edge
        moves = [
            (st.at[k, pl.ds(last, edge)], rn.at[k, 0], (f_next, t)),
            (st.at[k, pl.ds(0, edge)], rn.at[k, 1], (f_prev, t)),
            (pk.at[k, pl.ds(0, 96)], rw.at[k, pl.ds(0, 96)], (f, t_next)),
            (pk.at[k, pl.ds(96, 96)], rw.at[k, pl.ds(96, 96)], (f, t_prev)),
        ]
        corner = 192
        for fd in (f_prev, f_next):
            for td in (t_prev, t_next):
                part = pl.ds(corner, 16)
                moves.append((pk.at[k, part], rw.at[k, part], (fd, td)))
                corner += 16
        copies = [
            remote(src, dst, halo_send.at[k * 8 + j], halo_recv.at[k * 8 + j], device)
            for j, (src, dst, device) in enumerate(moves)
        ]
        for copy in copies:
            copy.start()
        for copy in copies:
            copy.wait_recv()
        above, below, left, right = f > 0, f < n_f - 1, t > 0, t < 3

        def valid(flag, values):
            return jnp.where(flag, values.astype(F32), 0.0)

        pd[0:3, 8 : 8 + grid_cols, :] = valid(above, rn[k, 0]).reshape(3, grid_cols, chans)
        pd[3 + grid_rows : 6 + grid_rows, 8 : 8 + grid_cols, :] = valid(below, rn[k, 1]).reshape(
            3, grid_cols, chans
        )
        flags = (
            left,
            right,
            jnp.logical_and(below, right),
            jnp.logical_and(below, left),
            jnp.logical_and(above, right),
            jnp.logical_and(above, left),
        )
        starts = (0, 96, 192, 208, 224, 240, 256)
        came = jnp.concatenate(
            [valid(flags[j], rw[k, starts[j] : starts[j + 1]]) for j in range(6)], axis=0
        ).astype(BF)
        strips = jnp.dot(place_ref[...], came, preferred_element_type=F32)
        count = (grid_rows + 6) * 8
        pd[:, 0:8, :] = strips[:count].reshape(grid_rows + 6, 8, chans)
        pd[:, wide - 8 : wide, :] = strips[count:].reshape(grid_rows + 6, 8, chans)

        @pl.loop(0, grid_rows + 6)
        def _(r):
            line = pd[r]
            for b in range(7):
                sh[b, r] = line[5 + b : 5 + b + grid_cols].reshape(grid_cols // 8, 8, chans)

        @pl.loop(0, (grid_rows // 4) * (chans // 128))
        def _(i):
            first = (i // (chans // 128)) * 4
            lanes = pl.ds(pl.multiple_of((i % (chans // 128)) * 128, 128), 128)
            totals = [jnp.zeros((grid_cols // 8, 8, 128), F32) for _ in range(4)]
            for b in range(7):
                weights = [wb[k, a, b, :, lanes] for a in range(7)]
                for r in range(10):
                    values = sh[b, first + r, :, :, lanes]
                    for j in range(4):
                        if 0 <= r - j < 7:
                            totals[j] = totals[j] + values * weights[r - j]
            for j in range(4):
                cv[first + j, :, :, lanes] = totals[j]

        @pl.loop(0, grid_rows // 8)
        def _(i):
            span = pl.ds(pl.multiple_of(i * cells, cells), cells)
            total = cv[pl.ds(i * 8, 8)].reshape(cells, chans)
            center = total - jnp.mean(total, axis=-1, keepdims=True)
            spread = jnp.mean(center * center, axis=-1, keepdims=True)
            pnorm = (center * lax.rsqrt(spread + EPS) * sgain_ref[k : k + 1, :]).astype(BF)
            inner = jax.nn.gelu(
                jnp.dot(pnorm, one_ref[k], preferred_element_type=F32), approximate=True
            ).astype(BF)
            lowered = jnp.dot(inner, two_ref[k], preferred_element_type=F32)
            values = masked(span, st[k, span, :].astype(F32) + lowered)
            if k == 0:
                keep(1, i, span, values)
            else:
                out_ref[pl.ds(i * 8, 8)] = values.reshape(8, grid_cols, chans)

        for copy in copies:
            copy.wait_send()


def halo_matrices(grid_rows, grid_cols):
    pick = np.zeros((256, grid_rows * grid_cols), np.float32)
    place = np.zeros((2 * (grid_rows + 6) * 8, 256), np.float32)
    side = (grid_rows + 6) * 8
    for r in range(grid_rows):
        for j in range(3):
            pick[r * 3 + j, r * grid_cols + grid_cols - 3 + j] = 1
            pick[96 + r * 3 + j, r * grid_cols + j] = 1
            place[(3 + r) * 8 + 5 + j, r * 3 + j] = 1
            place[side + (3 + r) * 8 + j, 96 + r * 3 + j] = 1
    corner = 192
    for down in (0, 1):
        for right in (0, 1):
            for i in range(3):
                for j in range(3):
                    row = grid_rows - 3 + i if down else i
                    col = grid_cols - 3 + j if right else j
                    pick[corner + i * 3 + j, row * grid_cols + col] = 1
                    to_row = i if down else grid_rows + 3 + i
                    to = to_row * 8 + 5 + j if right else side + to_row * 8 + j
                    place[to, corner + i * 3 + j] = 1
            corner += 16
    return jnp.asarray(pick, BF), jnp.asarray(place, BF)


def atmosphere_kernel(
    xs, zs,
    tok_ref, gain_ref, up_ref, down_ref, wfi_ref, wfo_ref,
    sea_ref, mask_ref, map_ref, couple_ref, taps_ref, sgain_ref, one_ref, two_ref, pick_ref, place_ref,
    atm_ref, out_ref,
    yb, gw, tk, nm, hd, fi, sb, rb, acc, at, ao, wn,
    y_send, y_recv, ring_send, ring_recv, tok_send, tok_recv, fi_send, fi_recv,
    rs_send, rs_recv, at_send, at_recv, fx_send, fx_recv, rim_send, rim_recv,
    mk, oh, wb, st, pd, sh, cv, pk, rw, rn, halo_send, halo_recv,
):
    f = lax.axis_index("fsdp")
    t = lax.axis_index("tile")
    n_f = 2 * xs * zs
    x, z, yl = f // (2 * zs), (f // 2) % zs, f % 2
    yh, c = t // 2, t % 2
    yp = f + 1 - 2 * yl
    x_right = (f + 2 * zs) % n_f
    x_left = (f - 2 * zs + n_f) % n_f
    z_right = x * 2 * zs + ((z + 1) % zs) * 2 + yl
    z_left = x * 2 * zs + ((z + zs - 1) % zs) * 2 + yl
    f_next, f_prev = (f + 1) % n_f, (f + n_f - 1) % n_f
    t_core = yh * 2 + (1 - c)
    t_far = (1 - yh) * 2 + c
    t_diag = (1 - yh) * 2 + (1 - c)
    rows = tok_ref.shape[0]
    quarter = rows // 4
    feat = tok_ref.shape[1]
    width = gw.shape[-1]
    d_model = 4 * feat

    barrier = pltpu.get_barrier_semaphore()
    for other in (x_right, x_left, z_right, z_left):
        pl.semaphore_signal(barrier, inc=1, device_id=(other, t), device_id_type=MESH)
    for other in (t_core, t_far, t_diag):
        pl.semaphore_signal(barrier, inc=1, device_id=(f, other), device_id_type=MESH)
    for other in (f_prev, f_next):
        for q in range(4):
            pl.semaphore_signal(barrier, inc=1, device_id=(other, q), device_id_type=MESH)
    pl.semaphore_wait(barrier, 15)

    def remote(src, dst, send, recv, device):
        return pltpu.make_async_remote_copy(
            src_ref=src, dst_ref=dst, send_sem=send, recv_sem=recv,
            device_id=device, device_id_type=MESH,
        )

    y_copies = [
        remote(ref, yb.at[w], y_send.at[w], y_recv.at[w], (yp, t))
        for w, ref in enumerate((up_ref, down_ref))
    ]
    for copy in y_copies:
        copy.start()
    shared = []
    for src, dst, send, recv in ((tok_ref, tk, tok_send, tok_recv), (wfi_ref, fi, fi_send, fi_recv)):
        far = remote(src, dst.at[t], send.at[1], recv.at[1], (f, t_far))
        near = remote(src, dst.at[t], send.at[0], recv.at[0], (f, t_core))
        relay = remote(dst.at[t_far], dst.at[t_far], send.at[2], recv.at[2], (f, t_core))
        shared.append((near, far, relay))
    for near, far, relay in shared:
        far.start()
        near.start()

    def ring_round(w, stream, stage, s):
        on_x = (stream == 0) == (stage == 0)
        n = xs if on_x else zs
        here = x if on_x else z
        last = s == n // 2 - 1
        copies = []
        for way in (0, 1):
            chunk = (here - s + n) % n if way == 0 else (here + s) % n
            if last:
                pieces = 2 * stream + way
            else:
                pieces = pl.ds(2 * stream, 2)
            if stage == 0:
                part = gw.at[w, pieces, chunk, z] if on_x else gw.at[w, pieces, x, chunk]
            else:
                part = gw.at[w, pieces, chunk] if on_x else gw.at[w, pieces, :, chunk]
            if on_x:
                target = x_right if way == 0 else x_left
            else:
                target = z_right if way == 0 else z_left
            at_sem = (((w * 2 + stream) * 2 + stage) * 4 + s) * 2 + way
            copies.append(
                remote(part, part, ring_send.at[at_sem], ring_recv.at[at_sem], (target, t))
            )
        return copies

    done = []

    def start(copies):
        for copy in copies:
            copy.start()
        done.extend(copies)
        return copies

    def arrive(copies):
        for copy in copies:
            copy.wait_recv()

    for w, ref in enumerate((up_ref, down_ref)):
        y_copies[w].wait_recv()
        for p in range(4):
            mine = ref[:, p * width : (p + 1) * width].astype(F32)
            other = yb[w, :, p * width : (p + 1) * width].astype(F32)
            first = jnp.where(yl == 0, mine, other)
            second = jnp.where(yl == 0, other, mine)
            gw[w, p, x, z] = jnp.concatenate([first, second], axis=0).astype(BF)
        if w == 0:
            up_small = [start(ring_round(0, b, 0, 0)) for b in (0, 1)]
    down_small = [start(ring_round(1, b, 0, 0)) for b in (0, 1)]
    tk[t] = tok_ref[...]
    fi[t] = wfi_ref[...]

    sizes = (xs // 2, zs // 2)
    for s in range(1, max(sizes)):
        for w, small in ((0, up_small), (1, down_small)):
            for b in (0, 1):
                if s < sizes[b]:
                    arrive(small[b])
                    small[b] = start(ring_round(w, b, 0, s))
    arrive(up_small[0])
    up_a = start(ring_round(0, 0, 1, 0))
    arrive(up_small[1])
    up_b = start(ring_round(0, 1, 1, 0))
    arrive(down_small[0])
    down_a = start(ring_round(1, 0, 1, 0))
    arrive(down_small[1])
    down_b = start(ring_round(1, 1, 1, 0))

    for near, far, relay in shared:
        far.wait_recv()
        relay.start()

    arrive(up_a)
    up_a = start(ring_round(0, 0, 1, 1)) if zs // 2 > 1 else []
    arrive(up_b)
    up_b = start(ring_round(0, 1, 1, 1)) if xs // 2 > 1 else []
    arrive(down_a)
    down_a = start(ring_round(1, 0, 1, 1)) if zs // 2 > 1 else []

    shared[0][0].wait_recv()
    shared[0][2].wait_recv()
    step = min(32, quarter)

    @pl.loop(0, rows // step)
    def _(i):
        span = pl.ds(pl.multiple_of(i * step, step), step)
        values = [tk[q, span, :].astype(F32) for q in range(4)]
        mean = sum(jnp.sum(v, axis=-1, keepdims=True) for v in values) / d_model
        centers = [v - mean for v in values]
        spread = sum(jnp.sum(v * v, axis=-1, keepdims=True) for v in centers) / d_model
        inverse = lax.rsqrt(spread + EPS)
        for q in range(4):
            gain = gain_ref[:, q * feat : (q + 1) * feat]
            nm[span, q * feat : (q + 1) * feat] = (centers[q] * inverse * gain).astype(BF)

    ocean_prepare(f * rows - quarter, mask_ref, map_ref, taps_ref, mk, oh, wb)

    for s in range(2, zs // 2):
        arrive(up_a)
        up_a = start(ring_round(0, 0, 1, s))
        if s == 2:
            arrive(down_b)
            down_b = start(ring_round(1, 1, 1, 1)) if xs // 2 > 1 else []
        arrive(down_a)
        down_a = start(ring_round(1, 0, 1, s))
    if zs // 2 <= 2 and xs // 2 > 1:
        arrive(down_b)
        down_b = start(ring_round(1, 1, 1, 1))
    arrive(up_b)
    arrive(up_a)

    @pl.loop(0, 8)
    def _(i):
        half, block = i // 4, i % 4
        span = pl.ds(pl.multiple_of(block * quarter, quarter), quarter)
        rhs = jnp.concatenate(
            [gw[0, half * 2 + k].reshape(d_model, width) for k in (0, 1)], axis=1
        )
        pre = jnp.dot(nm[span, :], rhs, preferred_element_type=F32)
        hd[half, span, :] = jax.nn.gelu(pre, approximate=True).astype(BF)

    arrive(down_b)
    arrive(down_a)

    def partial(block, half):
        span = pl.ds(pl.multiple_of(block * quarter, quarter), quarter)
        lhs = jnp.concatenate([hd[0, span, :], hd[1, span, :]], axis=1)
        part = pl.ds(half * (xs // 2), xs // 2)
        rhs = jnp.concatenate(
            [gw[1, p, part].reshape(d_model // 2, width) for p in range(4)], axis=1
        )
        return nt_dot(lhs, rhs)

    def sums(k, half, target):
        return remote(
            sb.at[k, half], rb.at[k, half], rs_send.at[2 * k + half], rs_recv.at[2 * k + half],
            (f, target),
        )

    to_core = [sums(0, half, t_core) for half in (0, 1)]
    to_far = [sums(1, half, t_far) for half in (0, 1)]
    to_core2 = [sums(2, half, t_core) for half in (0, 1)]

    for half in (0, 1):
        sb[0, half] = partial(t_diag, half).astype(BF)
        to_core[half].start()
    for half in (0, 1):
        acc[half] = partial(t_far, half)
        to_core[half].wait_recv()
        sb[1, half] = (acc[half] + rb[0, half].astype(F32)).astype(BF)
        to_far[half].start()
    for half in (0, 1):
        sb[2, half] = partial(t_core, half).astype(BF)
        to_core2[half].start()
    for half in (0, 1):
        acc[half] = partial(t, half)
    mine = pl.ds(pl.multiple_of(t * quarter, quarter), quarter)
    for half in (0, 1):
        to_core2[half].wait_recv()
        to_far[half].wait_recv()
        for k in (0, 1):
            q = 2 * half + k
            cols = slice(k * feat, (k + 1) * feat)
            delta = acc[half, :, cols] + rb[2, half, :, cols].astype(F32) + rb[1, half, :, cols].astype(F32)
            at[q] = (tk[q, mine, :].astype(F32) + delta).astype(BF)

    at_copies = []
    for k in range(1, 4):
        q = (t + k) % 4
        at_copies.append(remote(at.at[q], ao.at[t], at_send.at[k - 1], at_recv.at[k - 1], (f, q)))
        at_copies[-1].start()
    ao[t] = at[t]

    shared[1][0].wait_recv()
    shared[1][2].wait_recv()
    pre = jnp.dot(
        jnp.concatenate([at[q] for q in range(4)], axis=1),
        fi[...].reshape(d_model, fi.shape[-1]),
        preferred_element_type=F32,
    )
    flux_hidden = jax.nn.gelu(pre, approximate=True).astype(BF)
    wn[1 + t] = jnp.dot(flux_hidden, wfo_ref[...], preferred_element_type=F32).astype(BF)
    fx_copies = []
    for k in range(1, 4):
        fx_copies.append(
            remote(wn.at[1 + t], wn.at[1 + t], fx_send.at[k - 1], fx_recv.at[k - 1], (f, (t + k) % 4))
        )
        fx_copies[-1].start()

    def rim(slot, source, target):
        return [
            remote(wn.at[source], wn.at[slot], rim_send.at[q], rim_recv.at[slot // 5], (target, q))
            for q in range(4)
        ]

    low = rim(0, 4, f_next)
    high = rim(5, 1, f_prev)

    @pl.when(t == 3)
    def _():
        for copy in low:
            copy.start()

    @pl.when(t == 0)
    def _():
        for copy in high:
            copy.start()

    for copy in at_copies:
        copy.wait_recv()
    for q in range(4):
        atm_ref[pl.ds(q * quarter, quarter), :] = ao[q]
    for copy in fx_copies:
        copy.wait_recv()
    low[0].wait_recv()
    high[0].wait_recv()
    ocean(
        f, t, n_f, f_prev, f_next, remote, wn, sea_ref, couple_ref, sgain_ref, one_ref, two_ref,
        pick_ref, place_ref, out_ref, mk, oh, wb, st, pd, sh, cv, pk, rw, rn, halo_send, halo_recv,
    )

    @pl.when(t == 3)
    def _():
        for copy in low:
            copy.wait_send()

    @pl.when(t == 0)
    def _():
        for copy in high:
            copy.wait_send()

    for copy in y_copies + done + at_copies + fx_copies + to_core + to_far + to_core2:
        copy.wait_send()
    for trio in shared:
        for copy in trio:
            copy.wait_send()


def body(
    tokens,
    ln_gain,
    w_up,
    w_down,
    w_flux_in,
    w_flux_out,
    ocean_state,
    land_mask,
    column_map,
    w_couple,
    dw_kernel,
    ocean_gain,
    w_pw1,
    w_pw2,
):
    xs, zs = XS, ZS
    rows, feat = tokens.shape
    d_model = 4 * feat
    shard, hidden = w_up.shape
    width = hidden // 4
    fh, flx = w_flux_out.shape
    quarter = rows // 4
    grid_rows, grid_cols, chans = ocean_state.shape
    cells = grid_rows * grid_cols
    pick, place = halo_matrices(grid_rows, grid_cols)
    dma = pltpu.SemaphoreType.DMA
    vm = pl.BlockSpec(memory_space=pltpu.VMEM)
    return pl.pallas_call(
        functools.partial(atmosphere_kernel, xs, zs),
        out_shape=(
            jax.ShapeDtypeStruct((rows, feat), BF),
            jax.ShapeDtypeStruct(ocean_state.shape, BF),
        ),
        in_specs=[vm] * 16,
        out_specs=(vm, vm),
        scratch_shapes=[
            pltpu.VMEM((2, shard, hidden), BF),
            pltpu.VMEM((2, 4, xs, zs, 2 * shard, width), BF),
            pltpu.VMEM((4, rows, feat), BF),
            pltpu.VMEM((rows, d_model), BF),
            pltpu.VMEM((2, rows, hidden // 2), BF),
            pltpu.VMEM((4, feat, fh), BF),
            pltpu.VMEM((3, 2, quarter, d_model // 2), BF),
            pltpu.VMEM((3, 2, quarter, d_model // 2), BF),
            pltpu.VMEM((2, quarter, d_model // 2), F32),
            pltpu.VMEM((4, quarter, feat), BF),
            pltpu.VMEM((4, quarter, feat), BF),
            pltpu.VMEM((6, quarter, flx), BF),
            dma((2,)), dma((2,)), dma((64,)), dma((64,)),
            dma((3,)), dma((3,)), dma((3,)), dma((3,)),
            dma((6,)), dma((6,)), dma((3,)), dma((3,)),
            dma((3,)), dma((3,)), dma((4,)), dma((2,)),
            pltpu.VMEM((cells, 128), F32),
            pltpu.VMEM((cells, 6 * quarter), BF),
            pltpu.VMEM((2, 7, 7, 8, chans), F32),
            pltpu.VMEM((2, cells, chans), BF),
            pltpu.VMEM((grid_rows + 6, grid_cols + 16, chans), F32),
            pltpu.VMEM((7, grid_rows + 6, grid_cols // 8, 8, chans), F32),
            pltpu.VMEM((grid_rows, grid_cols // 8, 8, chans), F32),
            pltpu.VMEM((2, 256, chans), BF),
            pltpu.VMEM((2, 256, chans), BF),
            pltpu.VMEM((2, 2, 3 * grid_cols, chans), BF),
            dma((16,)), dma((16,)),
        ],
        compiler_params=pltpu.CompilerParams(
            collective_id=0, has_side_effects=True, vmem_limit_bytes=60 * 1024 * 1024
        ),
        name="coupled_step",
    )(
        tokens, ln_gain.reshape(1, d_model), w_up, w_down.T, w_flux_in, w_flux_out,
        ocean_state, land_mask, column_map, w_couple, dw_kernel, ocean_gain, w_pw1, w_pw2,
        pick, place,
    )


def solution(mesh):
    placed = (
        P("fsdp", "tile"),
        P(),
        P("fsdp", "tile"),
        P("tile", "fsdp"),
        P("tile", None),
        P(),
        P("fsdp", "tile", None),
        P("fsdp", "tile"),
        P("fsdp", "tile"),
        P(),
        P(),
        P(),
        P(),
        P(),
    )
    return jax.shard_map(
        body,
        mesh=mesh,
        in_specs=placed,
        out_specs=(P("fsdp", "tile"), P("fsdp", "tile", None)),
        check_vma=False,
    )
```

```python
import functools

import jax
import jax.numpy as jnp
from jax import lax
from jax.experimental import pallas as pl
from jax.experimental.pallas import tpu as pltpu
from jax.sharding import PartitionSpec as P
import numpy as np

MESH = pl.DeviceIdType.MESH
BF = jnp.bfloat16
F32 = jnp.float32
EPS = 1e-06
XS = 4
ZS = 8


def nt_dot(lhs, rhs):
    return lax.dot_general(lhs, rhs, (((1,), (1,)), ((), ())), preferred_element_type=F32)


def ocean_prepare(first, mask_ref, map_ref, taps_ref, mk, oh, wb):
    grid_rows, grid_cols = map_ref.shape
    tiles = oh.shape[1] // 128

    @pl.loop(0, grid_rows)
    def _(r):
        square = (grid_cols, grid_cols)
        eye = (
            lax.broadcasted_iota(jnp.int32, square, 0) == lax.broadcasted_iota(jnp.int32, square, 1)
        ).astype(F32)
        ones = jnp.ones((grid_cols, 128), BF)

        def upright(line):
            return jnp.dot((eye * line).astype(BF), ones, preferred_element_type=F32)

        index = map_ref[pl.ds(r, 1), :] - first
        high = upright((index >> 5).astype(F32))
        low = upright((index & 31).astype(F32))
        index_up = high * 32.0 + low
        span = pl.ds(pl.multiple_of(r * grid_cols, grid_cols), grid_cols)
        mk[span, :] = upright(mask_ref[pl.ds(r, 1), :].astype(F32))
        lane = lax.broadcasted_iota(jnp.int32, (grid_cols, 128), 1).astype(F32)
        for k in range(tiles):
            oh[span, k * 128 : (k + 1) * 128] = jnp.where(
                index_up == lane + 128.0 * k, 1.0, 0.0
            ).astype(BF)

    for k in range(taps_ref.shape[2]):
        for a in range(7):
            for b in range(7):
                wb[k, a, b] = jnp.broadcast_to(taps_ref[a, b, k : k + 1, :], wb.shape[3:])


def ocean(
    f, t, n_f, f_prev, f_next, remote, wn, sea_ref, couple_ref, sgain_ref, one_ref, two_ref,
    pick_ref, place_ref, out_ref, mk, oh, wb, st, pd, sh, cv, pk, rw, rn, halo_send, halo_recv,
):
    grid_rows, grid_cols, chans = sea_ref.shape
    cells = 8 * grid_cols
    wide = pd.shape[1]
    t_next, t_prev = (t + 1) % 4, (t + 3) % 4
    edge = 3 * grid_cols

    def masked(span, values):
        return (jnp.concatenate([mk[span, :]] * (chans // 128), axis=1) * values).astype(BF)

    def keep(k, i, span, values):
        st[k, span, :] = values
        pd[pl.ds(3 + i * 8, 8), 8 : 8 + grid_cols, :] = values.astype(F32).reshape(
            8, grid_cols, chans
        )

    @pl.loop(0, grid_rows // 8)
    def _(i):
        span = pl.ds(pl.multiple_of(i * cells, cells), cells)
        picked = jnp.dot(
            oh[span, :], wn[...].reshape(oh.shape[1], wn.shape[2]), preferred_element_type=F32
        ).astype(BF)
        forcing = jnp.dot(picked, couple_ref[...], preferred_element_type=F32)
        before = sea_ref[pl.ds(i * 8, 8)].reshape(cells, chans).astype(F32)
        keep(0, i, span, masked(span, before + forcing))

    for k in range(2):
        pk[k] = jnp.dot(pick_ref[...], st[k], preferred_element_type=F32).astype(BF)
        last = grid_rows * grid_cols - edge
        moves = [
            (st.at[k, pl.ds(last, edge)], rn.at[k, 0], (f_next, t)),
            (st.at[k, pl.ds(0, edge)], rn.at[k, 1], (f_prev, t)),
            (pk.at[k, pl.ds(0, 96)], rw.at[k, pl.ds(0, 96)], (f, t_next)),
            (pk.at[k, pl.ds(96, 96)], rw.at[k, pl.ds(96, 96)], (f, t_prev)),
        ]
        corner = 192
        for fd in (f_prev, f_next):
            for td in (t_prev, t_next):
                part = pl.ds(corner, 16)
                moves.append((pk.at[k, part], rw.at[k, part], (fd, td)))
                corner += 16
        copies = [
            remote(src, dst, halo_send.at[k * 8 + j], halo_recv.at[k * 8 + j], device)
            for j, (src, dst, device) in enumerate(moves)
        ]
        for copy in copies:
            copy.start()
        for copy in copies:
            copy.wait_recv()
        above, below, left, right = f > 0, f < n_f - 1, t > 0, t < 3

        def valid(flag, values):
            return jnp.where(flag, values.astype(F32), 0.0)

        pd[0:3, 8 : 8 + grid_cols, :] = valid(above, rn[k, 0]).reshape(3, grid_cols, chans)
        pd[3 + grid_rows : 6 + grid_rows, 8 : 8 + grid_cols, :] = valid(below, rn[k, 1]).reshape(
            3, grid_cols, chans
        )
        flags = (
            left,
            right,
            jnp.logical_and(below, right),
            jnp.logical_and(below, left),
            jnp.logical_and(above, right),
            jnp.logical_and(above, left),
        )
        starts = (0, 96, 192, 208, 224, 240, 256)
        came = jnp.concatenate(
            [valid(flags[j], rw[k, starts[j] : starts[j + 1]]) for j in range(6)], axis=0
        ).astype(BF)
        strips = jnp.dot(place_ref[...], came, preferred_element_type=F32)
        count = (grid_rows + 6) * 8
        pd[:, 0:8, :] = strips[:count].reshape(grid_rows + 6, 8, chans)
        pd[:, wide - 8 : wide, :] = strips[count:].reshape(grid_rows + 6, 8, chans)

        @pl.loop(0, grid_rows + 6)
        def _(r):
            line = pd[r]
            for b in range(7):
                sh[b, r] = line[5 + b : 5 + b + grid_cols].reshape(grid_cols // 8, 8, chans)

        @pl.loop(0, (grid_rows // 4) * (chans // 128))
        def _(i):
            first = (i // (chans // 128)) * 4
            lanes = pl.ds(pl.multiple_of((i % (chans // 128)) * 128, 128), 128)
            totals = [jnp.zeros((grid_cols // 8, 8, 128), F32) for _ in range(4)]
            for b in range(7):
                weights = [wb[k, a, b, :, lanes] for a in range(7)]
                for r in range(10):
                    values = sh[b, first + r, :, :, lanes]
                    for j in range(4):
                        if 0 <= r - j < 7:
                            totals[j] = totals[j] + values * weights[r - j]
            for j in range(4):
                cv[first + j, :, :, lanes] = totals[j]

        @pl.loop(0, grid_rows // 8)
        def _(i):
            span = pl.ds(pl.multiple_of(i * cells, cells), cells)
            total = cv[pl.ds(i * 8, 8)].reshape(cells, chans)
            center = total - jnp.mean(total, axis=-1, keepdims=True)
            spread = jnp.mean(center * center, axis=-1, keepdims=True)
            pnorm = (center * lax.rsqrt(spread + EPS) * sgain_ref[k : k + 1, :]).astype(BF)
            inner = jax.nn.gelu(
                jnp.dot(pnorm, one_ref[k], preferred_element_type=F32), approximate=True
            ).astype(BF)
            lowered = jnp.dot(inner, two_ref[k], preferred_element_type=F32)
            values = masked(span, st[k, span, :].astype(F32) + lowered)
            if k == 0:
                keep(1, i, span, values)
            else:
                out_ref[pl.ds(i * 8, 8)] = values.reshape(8, grid_cols, chans)

        for copy in copies:
            copy.wait_send()


def halo_matrices(grid_rows, grid_cols):
    pick = np.zeros((256, grid_rows * grid_cols), np.float32)
    place = np.zeros((2 * (grid_rows + 6) * 8, 256), np.float32)
    side = (grid_rows + 6) * 8
    for r in range(grid_rows):
        for j in range(3):
            pick[r * 3 + j, r * grid_cols + grid_cols - 3 + j] = 1
            pick[96 + r * 3 + j, r * grid_cols + j] = 1
            place[(3 + r) * 8 + 5 + j, r * 3 + j] = 1
            place[side + (3 + r) * 8 + j, 96 + r * 3 + j] = 1
    corner = 192
    for down in (0, 1):
        for right in (0, 1):
            for i in range(3):
                for j in range(3):
                    row = grid_rows - 3 + i if down else i
                    col = grid_cols - 3 + j if right else j
                    pick[corner + i * 3 + j, row * grid_cols + col] = 1
                    to_row = i if down else grid_rows + 3 + i
                    to = to_row * 8 + 5 + j if right else side + to_row * 8 + j
                    place[to, corner + i * 3 + j] = 1
            corner += 16
    return jnp.asarray(pick, BF), jnp.asarray(place, BF)


def atmosphere_kernel(
    xs, zs,
    tok_ref, gain_ref, up_ref, down_ref, wfi_ref, wfo_hbm,
    sea_hbm, mask_ref, map_ref, couple_hbm, taps_ref, sgain_ref, one_hbm, two_hbm, pick_hbm, place_hbm,
    atm_ref, out_ref,
    yb, gw, tk, nm, hd, fi, sb, rb, acc, at, ao, wn,
    y_send, y_recv, ring_send, ring_recv, tok_send, tok_recv, fi_send, fi_recv,
    rs_send, rs_recv, at_send, at_recv, fx_send, fx_recv, rim_send, rim_recv,
    mk, oh, wb, st, pd, sh, cv, pk, rw, rn, halo_send, halo_recv,
    wfo_ref, sea_ref, couple_ref, one_ref, two_ref, pick_ref, place_ref, load_sem,
    tok_hop, fi_hop, rs_hop, hop_send, hop_recv,
):
    f = lax.axis_index("fsdp")
    t = lax.axis_index("tile")
    n_f = 2 * xs * zs
    x, z, yl = f // (2 * zs), (f // 2) % zs, f % 2
    yh, c = t // 2, t % 2
    yp = f + 1 - 2 * yl
    x_right = (f + 2 * zs) % n_f
    x_left = (f - 2 * zs + n_f) % n_f
    z_right = x * 2 * zs + ((z + 1) % zs) * 2 + yl
    z_left = x * 2 * zs + ((z + zs - 1) % zs) * 2 + yl
    f_next, f_prev = (f + 1) % n_f, (f + n_f - 1) % n_f
    t_core = yh * 2 + (1 - c)
    t_far = (1 - yh) * 2 + c
    t_diag = (1 - yh) * 2 + (1 - c)
    rows = tok_ref.shape[0]
    quarter = rows // 4
    feat = tok_ref.shape[1]
    width = gw.shape[-1]
    d_model = 4 * feat

    barrier = pltpu.get_barrier_semaphore()
    for other in (x_right, x_left, z_right, z_left):
        pl.semaphore_signal(barrier, inc=1, device_id=(other, t), device_id_type=MESH)
    for other in (t_core, t_far, t_diag):
        pl.semaphore_signal(barrier, inc=1, device_id=(f, other), device_id_type=MESH)
    for other in (f_prev, f_next):
        for q in range(4):
            pl.semaphore_signal(barrier, inc=1, device_id=(other, q), device_id_type=MESH)
    tok_load = pltpu.make_async_copy(tok_ref, tk.at[t], load_sem.at[0])
    fi_load = pltpu.make_async_copy(wfi_ref, fi.at[t], load_sem.at[1])
    loads = [
        pltpu.make_async_copy(src, dst, load_sem.at[2 + j])
        for j, (src, dst) in enumerate((
            (wfo_hbm, wfo_ref), (sea_hbm, sea_ref), (couple_hbm, couple_ref), (one_hbm, one_ref),
            (two_hbm, two_ref), (pick_hbm, pick_ref), (place_hbm, place_ref),
        ))
    ]
    tok_load.start()
    pl.semaphore_wait(barrier, 15)

    def remote(src, dst, send, recv, device):
        return pltpu.make_async_remote_copy(
            src_ref=src, dst_ref=dst, send_sem=send, recv_sem=recv,
            device_id=device, device_id_type=MESH,
        )

    y_copies = [
        remote(ref, yb.at[w], y_send.at[w], y_recv.at[w], (yp, t))
        for w, ref in enumerate((up_ref, down_ref))
    ]
    for copy in y_copies:
        copy.start()
    y_at = yh * 2 + yl
    y_ways = []
    for way in (1, 3):
        y_to = (y_at + way) % 4
        y_ways.append((f - yl + y_to % 2, (y_to // 2) * 2 + c))

    def far_out(src, hop, sem):
        return [
            remote(src[h], hop.at[h], hop_send.at[sem + h], hop_recv.at[sem + h], y_ways[h])
            for h in (0, 1)
        ]

    def far_on(hop, dst, sem):
        copies = []
        for h in (0, 1):
            origin = (1 - y_ways[h][1] // 2) * 2 + c
            copies.append(
                remote(
                    hop.at[h], dst(origin, h), hop_send.at[sem + 2 + h], hop_recv.at[sem + 2 + h],
                    y_ways[h],
                )
            )
        return copies

    half_rows, half_feat = rows // 2, feat // 2
    tok_parts = [pl.ds(h * half_rows, half_rows) for h in (0, 1)]
    fi_parts = [pl.ds(h * half_feat, half_feat) for h in (0, 1)]
    tok_out = far_out([tok_ref.at[part] for part in tok_parts], tok_hop, 0)
    tok_on = far_on(tok_hop, lambda q, h: tk.at[q, tok_parts[h]], 0)
    fi_out = far_out([wfi_ref.at[part] for part in fi_parts], fi_hop, 4)
    fi_on = far_on(fi_hop, lambda q, h: fi.at[q, fi_parts[h]], 4)
    tok_near = remote(tok_ref, tk.at[t], tok_send.at[0], tok_recv.at[0], (f, t_core))
    fi_near = remote(wfi_ref, fi.at[t], fi_send.at[0], fi_recv.at[0], (f, t_core))
    tok_relay = remote(tk.at[t_far], tk.at[t_far], tok_send.at[1], tok_recv.at[1], (f, t_core))
    fi_relay = remote(fi.at[t_far], fi.at[t_far], fi_send.at[1], fi_recv.at[1], (f, t_core))

    def ring_round(w, stream, stage, s):
        on_x = (stream == 0) == (stage == 0)
        n = xs if on_x else zs
        here = x if on_x else z
        last = s == n // 2 - 1
        copies = []
        for way in (0, 1):
            chunk = (here - s + n) % n if way == 0 else (here + s) % n
            if last:
                pieces = 2 * stream + way
            else:
                pieces = pl.ds(2 * stream, 2)
            if stage == 0:
                part = gw.at[w, pieces, chunk, z] if on_x else gw.at[w, pieces, x, chunk]
            else:
                part = gw.at[w, pieces, chunk] if on_x else gw.at[w, pieces, :, chunk]
            if on_x:
                target = x_right if way == 0 else x_left
            else:
                target = z_right if way == 0 else z_left
            at_sem = (((w * 2 + stream) * 2 + stage) * 4 + s) * 2 + way
            copies.append(
                remote(part, part, ring_send.at[at_sem], ring_recv.at[at_sem], (target, t))
            )
        return copies

    done = []

    def start(copies):
        for copy in copies:
            copy.start()
        done.extend(copies)
        return copies

    def arrive(copies):
        for copy in copies:
            copy.wait_recv()

    def advance(old, w, stream, stage, s):
        arrive(old)
        return start(ring_round(w, stream, stage, s))

    def assemble(w, ref):
        y_copies[w].wait_recv()
        for p in range(4):
            mine = ref[:, p * width : (p + 1) * width].astype(F32)
            other = yb[w, :, p * width : (p + 1) * width].astype(F32)
            first = jnp.where(yl == 0, mine, other)
            second = jnp.where(yl == 0, other, mine)
            gw[w, p, x, z] = jnp.concatenate([first, second], axis=0).astype(BF)

    for copy in tok_out:
        copy.start()
    tok_near.start()
    for copy in loads:
        copy.start()
    fi_load.start()
    assemble(0, up_ref)
    up_b = start(ring_round(0, 1, 0, 0))
    up_a = start(ring_round(0, 0, 0, 0))
    assemble(1, down_ref)
    up_a = advance(up_a, 0, 0, 0, 1)
    up_b = advance(up_b, 0, 1, 0, 1)
    down_b = start(ring_round(1, 1, 0, 0))
    up_b = advance(up_b, 0, 1, 0, 2)
    up_a = advance(up_a, 0, 0, 1, 0)
    arrive(tok_out)
    start(tok_on)
    up_b = advance(up_b, 0, 1, 0, 3)
    down_a = start(ring_round(1, 0, 0, 0))
    down_b = advance(down_b, 1, 1, 0, 1)
    up_b = advance(up_b, 0, 1, 1, 0)
    down_a = advance(down_a, 1, 0, 0, 1)
    down_b = advance(down_b, 1, 1, 0, 2)
    up_a = advance(up_a, 0, 0, 1, 1)
    arrive(tok_on)
    start([tok_relay])
    start(fi_out)
    start([fi_near])
    down_b = advance(down_b, 1, 1, 0, 3)
    tok_load.wait()
    tok_near.wait_recv()
    tok_relay.wait_recv()
    step = min(32, quarter)

    @pl.loop(0, rows // step)
    def _(i):
        span = pl.ds(pl.multiple_of(i * step, step), step)
        values = [tk[q, span, :].astype(F32) for q in range(4)]
        mean = sum(jnp.sum(v, axis=-1, keepdims=True) for v in values) / d_model
        centers = [v - mean for v in values]
        spread = sum(jnp.sum(v * v, axis=-1, keepdims=True) for v in centers) / d_model
        inverse = lax.rsqrt(spread + EPS)
        for q in range(4):
            gain = gain_ref[q * feat : (q + 1) * feat][None, :]
            nm[span, q * feat : (q + 1) * feat] = (centers[q] * inverse * gain).astype(BF)

    up_a = advance(up_a, 0, 0, 1, 2)
    up_b = advance(up_b, 0, 1, 1, 1)
    ocean_prepare(f * rows - quarter, mask_ref, map_ref, taps_ref, mk, oh, wb)
    up_a = advance(up_a, 0, 0, 1, 3)
    down_a = advance(down_a, 1, 0, 1, 0)
    arrive(fi_out)
    start(fi_on)
    arrive(up_b)
    down_b = advance(down_b, 1, 1, 1, 0)
    arrive(up_a)
    down_a = advance(down_a, 1, 0, 1, 1)

    def up_block(half, block):
        span = pl.ds(pl.multiple_of(block * quarter, quarter), quarter)
        rhs = jnp.concatenate(
            [gw[0, half * 2 + k].reshape(d_model, width) for k in (0, 1)], axis=1
        )
        pre = jnp.dot(nm[span, :], rhs, preferred_element_type=F32)
        hd[half, span, :] = jax.nn.gelu(pre, approximate=True).astype(BF)

    for half in (0, 1):
        @pl.loop(0, 4)
        def _(block):
            up_block(half, block)

        if half == 0:
            down_a = advance(down_a, 1, 0, 1, 2)
            down_b = advance(down_b, 1, 1, 1, 1)
            arrive(fi_on)
            start([fi_relay])
    down_a = advance(down_a, 1, 0, 1, 3)
    arrive(down_b)
    arrive(down_a)

    def partial(block, half):
        span = pl.ds(pl.multiple_of(block * quarter, quarter), quarter)
        lhs = jnp.concatenate([hd[0, span, :], hd[1, span, :]], axis=1)
        part = pl.ds(half * (xs // 2), xs // 2)
        rhs = jnp.concatenate(
            [gw[1, p, part].reshape(d_model // 2, width) for p in range(4)], axis=1
        )
        return nt_dot(lhs, rhs)

    def sums(k, half, target):
        return remote(
            sb.at[k, half], rb.at[k, half], rs_send.at[2 * k + half], rs_recv.at[2 * k + half],
            (f, target),
        )

    to_core = [sums(0, half, t_core) for half in (0, 1)]
    far_sums = far_out([sb.at[1, half] for half in (0, 1)], rs_hop, 8)
    far_sums_on = far_on(rs_hop, lambda q, half: rb.at[1, half], 8)
    to_core2 = [sums(2, half, t_core) for half in (0, 1)]

    for half in (0, 1):
        sb[0, half] = partial(t_diag, half).astype(BF)
        to_core[half].start()
    for half in (0, 1):
        acc[half] = partial(t_far, half)
        to_core[half].wait_recv()
        sb[1, half] = (acc[half] + rb[0, half].astype(F32)).astype(BF)
        far_sums[half].start()
    for half in (0, 1):
        sb[2, half] = partial(t_core, half).astype(BF)
        to_core2[half].start()
    for half in (0, 1):
        acc[half] = partial(t, half)
    arrive(far_sums)
    start(far_sums_on)
    mine = pl.ds(pl.multiple_of(t * quarter, quarter), quarter)
    for half in (0, 1):
        to_core2[half].wait_recv()
        far_sums_on[half].wait_recv()
        for k in (0, 1):
            q = 2 * half + k
            cols = slice(k * feat, (k + 1) * feat)
            delta = acc[half, :, cols] + rb[2, half, :, cols].astype(F32) + rb[1, half, :, cols].astype(F32)
            at[q] = (tk[q, mine, :].astype(F32) + delta).astype(BF)

    at_copies = []
    for k in range(1, 4):
        q = (t + k) % 4
        at_copies.append(remote(at.at[q], ao.at[t], at_send.at[k - 1], at_recv.at[k - 1], (f, q)))
        at_copies[-1].start()
    ao[t] = at[t]

    fi_load.wait()
    fi_near.wait_recv()
    fi_relay.wait_recv()
    for copy in loads:
        copy.wait()
    pre = jnp.dot(
        jnp.concatenate([at[q] for q in range(4)], axis=1),
        fi[...].reshape(d_model, fi.shape[-1]),
        preferred_element_type=F32,
    )
    flux_hidden = jax.nn.gelu(pre, approximate=True).astype(BF)
    wn[1 + t] = jnp.dot(flux_hidden, wfo_ref[...], preferred_element_type=F32).astype(BF)
    fx_copies = []
    for k in range(1, 4):
        fx_copies.append(
            remote(wn.at[1 + t], wn.at[1 + t], fx_send.at[k - 1], fx_recv.at[k - 1], (f, (t + k) % 4))
        )
        fx_copies[-1].start()

    def rim(slot, source, target):
        return [
            remote(wn.at[source], wn.at[slot], rim_send.at[q], rim_recv.at[slot // 5], (target, q))
            for q in range(4)
        ]

    low = rim(0, 4, f_next)
    high = rim(5, 1, f_prev)

    @pl.when(t == 3)
    def _():
        for copy in low:
            copy.start()

    @pl.when(t == 0)
    def _():
        for copy in high:
            copy.start()

    for copy in at_copies:
        copy.wait_recv()
    for q in range(4):
        atm_ref[pl.ds(q * quarter, quarter), :] = ao[q]
    for copy in fx_copies:
        copy.wait_recv()
    low[0].wait_recv()
    high[0].wait_recv()
    ocean(
        f, t, n_f, f_prev, f_next, remote, wn, sea_ref, couple_ref, sgain_ref, one_ref, two_ref,
        pick_ref, place_ref, out_ref, mk, oh, wb, st, pd, sh, cv, pk, rw, rn, halo_send, halo_recv,
    )

    @pl.when(t == 3)
    def _():
        for copy in low:
            copy.wait_send()

    @pl.when(t == 0)
    def _():
        for copy in high:
            copy.wait_send()

    for copy in y_copies + done + tok_out + [tok_near] + at_copies + fx_copies + to_core + far_sums + to_core2:
        copy.wait_send()


def body(
    tokens,
    ln_gain,
    w_up,
    w_down,
    w_flux_in,
    w_flux_out,
    ocean_state,
    land_mask,
    column_map,
    w_couple,
    dw_kernel,
    ocean_gain,
    w_pw1,
    w_pw2,
):
    xs, zs = XS, ZS
    rows, feat = tokens.shape
    d_model = 4 * feat
    shard, hidden = w_up.shape
    width = hidden // 4
    fh, flx = w_flux_out.shape
    quarter = rows // 4
    grid_rows, grid_cols, chans = ocean_state.shape
    cells = grid_rows * grid_cols
    pick, place = halo_matrices(grid_rows, grid_cols)
    dma = pltpu.SemaphoreType.DMA
    vm = pl.BlockSpec(memory_space=pltpu.VMEM)
    hb = pl.BlockSpec(memory_space=pl.ANY)
    return pl.pallas_call(
        functools.partial(atmosphere_kernel, xs, zs),
        out_shape=(
            jax.ShapeDtypeStruct((rows, feat), BF),
            jax.ShapeDtypeStruct(ocean_state.shape, BF),
        ),
        in_specs=[hb, vm, vm, vm, hb, hb, hb, vm, vm, hb, vm, vm, hb, hb, hb, hb],
        out_specs=(vm, vm),
        scratch_shapes=[
            pltpu.VMEM((2, shard, hidden), BF),
            pltpu.VMEM((2, 4, xs, zs, 2 * shard, width), BF),
            pltpu.VMEM((4, rows, feat), BF),
            pltpu.VMEM((rows, d_model), BF),
            pltpu.VMEM((2, rows, hidden // 2), BF),
            pltpu.VMEM((4, feat, fh), BF),
            pltpu.VMEM((3, 2, quarter, d_model // 2), BF),
            pltpu.VMEM((3, 2, quarter, d_model // 2), BF),
            pltpu.VMEM((2, quarter, d_model // 2), F32),
            pltpu.VMEM((4, quarter, feat), BF),
            pltpu.VMEM((4, quarter, feat), BF),
            pltpu.VMEM((6, quarter, flx), BF),
            dma((2,)), dma((2,)), dma((64,)), dma((64,)),
            dma((3,)), dma((3,)), dma((3,)), dma((3,)),
            dma((6,)), dma((6,)), dma((3,)), dma((3,)),
            dma((3,)), dma((3,)), dma((4,)), dma((2,)),
            pltpu.VMEM((cells, 128), F32),
            pltpu.VMEM((cells, 6 * quarter), BF),
            pltpu.VMEM((2, 7, 7, 8, chans), F32),
            pltpu.VMEM((2, cells, chans), BF),
            pltpu.VMEM((grid_rows + 6, grid_cols + 16, chans), F32),
            pltpu.VMEM((7, grid_rows + 6, grid_cols // 8, 8, chans), F32),
            pltpu.VMEM((grid_rows, grid_cols // 8, 8, chans), F32),
            pltpu.VMEM((2, 256, chans), BF),
            pltpu.VMEM((2, 256, chans), BF),
            pltpu.VMEM((2, 2, 3 * grid_cols, chans), BF),
            dma((16,)), dma((16,)),
            pltpu.VMEM(w_flux_out.shape, BF),
            pltpu.VMEM(ocean_state.shape, BF),
            pltpu.VMEM(w_couple.shape, BF),
            pltpu.VMEM(w_pw1.shape, BF),
            pltpu.VMEM(w_pw2.shape, BF),
            pltpu.VMEM(pick.shape, BF),
            pltpu.VMEM(place.shape, BF),
            dma((9,)),
            pltpu.VMEM((2, rows // 2, feat), BF),
            pltpu.VMEM((2, feat // 2, fh), BF),
            pltpu.VMEM((2, quarter, d_model // 2), BF),
            dma((12,)), dma((12,)),
        ],
        compiler_params=pltpu.CompilerParams(
            collective_id=0, has_side_effects=True, vmem_limit_bytes=60 * 1024 * 1024
        ),
        name="coupled_step",
    )(
        tokens, ln_gain, w_up, w_down.T, w_flux_in, w_flux_out,
        ocean_state, land_mask, column_map, w_couple, dw_kernel.transpose(1, 2, 0, 3), ocean_gain, w_pw1, w_pw2,
        pick, place,
    )


def solution(mesh):
    placed = (
        P("fsdp", "tile"),
        P(),
        P("fsdp", "tile"),
        P("tile", "fsdp"),
        P("tile", None),
        P(),
        P("fsdp", "tile", None),
        P("fsdp", "tile"),
        P("fsdp", "tile"),
        P(),
        P(),
        P(),
        P(),
        P(),
    )
    return jax.shard_map(
        body,
        mesh=mesh,
        in_specs=placed,
        out_specs=(P("fsdp", "tile"), P("fsdp", "tile", None)),
        check_vma=False,
    )
```

```python
import functools

import jax
import jax.numpy as jnp
from jax import lax
from jax.experimental import pallas as pl
from jax.experimental.pallas import tpu as pltpu
from jax.sharding import PartitionSpec as P
import numpy as np

MESH = pl.DeviceIdType.MESH
BF = jnp.bfloat16
F32 = jnp.float32
EPS = 1e-06
XS = 4
ZS = 8


def nt_dot(lhs, rhs):
    return lax.dot_general(lhs, rhs, (((1,), (1,)), ((), ())), preferred_element_type=F32)


def ocean_prepare(first, mask_ref, map_ref, taps_ref, mk, oh, wb):
    grid_rows, grid_cols = map_ref.shape
    tiles = oh.shape[1] // 128

    @pl.loop(0, grid_rows)
    def _(r):
        square = (grid_cols, grid_cols)
        eye = (
            lax.broadcasted_iota(jnp.int32, square, 0) == lax.broadcasted_iota(jnp.int32, square, 1)
        ).astype(F32)
        ones = jnp.ones((grid_cols, 128), BF)

        def upright(line):
            return jnp.dot((eye * line).astype(BF), ones, preferred_element_type=F32)

        index = map_ref[pl.ds(r, 1), :] - first
        high = upright((index >> 5).astype(F32))
        low = upright((index & 31).astype(F32))
        index_up = high * 32.0 + low
        span = pl.ds(pl.multiple_of(r * grid_cols, grid_cols), grid_cols)
        mk[span, :] = upright(mask_ref[pl.ds(r, 1), :].astype(F32))
        lane = lax.broadcasted_iota(jnp.int32, (grid_cols, 128), 1).astype(F32)
        for k in range(tiles):
            oh[span, k * 128 : (k + 1) * 128] = jnp.where(
                index_up == lane + 128.0 * k, 1.0, 0.0
            ).astype(BF)

    for k in range(taps_ref.shape[2]):
        for a in range(7):
            for b in range(7):
                wb[k, a, b] = jnp.broadcast_to(taps_ref[a, b, k : k + 1, :], wb.shape[3:])


def ocean(
    f, t, n_f, f_prev, f_next, remote, wn, sea_ref, couple_ref, sgain_ref, one_ref, two_ref,
    pick_ref, place_ref, out_ref, mk, oh, wb, st, pd, sh, cv, pk, rw, rn, halo_send, halo_recv, at_copies,
):
    grid_rows, grid_cols, chans = sea_ref.shape
    cells = 8 * grid_cols
    wide = pd.shape[1]
    t_next, t_prev = (t + 1) % 4, (t + 3) % 4
    edge = 3 * grid_cols

    def masked(span, values):
        return (jnp.concatenate([mk[span, :]] * (chans // 128), axis=1) * values).astype(BF)

    def keep(k, i, span, values):
        st[k, span, :] = values
        pd[pl.ds(3 + i * 8, 8), 8 : 8 + grid_cols, :] = values.astype(F32).reshape(
            8, grid_cols, chans
        )

    @pl.loop(0, grid_rows // 8)
    def _(i):
        span = pl.ds(pl.multiple_of(i * cells, cells), cells)
        picked = jnp.dot(
            oh[span, :], wn[...].reshape(oh.shape[1], wn.shape[2]), preferred_element_type=F32
        ).astype(BF)
        forcing = jnp.dot(picked, couple_ref[...], preferred_element_type=F32)
        before = sea_ref[pl.ds(i * 8, 8)].reshape(cells, chans).astype(F32)
        keep(0, i, span, masked(span, before + forcing))

    for k in range(2):
        pk[k] = jnp.dot(pick_ref[...], st[k], preferred_element_type=F32).astype(BF)
        last = grid_rows * grid_cols - edge
        moves = [
            (st.at[k, pl.ds(last, edge)], rn.at[k, 0], (f_next, t)),
            (st.at[k, pl.ds(0, edge)], rn.at[k, 1], (f_prev, t)),
            (pk.at[k, pl.ds(0, 96)], rw.at[k, pl.ds(0, 96)], (f, t_next)),
            (pk.at[k, pl.ds(96, 96)], rw.at[k, pl.ds(96, 96)], (f, t_prev)),
        ]
        corner = 192
        for fd in (f_prev, f_next):
            for td in (t_prev, t_next):
                part = pl.ds(corner, 16)
                moves.append((pk.at[k, part], rw.at[k, part], (fd, td)))
                corner += 16
        copies = [
            remote(src, dst, halo_send.at[k * 8 + j], halo_recv.at[k * 8 + j], device)
            for j, (src, dst, device) in enumerate(moves)
        ]
        for copy in copies:
            copy.start()
        for copy in copies:
            copy.wait_recv()
        if k == 0:
            for copy in at_copies:
                copy.start()
        above, below, left, right = f > 0, f < n_f - 1, t > 0, t < 3

        def valid(flag, values):
            return jnp.where(flag, values.astype(F32), 0.0)

        pd[0:3, 8 : 8 + grid_cols, :] = valid(above, rn[k, 0]).reshape(3, grid_cols, chans)
        pd[3 + grid_rows : 6 + grid_rows, 8 : 8 + grid_cols, :] = valid(below, rn[k, 1]).reshape(
            3, grid_cols, chans
        )
        flags = (
            left,
            right,
            jnp.logical_and(below, right),
            jnp.logical_and(below, left),
            jnp.logical_and(above, right),
            jnp.logical_and(above, left),
        )
        starts = (0, 96, 192, 208, 224, 240, 256)
        came = jnp.concatenate(
            [valid(flags[j], rw[k, starts[j] : starts[j + 1]]) for j in range(6)], axis=0
        ).astype(BF)
        strips = jnp.dot(place_ref[...], came, preferred_element_type=F32)
        count = (grid_rows + 6) * 8
        pd[:, 0:8, :] = strips[:count].reshape(grid_rows + 6, 8, chans)
        pd[:, wide - 8 : wide, :] = strips[count:].reshape(grid_rows + 6, 8, chans)

        @pl.loop(0, grid_rows + 6)
        def _(r):
            line = pd[r]
            for b in range(7):
                sh[b, r] = line[5 + b : 5 + b + grid_cols].reshape(grid_cols // 8, 8, chans)

        @pl.loop(0, (grid_rows // 4) * (chans // 128))
        def _(i):
            first = (i // (chans // 128)) * 4
            lanes = pl.ds(pl.multiple_of((i % (chans // 128)) * 128, 128), 128)
            totals = [jnp.zeros((grid_cols // 8, 8, 128), F32) for _ in range(4)]
            for b in range(7):
                weights = [wb[k, a, b, :, lanes] for a in range(7)]
                for r in range(10):
                    values = sh[b, first + r, :, :, lanes]
                    for j in range(4):
                        if 0 <= r - j < 7:
                            totals[j] = totals[j] + values * weights[r - j]
            for j in range(4):
                cv[first + j, :, :, lanes] = totals[j]

        @pl.loop(0, grid_rows // 8)
        def _(i):
            span = pl.ds(pl.multiple_of(i * cells, cells), cells)
            total = cv[pl.ds(i * 8, 8)].reshape(cells, chans)
            center = total - jnp.mean(total, axis=-1, keepdims=True)
            spread = jnp.mean(center * center, axis=-1, keepdims=True)
            pnorm = (center * lax.rsqrt(spread + EPS) * sgain_ref[k : k + 1, :]).astype(BF)
            inner = jax.nn.gelu(
                jnp.dot(pnorm, one_ref[k], preferred_element_type=F32), approximate=True
            ).astype(BF)
            lowered = jnp.dot(inner, two_ref[k], preferred_element_type=F32)
            values = masked(span, st[k, span, :].astype(F32) + lowered)
            if k == 0:
                keep(1, i, span, values)
            else:
                out_ref[pl.ds(i * 8, 8)] = values.reshape(8, grid_cols, chans)

        for copy in copies:
            copy.wait_send()


def halo_matrices(grid_rows, grid_cols):
    pick = np.zeros((256, grid_rows * grid_cols), np.float32)
    place = np.zeros((2 * (grid_rows + 6) * 8, 256), np.float32)
    side = (grid_rows + 6) * 8
    for r in range(grid_rows):
        for j in range(3):
            pick[r * 3 + j, r * grid_cols + grid_cols - 3 + j] = 1
            pick[96 + r * 3 + j, r * grid_cols + j] = 1
            place[(3 + r) * 8 + 5 + j, r * 3 + j] = 1
            place[side + (3 + r) * 8 + j, 96 + r * 3 + j] = 1
    corner = 192
    for down in (0, 1):
        for right in (0, 1):
            for i in range(3):
                for j in range(3):
                    row = grid_rows - 3 + i if down else i
                    col = grid_cols - 3 + j if right else j
                    pick[corner + i * 3 + j, row * grid_cols + col] = 1
                    to_row = i if down else grid_rows + 3 + i
                    to = to_row * 8 + 5 + j if right else side + to_row * 8 + j
                    place[to, corner + i * 3 + j] = 1
            corner += 16
    return jnp.asarray(pick, BF), jnp.asarray(place, BF)


def atmosphere_kernel(
    xs, zs,
    tok_ref, gain_ref, up_ref, down_ref, wfi_ref, wfo_hbm,
    sea_hbm, mask_ref, map_ref, couple_hbm, taps_ref, sgain_ref, one_hbm, two_hbm, pick_hbm, place_hbm,
    atm_ref, out_ref,
    yb, gw, tk, nm, hd, fi, sb, rb, acc, at, ao, wn,
    y_send, y_recv, ring_send, ring_recv, tok_send, tok_recv, fi_send, fi_recv,
    rs_send, rs_recv, at_send, at_recv, fx_send, fx_recv, rim_send, rim_recv,
    mk, oh, wb, st, pd, sh, cv, pk, rw, rn, halo_send, halo_recv,
    wfo_ref, sea_ref, couple_ref, one_ref, two_ref, pick_ref, place_ref, load_sem,
    tok_hop, fi_hop, rs_hop, hop_send, hop_recv,
):
    f = lax.axis_index("fsdp")
    t = lax.axis_index("tile")
    n_f = 2 * xs * zs
    x, z, yl = f // (2 * zs), (f // 2) % zs, f % 2
    yh, c = t // 2, t % 2
    yp = f + 1 - 2 * yl
    x_right = (f + 2 * zs) % n_f
    x_left = (f - 2 * zs + n_f) % n_f
    z_right = x * 2 * zs + ((z + 1) % zs) * 2 + yl
    z_left = x * 2 * zs + ((z + zs - 1) % zs) * 2 + yl
    f_next, f_prev = (f + 1) % n_f, (f + n_f - 1) % n_f
    t_core = yh * 2 + (1 - c)
    t_far = (1 - yh) * 2 + c
    t_diag = (1 - yh) * 2 + (1 - c)
    rows = tok_ref.shape[0]
    quarter = rows // 4
    feat = tok_ref.shape[1]
    width = gw.shape[-1]
    d_model = 4 * feat

    barrier = pltpu.get_barrier_semaphore()
    for other in (x_right, x_left, z_right, z_left):
        pl.semaphore_signal(barrier, inc=1, device_id=(other, t), device_id_type=MESH)
    for other in (t_core, t_far, t_diag):
        pl.semaphore_signal(barrier, inc=1, device_id=(f, other), device_id_type=MESH)
    for other in (f_prev, f_next):
        for q in range(4):
            pl.semaphore_signal(barrier, inc=1, device_id=(other, q), device_id_type=MESH)
    tok_load = pltpu.make_async_copy(tok_ref, tk.at[t], load_sem.at[0])
    fi_load = pltpu.make_async_copy(wfi_ref, fi.at[t], load_sem.at[1])
    loads = [
        pltpu.make_async_copy(src, dst, load_sem.at[2 + j])
        for j, (src, dst) in enumerate((
            (wfo_hbm, wfo_ref), (sea_hbm, sea_ref), (couple_hbm, couple_ref), (one_hbm, one_ref),
            (two_hbm, two_ref), (pick_hbm, pick_ref), (place_hbm, place_ref),
        ))
    ]
    tok_load.start()
    pl.semaphore_wait(barrier, 15)

    def remote(src, dst, send, recv, device):
        return pltpu.make_async_remote_copy(
            src_ref=src, dst_ref=dst, send_sem=send, recv_sem=recv,
            device_id=device, device_id_type=MESH,
        )

    y_copies = [
        remote(ref, yb.at[w], y_send.at[w], y_recv.at[w], (yp, t))
        for w, ref in enumerate((up_ref, down_ref))
    ]
    for copy in y_copies:
        copy.start()
    y_at = yh * 2 + yl
    y_ways = []
    for way in (1, 3):
        y_to = (y_at + way) % 4
        y_ways.append((f - yl + y_to % 2, (y_to // 2) * 2 + c))

    def far_out(src, hop, sem):
        return [
            remote(src[h], hop.at[h], hop_send.at[sem + h], hop_recv.at[sem + h], y_ways[h])
            for h in (0, 1)
        ]

    def far_on(hop, dst, sem):
        copies = []
        for h in (0, 1):
            origin = (1 - y_ways[h][1] // 2) * 2 + c
            copies.append(
                remote(
                    hop.at[h], dst(origin, h), hop_send.at[sem + 2 + h], hop_recv.at[sem + 2 + h],
                    y_ways[h],
                )
            )
        return copies

    half_rows, half_feat = rows // 2, feat // 2
    tok_parts = [pl.ds(h * half_rows, half_rows) for h in (0, 1)]
    fi_parts = [pl.ds(h * half_feat, half_feat) for h in (0, 1)]
    tok_out = far_out([tok_ref.at[part] for part in tok_parts], tok_hop, 0)
    tok_on = far_on(tok_hop, lambda q, h: tk.at[q, tok_parts[h]], 0)
    fi_out = far_out([wfi_ref.at[part] for part in fi_parts], fi_hop, 4)
    fi_on = far_on(fi_hop, lambda q, h: fi.at[q, fi_parts[h]], 4)
    tok_near = remote(tok_ref, tk.at[t], tok_send.at[0], tok_recv.at[0], (f, t_core))
    fi_near = remote(wfi_ref, fi.at[t], fi_send.at[0], fi_recv.at[0], (f, t_core))
    tok_relay = remote(tk.at[t_far], tk.at[t_far], tok_send.at[1], tok_recv.at[1], (f, t_core))
    fi_relay = remote(fi.at[t_far], fi.at[t_far], fi_send.at[1], fi_recv.at[1], (f, t_core))

    def ring_round(w, stream, stage, s):
        on_x = (stream == 0) == (stage == 0)
        n = xs if on_x else zs
        here = x if on_x else z
        last = s == n // 2 - 1
        copies = [[], []]
        for k in (0, 1):
            piece = 2 * stream + k
            for way in (0, 1):
                if last and way != k:
                    continue
                chunk = (here - s + n) % n if way == 0 else (here + s) % n
                if stage == 0:
                    part = gw.at[w, piece, chunk, z] if on_x else gw.at[w, piece, x, chunk]
                else:
                    part = gw.at[w, piece, chunk] if on_x else gw.at[w, piece, :, chunk]
                if on_x:
                    target = x_right if way == 0 else x_left
                else:
                    target = z_right if way == 0 else z_left
                at_sem = ((((w * 2 + stream) * 2 + stage) * 4 + s) * 2 + way) * 2 + k
                copies[k].append(
                    remote(part, part, ring_send.at[at_sem], ring_recv.at[at_sem], (target, t))
                )
        return copies

    done = []

    def start(copies):
        for copy in copies:
            copy.start()
        done.extend(copies)
        return copies

    def arrive(copies):
        for copy in copies:
            copy.wait_recv()

    def begin(w, stream):
        new = ring_round(w, stream, 0, 0)
        start(new[0] + new[1])
        return new

    def advance(old, w, stream, stage, s):
        new = ring_round(w, stream, stage, s)
        for k in (0, 1):
            arrive(old[k])
            start(new[k])
        return new

    def assemble(w, ref):
        y_copies[w].wait_recv()
        for p in range(4):
            mine = ref[:, p * width : (p + 1) * width].astype(F32)
            other = yb[w, :, p * width : (p + 1) * width].astype(F32)
            first = jnp.where(yl == 0, mine, other)
            second = jnp.where(yl == 0, other, mine)
            gw[w, p, x, z] = jnp.concatenate([first, second], axis=0).astype(BF)

    for copy in tok_out:
        copy.start()
    tok_near.start()
    for copy in loads:
        copy.start()
    fi_load.start()
    assemble(0, up_ref)
    up_b = begin(0, 1)
    up_a = begin(0, 0)
    assemble(1, down_ref)
    up_a = advance(up_a, 0, 0, 0, 1)
    up_b = advance(up_b, 0, 1, 0, 1)
    down_b = begin(1, 1)
    up_b = advance(up_b, 0, 1, 0, 2)
    up_a = advance(up_a, 0, 0, 1, 0)
    arrive(tok_out)
    start(tok_on)
    up_b = advance(up_b, 0, 1, 0, 3)
    down_a = begin(1, 0)
    down_b = advance(down_b, 1, 1, 0, 1)
    up_b = advance(up_b, 0, 1, 1, 0)
    down_a = advance(down_a, 1, 0, 0, 1)
    down_b = advance(down_b, 1, 1, 0, 2)
    up_a = advance(up_a, 0, 0, 1, 1)
    arrive(tok_on)
    start([tok_relay])
    start(fi_out)
    start([fi_near])
    down_b = advance(down_b, 1, 1, 0, 3)
    tok_load.wait()
    tok_near.wait_recv()
    tok_relay.wait_recv()
    step = min(32, quarter)

    @pl.loop(0, rows // step)
    def _(i):
        span = pl.ds(pl.multiple_of(i * step, step), step)
        values = [tk[q, span, :].astype(F32) for q in range(4)]
        mean = sum(jnp.sum(v, axis=-1, keepdims=True) for v in values) / d_model
        centers = [v - mean for v in values]
        spread = sum(jnp.sum(v * v, axis=-1, keepdims=True) for v in centers) / d_model
        inverse = lax.rsqrt(spread + EPS)
        for q in range(4):
            gain = gain_ref[q * feat : (q + 1) * feat][None, :]
            nm[span, q * feat : (q + 1) * feat] = (centers[q] * inverse * gain).astype(BF)

    up_a = advance(up_a, 0, 0, 1, 2)
    up_b = advance(up_b, 0, 1, 1, 1)
    ocean_prepare(f * rows - quarter, mask_ref, map_ref, taps_ref, mk, oh, wb)
    up_a = advance(up_a, 0, 0, 1, 3)
    down_a = advance(down_a, 1, 0, 1, 0)
    arrive(fi_out)
    start(fi_on)
    arrive(up_b[0] + up_b[1])
    down_b = advance(down_b, 1, 1, 1, 0)
    arrive(up_a[0] + up_a[1])
    down_a = advance(down_a, 1, 0, 1, 1)

    def up_block(half, block):
        span = pl.ds(pl.multiple_of(block * quarter, quarter), quarter)
        rhs = jnp.concatenate(
            [gw[0, half * 2 + k].reshape(d_model, width) for k in (0, 1)], axis=1
        )
        pre = jnp.dot(nm[span, :], rhs, preferred_element_type=F32)
        hd[half, span, :] = jax.nn.gelu(pre, approximate=True).astype(BF)

    for half in (0, 1):
        @pl.loop(0, 4)
        def _(block):
            up_block(half, block)

        if half == 0:
            down_a = advance(down_a, 1, 0, 1, 2)
            down_b = advance(down_b, 1, 1, 1, 1)
            arrive(fi_on)
            start([fi_relay])
    down_a = advance(down_a, 1, 0, 1, 3)
    arrive(down_b[0] + down_b[1])
    arrive(down_a[0] + down_a[1])

    def partial(block, half):
        span = pl.ds(pl.multiple_of(block * quarter, quarter), quarter)
        lhs = jnp.concatenate([hd[0, span, :], hd[1, span, :]], axis=1)
        part = pl.ds(half * (xs // 2), xs // 2)
        rhs = jnp.concatenate(
            [gw[1, p, part].reshape(d_model // 2, width) for p in range(4)], axis=1
        )
        return nt_dot(lhs, rhs)

    def sums(k, half, target):
        return remote(
            sb.at[k, half], rb.at[k, half], rs_send.at[2 * k + half], rs_recv.at[2 * k + half],
            (f, target),
        )

    to_core = [sums(0, half, t_core) for half in (0, 1)]
    far_sums = far_out([sb.at[1, half] for half in (0, 1)], rs_hop, 8)
    far_sums_on = far_on(rs_hop, lambda q, half: rb.at[1, half], 8)
    to_core2 = [sums(2, half, t_core) for half in (0, 1)]

    for half in (0, 1):
        sb[0, half] = partial(t_diag, half).astype(BF)
        to_core[half].start()
    for half in (0, 1):
        acc[half] = partial(t_far, half)
        to_core[half].wait_recv()
        sb[1, half] = (acc[half] + rb[0, half].astype(F32)).astype(BF)
        far_sums[half].start()
    for half in (0, 1):
        sb[2, half] = partial(t_core, half).astype(BF)
        to_core2[half].start()
    for half in (0, 1):
        acc[half] = partial(t, half)
    arrive(far_sums)
    start(far_sums_on)
    mine = pl.ds(pl.multiple_of(t * quarter, quarter), quarter)
    for half in (0, 1):
        to_core2[half].wait_recv()
        far_sums_on[half].wait_recv()
        for k in (0, 1):
            q = 2 * half + k
            cols = slice(k * feat, (k + 1) * feat)
            delta = acc[half, :, cols] + rb[2, half, :, cols].astype(F32) + rb[1, half, :, cols].astype(F32)
            at[q] = (tk[q, mine, :].astype(F32) + delta).astype(BF)

    at_copies = []
    for k in range(1, 4):
        q = (t + k) % 4
        at_copies.append(remote(at.at[q], ao.at[t], at_send.at[k - 1], at_recv.at[k - 1], (f, q)))
    ao[t] = at[t]

    fi_load.wait()
    fi_near.wait_recv()
    fi_relay.wait_recv()
    for copy in loads:
        copy.wait()
    pre = jnp.dot(
        jnp.concatenate([at[q] for q in range(4)], axis=1),
        fi[...].reshape(d_model, fi.shape[-1]),
        preferred_element_type=F32,
    )
    flux_hidden = jax.nn.gelu(pre, approximate=True).astype(BF)
    wn[1 + t] = jnp.dot(flux_hidden, wfo_ref[...], preferred_element_type=F32).astype(BF)
    fx_copies = []
    for k in range(1, 4):
        fx_copies.append(
            remote(wn.at[1 + t], wn.at[1 + t], fx_send.at[k - 1], fx_recv.at[k - 1], (f, (t + k) % 4))
        )
        fx_copies[-1].start()

    def rim(slot, source, target):
        return [
            remote(wn.at[source], wn.at[slot], rim_send.at[q], rim_recv.at[slot // 5], (target, q))
            for q in range(4)
        ]

    low = rim(0, 4, f_next)
    high = rim(5, 1, f_prev)

    @pl.when(t == 3)
    def _():
        for copy in low:
            copy.start()

    @pl.when(t == 0)
    def _():
        for copy in high:
            copy.start()

    for copy in fx_copies:
        copy.wait_recv()
    low[0].wait_recv()
    high[0].wait_recv()
    ocean(
        f, t, n_f, f_prev, f_next, remote, wn, sea_ref, couple_ref, sgain_ref, one_ref, two_ref,
        pick_ref, place_ref, out_ref, mk, oh, wb, st, pd, sh, cv, pk, rw, rn, halo_send, halo_recv, at_copies,
    )
    for copy in at_copies:
        copy.wait_recv()
    for q in range(4):
        atm_ref[pl.ds(q * quarter, quarter), :] = ao[q]

    @pl.when(t == 3)
    def _():
        for copy in low:
            copy.wait_send()

    @pl.when(t == 0)
    def _():
        for copy in high:
            copy.wait_send()

    for copy in y_copies + done + tok_out + [tok_near] + at_copies + fx_copies + to_core + far_sums + to_core2:
        copy.wait_send()


def body(
    tokens,
    ln_gain,
    w_up,
    w_down,
    w_flux_in,
    w_flux_out,
    ocean_state,
    land_mask,
    column_map,
    w_couple,
    dw_kernel,
    ocean_gain,
    w_pw1,
    w_pw2,
):
    xs, zs = XS, ZS
    rows, feat = tokens.shape
    d_model = 4 * feat
    shard, hidden = w_up.shape
    width = hidden // 4
    fh, flx = w_flux_out.shape
    quarter = rows // 4
    grid_rows, grid_cols, chans = ocean_state.shape
    cells = grid_rows * grid_cols
    pick, place = halo_matrices(grid_rows, grid_cols)
    dma = pltpu.SemaphoreType.DMA
    vm = pl.BlockSpec(memory_space=pltpu.VMEM)
    hb = pl.BlockSpec(memory_space=pl.ANY)
    return pl.pallas_call(
        functools.partial(atmosphere_kernel, xs, zs),
        out_shape=(
            jax.ShapeDtypeStruct((rows, feat), BF),
            jax.ShapeDtypeStruct(ocean_state.shape, BF),
        ),
        in_specs=[hb, vm, vm, vm, hb, hb, hb, vm, vm, hb, vm, vm, hb, hb, hb, hb],
        out_specs=(vm, vm),
        scratch_shapes=[
            pltpu.VMEM((2, shard, hidden), BF),
            pltpu.VMEM((2, 4, xs, zs, 2 * shard, width), BF),
            pltpu.VMEM((4, rows, feat), BF),
            pltpu.VMEM((rows, d_model), BF),
            pltpu.VMEM((2, rows, hidden // 2), BF),
            pltpu.VMEM((4, feat, fh), BF),
            pltpu.VMEM((3, 2, quarter, d_model // 2), BF),
            pltpu.VMEM((3, 2, quarter, d_model // 2), BF),
            pltpu.VMEM((2, quarter, d_model // 2), F32),
            pltpu.VMEM((4, quarter, feat), BF),
            pltpu.VMEM((4, quarter, feat), BF),
            pltpu.VMEM((6, quarter, flx), BF),
            dma((2,)), dma((2,)), dma((128,)), dma((128,)),
            dma((3,)), dma((3,)), dma((3,)), dma((3,)),
            dma((6,)), dma((6,)), dma((3,)), dma((3,)),
            dma((3,)), dma((3,)), dma((4,)), dma((2,)),
            pltpu.VMEM((cells, 128), F32),
            pltpu.VMEM((cells, 6 * quarter), BF),
            pltpu.VMEM((2, 7, 7, 8, chans), F32),
            pltpu.VMEM((2, cells, chans), BF),
            pltpu.VMEM((grid_rows + 6, grid_cols + 16, chans), F32),
            pltpu.VMEM((7, grid_rows + 6, grid_cols // 8, 8, chans), F32),
            pltpu.VMEM((grid_rows, grid_cols // 8, 8, chans), F32),
            pltpu.VMEM((2, 256, chans), BF),
            pltpu.VMEM((2, 256, chans), BF),
            pltpu.VMEM((2, 2, 3 * grid_cols, chans), BF),
            dma((16,)), dma((16,)),
            pltpu.VMEM(w_flux_out.shape, BF),
            pltpu.VMEM(ocean_state.shape, BF),
            pltpu.VMEM(w_couple.shape, BF),
            pltpu.VMEM(w_pw1.shape, BF),
            pltpu.VMEM(w_pw2.shape, BF),
            pltpu.VMEM(pick.shape, BF),
            pltpu.VMEM(place.shape, BF),
            dma((9,)),
            pltpu.VMEM((2, rows // 2, feat), BF),
            pltpu.VMEM((2, feat // 2, fh), BF),
            pltpu.VMEM((2, quarter, d_model // 2), BF),
            dma((12,)), dma((12,)),
        ],
        compiler_params=pltpu.CompilerParams(
            collective_id=0, has_side_effects=True, vmem_limit_bytes=60 * 1024 * 1024
        ),
        name="coupled_step",
    )(
        tokens, ln_gain, w_up, w_down.T, w_flux_in, w_flux_out,
        ocean_state, land_mask, column_map, w_couple, dw_kernel.transpose(1, 2, 0, 3), ocean_gain, w_pw1, w_pw2,
        pick, place,
    )


def solution(mesh):
    placed = (
        P("fsdp", "tile"),
        P(),
        P("fsdp", "tile"),
        P("tile", "fsdp"),
        P("tile", None),
        P(),
        P("fsdp", "tile", None),
        P("fsdp", "tile"),
        P("fsdp", "tile"),
        P(),
        P(),
        P(),
        P(),
        P(),
    )
    return jax.shard_map(
        body,
        mesh=mesh,
        in_specs=placed,
        out_specs=(P("fsdp", "tile"), P("fsdp", "tile", None)),
        check_vma=False,
    )
```

```python
import functools

import jax
import jax.numpy as jnp
from jax import lax
from jax.experimental import pallas as pl
from jax.experimental.pallas import tpu as pltpu
from jax.sharding import PartitionSpec as P
import numpy as np

MESH = pl.DeviceIdType.MESH
BF = jnp.bfloat16
F32 = jnp.float32
EPS = 1e-06
XS = 4
ZS = 8
FIRST = 32


def nt_dot(lhs, rhs):
    return lax.dot_general(lhs, rhs, (((1,), (1,)), ((), ())), preferred_element_type=F32)


def ocean_prepare(first, mask_ref, map_ref, taps_ref, mk, oh, wb):
    grid_rows, grid_cols = map_ref.shape
    tiles = oh.shape[1] // 128

    @pl.loop(0, grid_rows)
    def _(r):
        square = (grid_cols, grid_cols)
        eye = (
            lax.broadcasted_iota(jnp.int32, square, 0) == lax.broadcasted_iota(jnp.int32, square, 1)
        ).astype(F32)
        ones = jnp.ones((grid_cols, 128), BF)

        def upright(line):
            return jnp.dot((eye * line).astype(BF), ones, preferred_element_type=F32)

        index = map_ref[pl.ds(r, 1), :] - first
        high = upright((index >> 5).astype(F32))
        low = upright((index & 31).astype(F32))
        index_up = high * 32.0 + low
        span = pl.ds(pl.multiple_of(r * grid_cols, grid_cols), grid_cols)
        mk[span, :] = upright(mask_ref[pl.ds(r, 1), :].astype(F32))
        lane = lax.broadcasted_iota(jnp.int32, (grid_cols, 128), 1).astype(F32)
        for k in range(tiles):
            oh[span, k * 128 : (k + 1) * 128] = jnp.where(
                index_up == lane + 128.0 * k, 1.0, 0.0
            ).astype(BF)

    for k in range(taps_ref.shape[2]):
        for a in range(7):
            for b in range(7):
                wb[k, a, b] = jnp.broadcast_to(taps_ref[a, b, k : k + 1, :], wb.shape[3:])


def ocean(
    f, t, n_f, f_prev, f_next, remote, wn, sea_ref, couple_ref, sgain_ref, one_ref, two_ref,
    pick_ref, place_ref, out_ref, mk, oh, wb, st, pd, sh, cv, pk, rw, rn, halo_send, halo_recv, at_copies,
):
    grid_rows, grid_cols, chans = sea_ref.shape
    cells = 8 * grid_cols
    wide = pd.shape[1]
    t_next, t_prev = (t + 1) % 4, (t + 3) % 4
    edge = 3 * grid_cols

    def masked(span, values):
        return (jnp.concatenate([mk[span, :]] * (chans // 128), axis=1) * values).astype(BF)

    def keep(k, i, span, values):
        st[k, span, :] = values
        pd[pl.ds(3 + i * 8, 8), 8 : 8 + grid_cols, :] = values.astype(F32).reshape(
            8, grid_cols, chans
        )

    @pl.loop(0, grid_rows // 8)
    def _(i):
        span = pl.ds(pl.multiple_of(i * cells, cells), cells)
        picked = jnp.dot(
            oh[span, :], wn[...].reshape(oh.shape[1], wn.shape[2]), preferred_element_type=F32
        ).astype(BF)
        forcing = jnp.dot(picked, couple_ref[...], preferred_element_type=F32)
        before = sea_ref[pl.ds(i * 8, 8)].reshape(cells, chans).astype(F32)
        keep(0, i, span, masked(span, before + forcing))

    for k in range(2):
        pk[k] = jnp.dot(pick_ref[...], st[k], preferred_element_type=F32).astype(BF)
        last = grid_rows * grid_cols - edge
        moves = [
            (st.at[k, pl.ds(last, edge)], rn.at[k, 0], (f_next, t)),
            (st.at[k, pl.ds(0, edge)], rn.at[k, 1], (f_prev, t)),
            (pk.at[k, pl.ds(0, 96)], rw.at[k, pl.ds(0, 96)], (f, t_next)),
            (pk.at[k, pl.ds(96, 96)], rw.at[k, pl.ds(96, 96)], (f, t_prev)),
        ]
        corner = 192
        for fd in (f_prev, f_next):
            for td in (t_prev, t_next):
                part = pl.ds(corner, 16)
                moves.append((pk.at[k, part], rw.at[k, part], (fd, td)))
                corner += 16
        copies = [
            remote(src, dst, halo_send.at[k * 8 + j], halo_recv.at[k * 8 + j], device)
            for j, (src, dst, device) in enumerate(moves)
        ]
        for copy in copies:
            copy.start()
        for copy in copies:
            copy.wait_recv()
        if k == 0:
            for copy in at_copies:
                copy.start()
        above, below, left, right = f > 0, f < n_f - 1, t > 0, t < 3

        def valid(flag, values):
            return jnp.where(flag, values.astype(F32), 0.0)

        pd[0:3, 8 : 8 + grid_cols, :] = valid(above, rn[k, 0]).reshape(3, grid_cols, chans)
        pd[3 + grid_rows : 6 + grid_rows, 8 : 8 + grid_cols, :] = valid(below, rn[k, 1]).reshape(
            3, grid_cols, chans
        )
        flags = (
            left,
            right,
            jnp.logical_and(below, right),
            jnp.logical_and(below, left),
            jnp.logical_and(above, right),
            jnp.logical_and(above, left),
        )
        starts = (0, 96, 192, 208, 224, 240, 256)
        came = jnp.concatenate(
            [valid(flags[j], rw[k, starts[j] : starts[j + 1]]) for j in range(6)], axis=0
        ).astype(BF)
        strips = jnp.dot(place_ref[...], came, preferred_element_type=F32)
        count = (grid_rows + 6) * 8
        pd[:, 0:8, :] = strips[:count].reshape(grid_rows + 6, 8, chans)
        pd[:, wide - 8 : wide, :] = strips[count:].reshape(grid_rows + 6, 8, chans)

        @pl.loop(0, grid_rows + 6)
        def _(r):
            line = pd[r]
            for b in range(7):
                sh[b, r] = line[5 + b : 5 + b + grid_cols].reshape(grid_cols // 8, 8, chans)

        @pl.loop(0, (grid_rows // 4) * (chans // 128))
        def _(i):
            first = (i // (chans // 128)) * 4
            lanes = pl.ds(pl.multiple_of((i % (chans // 128)) * 128, 128), 128)
            totals = [jnp.zeros((grid_cols // 8, 8, 128), F32) for _ in range(4)]
            for b in range(7):
                weights = [wb[k, a, b, :, lanes] for a in range(7)]
                for r in range(10):
                    values = sh[b, first + r, :, :, lanes]
                    for j in range(4):
                        if 0 <= r - j < 7:
                            totals[j] = totals[j] + values * weights[r - j]
            for j in range(4):
                cv[first + j, :, :, lanes] = totals[j]

        @pl.loop(0, grid_rows // 8)
        def _(i):
            span = pl.ds(pl.multiple_of(i * cells, cells), cells)
            total = cv[pl.ds(i * 8, 8)].reshape(cells, chans)
            center = total - jnp.mean(total, axis=-1, keepdims=True)
            spread = jnp.mean(center * center, axis=-1, keepdims=True)
            pnorm = (center * lax.rsqrt(spread + EPS) * sgain_ref[k : k + 1, :]).astype(BF)
            inner = jax.nn.gelu(
                jnp.dot(pnorm, one_ref[k], preferred_element_type=F32), approximate=True
            ).astype(BF)
            lowered = jnp.dot(inner, two_ref[k], preferred_element_type=F32)
            values = masked(span, st[k, span, :].astype(F32) + lowered)
            if k == 0:
                keep(1, i, span, values)
            else:
                out_ref[pl.ds(i * 8, 8)] = values.reshape(8, grid_cols, chans)

        for copy in copies:
            copy.wait_send()


def order_matrix(group, count):
    matrix = np.zeros((group * count, group * count), np.float32)
    for k in range(count):
        for i in range(group):
            if i < FIRST:
                to = k * FIRST + i
            else:
                to = count * FIRST + k * (group - FIRST) + i - FIRST
            matrix[k * group + i, to] = 1
    return jnp.asarray(matrix, BF)


def halo_matrices(grid_rows, grid_cols):
    pick = np.zeros((256, grid_rows * grid_cols), np.float32)
    place = np.zeros((2 * (grid_rows + 6) * 8, 256), np.float32)
    side = (grid_rows + 6) * 8
    for r in range(grid_rows):
        for j in range(3):
            pick[r * 3 + j, r * grid_cols + grid_cols - 3 + j] = 1
            pick[96 + r * 3 + j, r * grid_cols + j] = 1
            place[(3 + r) * 8 + 5 + j, r * 3 + j] = 1
            place[side + (3 + r) * 8 + j, 96 + r * 3 + j] = 1
    corner = 192
    for down in (0, 1):
        for right in (0, 1):
            for i in range(3):
                for j in range(3):
                    row = grid_rows - 3 + i if down else i
                    col = grid_cols - 3 + j if right else j
                    pick[corner + i * 3 + j, row * grid_cols + col] = 1
                    to_row = i if down else grid_rows + 3 + i
                    to = to_row * 8 + 5 + j if right else side + to_row * 8 + j
                    place[to, corner + i * 3 + j] = 1
            corner += 16
    return jnp.asarray(pick, BF), jnp.asarray(place, BF)


def atmosphere_kernel(
    xs, zs,
    tok_ref, gain_ref, up_ref, down_ref, wfi_ref, wfo_hbm,
    sea_hbm, mask_ref, map_ref, couple_hbm, taps_ref, sgain_ref, one_hbm, two_hbm, pick_hbm, place_hbm, order_hbm,
    atm_ref, out_ref,
    yb, gw, gd0, gd1, tk, nm, hd, fi, sb0, sb1, rb0, rb1, acc0, acc1, tp, order_ref, at, ao, wn,
    y_send, y_recv, ring_send, ring_recv, tok_send, tok_recv, fi_send, fi_recv,
    rs_send, rs_recv, at_send, at_recv, fx_send, fx_recv, rim_send, rim_recv,
    mk, oh, wb, st, pd, sh, cv, pk, rw, rn, halo_send, halo_recv,
    wfo_ref, sea_ref, couple_ref, one_ref, two_ref, pick_ref, place_ref, load_sem,
    tok_hop, fi_hop, rs_hop0, rs_hop1, hop_send, hop_recv,
):
    f = lax.axis_index("fsdp")
    t = lax.axis_index("tile")
    n_f = 2 * xs * zs
    x, z, yl = f // (2 * zs), (f // 2) % zs, f % 2
    yh, c = t // 2, t % 2
    yp = f + 1 - 2 * yl
    x_right = (f + 2 * zs) % n_f
    x_left = (f - 2 * zs + n_f) % n_f
    z_right = x * 2 * zs + ((z + 1) % zs) * 2 + yl
    z_left = x * 2 * zs + ((z + zs - 1) % zs) * 2 + yl
    f_next, f_prev = (f + 1) % n_f, (f + n_f - 1) % n_f
    t_core = yh * 2 + (1 - c)
    t_far = (1 - yh) * 2 + c
    t_diag = (1 - yh) * 2 + (1 - c)
    rows = tok_ref.shape[0]
    quarter = rows // 4
    feat = tok_ref.shape[1]
    width = gw.shape[-1]
    weights = (gw, gd0, gd1)
    d_model = 4 * feat

    barrier = pltpu.get_barrier_semaphore()
    for other in (x_right, x_left, z_right, z_left):
        pl.semaphore_signal(barrier, inc=1, device_id=(other, t), device_id_type=MESH)
    for other in (t_core, t_far, t_diag):
        pl.semaphore_signal(barrier, inc=1, device_id=(f, other), device_id_type=MESH)
    for other in (f_prev, f_next):
        for q in range(4):
            pl.semaphore_signal(barrier, inc=1, device_id=(other, q), device_id_type=MESH)
    tok_load = pltpu.make_async_copy(tok_ref, tk.at[t], load_sem.at[0])
    fi_load = pltpu.make_async_copy(wfi_ref, fi.at[t], load_sem.at[1])
    loads = [
        pltpu.make_async_copy(src, dst, load_sem.at[2 + j])
        for j, (src, dst) in enumerate((
            (wfo_hbm, wfo_ref), (sea_hbm, sea_ref), (couple_hbm, couple_ref), (one_hbm, one_ref),
            (two_hbm, two_ref), (pick_hbm, pick_ref), (place_hbm, place_ref),
            (order_hbm, order_ref),
        ))
    ]
    tok_load.start()
    pl.semaphore_wait(barrier, 15)

    def remote(src, dst, send, recv, device):
        return pltpu.make_async_remote_copy(
            src_ref=src, dst_ref=dst, send_sem=send, recv_sem=recv,
            device_id=device, device_id_type=MESH,
        )

    y_copies = [
        remote(ref, yb.at[w], y_send.at[w], y_recv.at[w], (yp, t))
        for w, ref in enumerate((up_ref, down_ref))
    ]
    for copy in y_copies:
        copy.start()
    y_at = yh * 2 + yl
    y_ways = []
    for way in (1, 3):
        y_to = (y_at + way) % 4
        y_ways.append((f - yl + y_to % 2, (y_to // 2) * 2 + c))

    def far_out(src, hop, sem):
        return [
            remote(src[h], hop.at[h], hop_send.at[sem + h], hop_recv.at[sem + h], y_ways[h])
            for h in (0, 1)
        ]

    def far_on(hop, dst, sem):
        copies = []
        for h in (0, 1):
            origin = (1 - y_ways[h][1] // 2) * 2 + c
            copies.append(
                remote(
                    hop.at[h], dst(origin, h), hop_send.at[sem + 2 + h], hop_recv.at[sem + 2 + h],
                    y_ways[h],
                )
            )
        return copies

    half_rows, half_feat = rows // 2, feat // 2
    tok_parts = [pl.ds(h * half_rows, half_rows) for h in (0, 1)]
    fi_parts = [pl.ds(h * half_feat, half_feat) for h in (0, 1)]
    tok_out = far_out([tok_ref.at[part] for part in tok_parts], tok_hop, 0)
    tok_on = far_on(tok_hop, lambda q, h: tk.at[q, tok_parts[h]], 0)
    fi_out = far_out([wfi_ref.at[part] for part in fi_parts], fi_hop, 4)
    fi_on = far_on(fi_hop, lambda q, h: fi.at[q, fi_parts[h]], 4)
    tok_near = remote(tok_ref, tk.at[t], tok_send.at[0], tok_recv.at[0], (f, t_core))
    fi_near = remote(wfi_ref, fi.at[t], fi_send.at[0], fi_recv.at[0], (f, t_core))
    tok_relay = remote(tk.at[t_far], tk.at[t_far], tok_send.at[1], tok_recv.at[1], (f, t_core))
    fi_relay = remote(fi.at[t_far], fi.at[t_far], fi_send.at[1], fi_recv.at[1], (f, t_core))

    def ring_round(w, stream, stage, s):
        on_x = (stream == 0) == (stage == 0)
        n = xs if on_x else zs
        here = x if on_x else z
        last = s == n // 2 - 1
        copies = [[], []]
        for k in (0, 1):
            piece = 2 * stream + k
            for way in (0, 1):
                if last and way != k:
                    continue
                chunk = (here - s + n) % n if way == 0 else (here + s) % n
                if stage == 0:
                    part = weights[w].at[piece, chunk, z] if on_x else weights[w].at[piece, x, chunk]
                else:
                    part = weights[w].at[piece, chunk] if on_x else weights[w].at[piece, :, chunk]
                if on_x:
                    target = x_right if way == 0 else x_left
                else:
                    target = z_right if way == 0 else z_left
                at_sem = ((((w * 2 + stream) * 2 + stage) * 4 + s) * 2 + way) * 2 + k
                copies[k].append(
                    remote(part, part, ring_send.at[at_sem], ring_recv.at[at_sem], (target, t))
                )
        return copies

    done = []

    def start(copies):
        for copy in copies:
            copy.start()
        done.extend(copies)
        return copies

    def arrive(copies):
        for copy in copies:
            copy.wait_recv()

    def begin(w, stream):
        new = ring_round(w, stream, 0, 0)
        start(new[0] + new[1])
        return new

    def advance(old, w, stream, stage, s):
        new = ring_round(w, stream, stage, s)
        for k in (0, 1):
            arrive(old[k])
            start(new[k])
        return new

    def assemble(w, ref):
        y_copies[w].wait_recv()
        for p in range(4):
            mine = ref[:, p * width : (p + 1) * width].astype(F32)
            other = yb[w, :, p * width : (p + 1) * width].astype(F32)
            first = jnp.where(yl == 0, mine, other)
            second = jnp.where(yl == 0, other, mine)
            both = jnp.concatenate([first, second], axis=0).astype(BF)
            if w == 0:
                gw[p, x, z] = both
            else:
                gd0[p, x, z] = both[:FIRST]
                gd1[p, x, z] = both[FIRST:]

    for copy in tok_out:
        copy.start()
    tok_near.start()
    for copy in loads:
        copy.start()
    fi_load.start()
    assemble(0, up_ref)
    up_b = begin(0, 1)
    up_a = begin(0, 0)
    assemble(1, down_ref)
    up_a = advance(up_a, 0, 0, 0, 1)
    up_b = advance(up_b, 0, 1, 0, 1)
    down_b = begin(1, 1)
    up_b = advance(up_b, 0, 1, 0, 2)
    up_a = advance(up_a, 0, 0, 1, 0)
    arrive(tok_out)
    start(tok_on)
    up_b = advance(up_b, 0, 1, 0, 3)
    down_a = begin(1, 0)
    last_a = begin(2, 0)
    down_b = advance(down_b, 1, 1, 0, 1)
    up_b = advance(up_b, 0, 1, 1, 0)
    down_a = advance(down_a, 1, 0, 0, 1)
    down_b = advance(down_b, 1, 1, 0, 2)
    up_a = advance(up_a, 0, 0, 1, 1)
    last_b = begin(2, 1)
    last_a = advance(last_a, 2, 0, 0, 1)
    arrive(tok_on)
    start([tok_relay])
    start(fi_out)
    start([fi_near])
    down_b = advance(down_b, 1, 1, 0, 3)
    last_b = advance(last_b, 2, 1, 0, 1)
    tok_load.wait()
    tok_near.wait_recv()
    tok_relay.wait_recv()
    step = min(32, quarter)

    @pl.loop(0, rows // step)
    def _(i):
        span = pl.ds(pl.multiple_of(i * step, step), step)
        values = [tk[q, span, :].astype(F32) for q in range(4)]
        mean = sum(jnp.sum(v, axis=-1, keepdims=True) for v in values) / d_model
        centers = [v - mean for v in values]
        spread = sum(jnp.sum(v * v, axis=-1, keepdims=True) for v in centers) / d_model
        inverse = lax.rsqrt(spread + EPS)
        for q in range(4):
            gain = gain_ref[q * feat : (q + 1) * feat][None, :]
            nm[span, q * feat : (q + 1) * feat] = (centers[q] * inverse * gain).astype(BF)

    up_a = advance(up_a, 0, 0, 1, 2)
    up_b = advance(up_b, 0, 1, 1, 1)
    last_b = advance(last_b, 2, 1, 0, 2)
    loads[-1].wait()
    mine = pl.ds(pl.multiple_of(t * quarter, quarter), quarter)
    for half in (0, 1):
        natural = jnp.concatenate([tk[2 * half + k, mine, :] for k in (0, 1)], axis=1)
        tp[half] = jnp.dot(natural, order_ref[...], preferred_element_type=F32).astype(BF)
    ocean_prepare(f * rows - quarter, mask_ref, map_ref, taps_ref, mk, oh, wb)
    up_a = advance(up_a, 0, 0, 1, 3)
    last_b = advance(last_b, 2, 1, 0, 3)
    down_a = advance(down_a, 1, 0, 1, 0)
    arrive(fi_out)
    start(fi_on)
    arrive(up_b[0] + up_b[1])
    down_b = advance(down_b, 1, 1, 1, 0)
    arrive(up_a[0] + up_a[1])
    down_a = advance(down_a, 1, 0, 1, 1)

    def up_block(half, block):
        span = pl.ds(pl.multiple_of(block * quarter, quarter), quarter)
        rhs = jnp.concatenate(
            [gw[half * 2 + k].reshape(d_model, width) for k in (0, 1)], axis=1
        )
        pre = jnp.dot(nm[span, :], rhs, preferred_element_type=F32)
        hd[half, span, :] = jax.nn.gelu(pre, approximate=True).astype(BF)

    for half in (0, 1):
        @pl.loop(0, 4)
        def _(block):
            up_block(half, block)

        if half == 0:
            down_a = advance(down_a, 1, 0, 1, 2)
            down_b = advance(down_b, 1, 1, 1, 1)
            arrive(fi_on)
            start([fi_relay])
    down_a = advance(down_a, 1, 0, 1, 3)
    arrive(down_b[0] + down_b[1])
    last_b = advance(last_b, 2, 1, 1, 0)
    arrive(down_a[0] + down_a[1])
    last_a = advance(last_a, 2, 0, 1, 0)

    def partial(j, block, half):
        span = pl.ds(pl.multiple_of(block * quarter, quarter), quarter)
        lhs = jnp.concatenate([hd[0, span, :], hd[1, span, :]], axis=1)
        part = pl.ds(half * (xs // 2), xs // 2)
        source = (gd0, gd1)[j]
        count = xs // 2 * zs * source.shape[3]
        rhs = jnp.concatenate([source[p, part].reshape(count, width) for p in range(4)], axis=1)
        return nt_dot(lhs, rhs)

    def sums(j, k, half):
        at_sem = j * 6 + 2 * k + half
        return remote(
            sb[j].at[k, half], rb[j].at[k, half], rs_send.at[at_sem], rs_recv.at[at_sem], (f, t_core)
        )

    sb, rb, acc, rs_hop = (sb0, sb1), (rb0, rb1), (acc0, acc1), (rs_hop0, rs_hop1)
    to_core = [[sums(j, 0, half) for half in (0, 1)] for j in (0, 1)]
    to_core2 = [[sums(j, 2, half) for half in (0, 1)] for j in (0, 1)]
    far_sums = [far_out([sb[j].at[1, half] for half in (0, 1)], rs_hop[j], 8 + 4 * j) for j in (0, 1)]
    far_sums_on = [
        far_on(rs_hop[j], lambda q, half, j=j: rb[j].at[1, half], 8 + 4 * j) for j in (0, 1)
    ]

    def send_far(j):
        for half in (0, 1):
            sb[j][0, half] = partial(j, t_diag, half).astype(BF)
            start([to_core[j][half]])
        for half in (0, 1):
            acc[j][half] = partial(j, t_far, half)
            arrive([to_core[j][half]])
            sb[j][1, half] = (acc[j][half] + rb[j][0, half].astype(F32)).astype(BF)
            start([far_sums[j][half]])

    def send_core(j):
        for half in (0, 1):
            sb[j][2, half] = partial(j, t_core, half).astype(BF)
            start([to_core2[j][half]])
        for half in (0, 1):
            acc[j][half] = partial(j, t, half)

    send_far(0)
    last_a = advance(last_a, 2, 0, 1, 1)
    send_core(0)
    last_b = advance(last_b, 2, 1, 1, 1)
    last_a = advance(last_a, 2, 0, 1, 2)
    arrive(far_sums[0])
    start(far_sums_on[0])
    last_a = advance(last_a, 2, 0, 1, 3)
    arrive(last_b[0] + last_b[1])
    arrive(last_a[0] + last_a[1])
    send_far(1)
    send_core(1)
    arrive(far_sums[1])
    start(far_sums_on[1])

    for j in (0, 1):
        arrive(to_core2[j])
        for half in (0, 1):
            acc[j][half] = acc[j][half] + rb[j][2, half].astype(F32)
    for half in (0, 1):
        deltas = []
        for j in (0, 1):
            arrive([far_sums_on[j][half]])
            deltas.append(acc[j][half] + rb[j][1, half].astype(F32))
        changed = (tp[half].astype(F32) + jnp.concatenate(deltas, axis=1)).astype(BF)
        natural = nt_dot(changed, order_ref[...]).astype(BF)
        for k in (0, 1):
            at[2 * half + k] = natural[:, k * feat : (k + 1) * feat]

    at_copies = []
    for k in range(1, 4):
        q = (t + k) % 4
        at_copies.append(remote(at.at[q], ao.at[t], at_send.at[k - 1], at_recv.at[k - 1], (f, q)))
    ao[t] = at[t]

    fi_load.wait()
    fi_near.wait_recv()
    fi_relay.wait_recv()
    for copy in loads[:-1]:
        copy.wait()
    pre = jnp.dot(
        jnp.concatenate([at[q] for q in range(4)], axis=1),
        fi[...].reshape(d_model, fi.shape[-1]),
        preferred_element_type=F32,
    )
    flux_hidden = jax.nn.gelu(pre, approximate=True).astype(BF)
    wn[1 + t] = jnp.dot(flux_hidden, wfo_ref[...], preferred_element_type=F32).astype(BF)
    fx_copies = []
    for k in range(1, 4):
        fx_copies.append(
            remote(wn.at[1 + t], wn.at[1 + t], fx_send.at[k - 1], fx_recv.at[k - 1], (f, (t + k) % 4))
        )
        fx_copies[-1].start()

    def rim(slot, source, target):
        return [
            remote(wn.at[source], wn.at[slot], rim_send.at[q], rim_recv.at[slot // 5], (target, q))
            for q in range(4)
        ]

    low = rim(0, 4, f_next)
    high = rim(5, 1, f_prev)

    @pl.when(t == 3)
    def _():
        for copy in low:
            copy.start()

    @pl.when(t == 0)
    def _():
        for copy in high:
            copy.start()

    for copy in fx_copies:
        copy.wait_recv()
    low[0].wait_recv()
    high[0].wait_recv()
    ocean(
        f, t, n_f, f_prev, f_next, remote, wn, sea_ref, couple_ref, sgain_ref, one_ref, two_ref,
        pick_ref, place_ref, out_ref, mk, oh, wb, st, pd, sh, cv, pk, rw, rn, halo_send, halo_recv, at_copies,
    )
    for copy in at_copies:
        copy.wait_recv()
    for q in range(4):
        atm_ref[pl.ds(q * quarter, quarter), :] = ao[q]

    @pl.when(t == 3)
    def _():
        for copy in low:
            copy.wait_send()

    @pl.when(t == 0)
    def _():
        for copy in high:
            copy.wait_send()

    for copy in y_copies + done + tok_out + [tok_near] + at_copies + fx_copies:
        copy.wait_send()


def body(
    tokens,
    ln_gain,
    w_up,
    w_down,
    w_flux_in,
    w_flux_out,
    ocean_state,
    land_mask,
    column_map,
    w_couple,
    dw_kernel,
    ocean_gain,
    w_pw1,
    w_pw2,
):
    xs, zs = XS, ZS
    rows, feat = tokens.shape
    d_model = 4 * feat
    shard, hidden = w_up.shape
    width = hidden // 4
    fh, flx = w_flux_out.shape
    quarter = rows // 4
    grid_rows, grid_cols, chans = ocean_state.shape
    cells = grid_rows * grid_cols
    pick, place = halo_matrices(grid_rows, grid_cols)
    order = order_matrix(2 * shard, xs * zs // 2)
    parts = (xs * zs // 2 * FIRST, xs * zs // 2 * (2 * shard - FIRST))
    dma = pltpu.SemaphoreType.DMA
    vm = pl.BlockSpec(memory_space=pltpu.VMEM)
    hb = pl.BlockSpec(memory_space=pl.ANY)
    return pl.pallas_call(
        functools.partial(atmosphere_kernel, xs, zs),
        out_shape=(
            jax.ShapeDtypeStruct((rows, feat), BF),
            jax.ShapeDtypeStruct(ocean_state.shape, BF),
        ),
        in_specs=[hb, vm, vm, vm, hb, hb, hb, vm, vm, hb, vm, vm, hb, hb, hb, hb, hb],
        out_specs=(vm, vm),
        scratch_shapes=[
            pltpu.VMEM((2, shard, hidden), BF),
            pltpu.VMEM((4, xs, zs, 2 * shard, width), BF),
            pltpu.VMEM((4, xs, zs, FIRST, width), BF),
            pltpu.VMEM((4, xs, zs, 2 * shard - FIRST, width), BF),
            pltpu.VMEM((4, rows, feat), BF),
            pltpu.VMEM((rows, d_model), BF),
            pltpu.VMEM((2, rows, hidden // 2), BF),
            pltpu.VMEM((4, feat, fh), BF),
            *(pltpu.VMEM((3, 2, quarter, n), BF) for n in parts),
            *(pltpu.VMEM((3, 2, quarter, n), BF) for n in parts),
            *(pltpu.VMEM((2, quarter, n), F32) for n in parts),
            pltpu.VMEM((2, quarter, d_model // 2), BF),
            pltpu.VMEM(order.shape, BF),
            pltpu.VMEM((4, quarter, feat), BF),
            pltpu.VMEM((4, quarter, feat), BF),
            pltpu.VMEM((6, quarter, flx), BF),
            dma((2,)), dma((2,)), dma((192,)), dma((192,)),
            dma((3,)), dma((3,)), dma((3,)), dma((3,)),
            dma((12,)), dma((12,)), dma((3,)), dma((3,)),
            dma((3,)), dma((3,)), dma((4,)), dma((2,)),
            pltpu.VMEM((cells, 128), F32),
            pltpu.VMEM((cells, 6 * quarter), BF),
            pltpu.VMEM((2, 7, 7, 8, chans), F32),
            pltpu.VMEM((2, cells, chans), BF),
            pltpu.VMEM((grid_rows + 6, grid_cols + 16, chans), F32),
            pltpu.VMEM((7, grid_rows + 6, grid_cols // 8, 8, chans), F32),
            pltpu.VMEM((grid_rows, grid_cols // 8, 8, chans), F32),
            pltpu.VMEM((2, 256, chans), BF),
            pltpu.VMEM((2, 256, chans), BF),
            pltpu.VMEM((2, 2, 3 * grid_cols, chans), BF),
            dma((16,)), dma((16,)),
            pltpu.VMEM(w_flux_out.shape, BF),
            pltpu.VMEM(ocean_state.shape, BF),
            pltpu.VMEM(w_couple.shape, BF),
            pltpu.VMEM(w_pw1.shape, BF),
            pltpu.VMEM(w_pw2.shape, BF),
            pltpu.VMEM(pick.shape, BF),
            pltpu.VMEM(place.shape, BF),
            dma((10,)),
            pltpu.VMEM((2, rows // 2, feat), BF),
            pltpu.VMEM((2, feat // 2, fh), BF),
            *(pltpu.VMEM((2, quarter, n), BF) for n in parts),
            dma((16,)), dma((16,)),
        ],
        compiler_params=pltpu.CompilerParams(
            collective_id=0, has_side_effects=True, vmem_limit_bytes=60 * 1024 * 1024
        ),
        name="coupled_step",
    )(
        tokens, ln_gain, w_up, w_down.T, w_flux_in, w_flux_out,
        ocean_state, land_mask, column_map, w_couple, dw_kernel.transpose(1, 2, 0, 3), ocean_gain, w_pw1, w_pw2,
        pick, place, order,
    )


def solution(mesh):
    placed = (
        P("fsdp", "tile"),
        P(),
        P("fsdp", "tile"),
        P("tile", "fsdp"),
        P("tile", None),
        P(),
        P("fsdp", "tile", None),
        P("fsdp", "tile"),
        P("fsdp", "tile"),
        P(),
        P(),
        P(),
        P(),
        P(),
    )
    return jax.shard_map(
        body,
        mesh=mesh,
        in_specs=placed,
        out_specs=(P("fsdp", "tile"), P("fsdp", "tile", None)),
        check_vma=False,
    )
```

```python
import functools

import jax
import jax.numpy as jnp
from jax import lax
from jax.experimental import pallas as pl
from jax.experimental.pallas import tpu as pltpu
from jax.sharding import PartitionSpec as P
import numpy as np

MESH = pl.DeviceIdType.MESH
BF = jnp.bfloat16
F32 = jnp.float32
EPS = 1e-06
XS = 4
ZS = 8


def nt_dot(lhs, rhs):
    return lax.dot_general(lhs, rhs, (((1,), (1,)), ((), ())), preferred_element_type=F32)


def ocean_prepare(first, mask_ref, map_ref, taps_ref, mk, oh, wb):
    grid_rows, grid_cols = map_ref.shape
    tiles = oh.shape[1] // 128

    @pl.loop(0, grid_rows)
    def _(r):
        square = (grid_cols, grid_cols)
        eye = (
            lax.broadcasted_iota(jnp.int32, square, 0) == lax.broadcasted_iota(jnp.int32, square, 1)
        ).astype(F32)
        ones = jnp.ones((grid_cols, 128), BF)

        def upright(line):
            return jnp.dot((eye * line).astype(BF), ones, preferred_element_type=F32)

        index = map_ref[pl.ds(r, 1), :] - first
        high = upright((index >> 5).astype(F32))
        low = upright((index & 31).astype(F32))
        index_up = high * 32.0 + low
        span = pl.ds(pl.multiple_of(r * grid_cols, grid_cols), grid_cols)
        mk[span, :] = upright(mask_ref[pl.ds(r, 1), :].astype(F32))
        lane = lax.broadcasted_iota(jnp.int32, (grid_cols, 128), 1).astype(F32)
        for k in range(tiles):
            oh[span, k * 128 : (k + 1) * 128] = jnp.where(
                index_up == lane + 128.0 * k, 1.0, 0.0
            ).astype(BF)

    for k in range(taps_ref.shape[2]):
        for a in range(7):
            for b in range(7):
                wb[k, a, b] = jnp.broadcast_to(taps_ref[a, b, k : k + 1, :], wb.shape[3:])


def ocean(
    f, t, n_f, f_prev, f_next, remote, wn, sea_ref, couple_ref, sgain_ref, one_ref, two_ref,
    pick_ref, place_ref, out_ref, mk, oh, wb, st, pd, sh, cv, pk, rw, rn, halo_send, halo_recv, at_copies,
):
    grid_rows, grid_cols, chans = sea_ref.shape
    cells = 8 * grid_cols
    wide = pd.shape[1]
    t_next, t_prev = (t + 1) % 4, (t + 3) % 4
    edge = 3 * grid_cols

    def masked(span, values):
        return (jnp.concatenate([mk[span, :]] * (chans // 128), axis=1) * values).astype(BF)

    def keep(k, i, span, values):
        st[k, span, :] = values
        pd[pl.ds(3 + i * 8, 8), 8 : 8 + grid_cols, :] = values.astype(F32).reshape(
            8, grid_cols, chans
        )

    @pl.loop(0, grid_rows // 8)
    def _(i):
        span = pl.ds(pl.multiple_of(i * cells, cells), cells)
        picked = jnp.dot(
            oh[span, :], wn[...].reshape(oh.shape[1], wn.shape[2]), preferred_element_type=F32
        ).astype(BF)
        forcing = jnp.dot(picked, couple_ref[...], preferred_element_type=F32)
        before = sea_ref[pl.ds(i * 8, 8)].reshape(cells, chans).astype(F32)
        keep(0, i, span, masked(span, before + forcing))

    for k in range(2):
        pk[k] = jnp.dot(pick_ref[...], st[k], preferred_element_type=F32).astype(BF)
        last = grid_rows * grid_cols - edge
        moves = [
            (st.at[k, pl.ds(last, edge)], rn.at[k, 0], (f_next, t)),
            (st.at[k, pl.ds(0, edge)], rn.at[k, 1], (f_prev, t)),
            (pk.at[k, pl.ds(0, 96)], rw.at[k, pl.ds(0, 96)], (f, t_next)),
            (pk.at[k, pl.ds(96, 96)], rw.at[k, pl.ds(96, 96)], (f, t_prev)),
        ]
        corner = 192
        for fd in (f_prev, f_next):
            for td in (t_prev, t_next):
                part = pl.ds(corner, 16)
                moves.append((pk.at[k, part], rw.at[k, part], (fd, td)))
                corner += 16
        copies = [
            remote(src, dst, halo_send.at[k * 8 + j], halo_recv.at[k * 8 + j], device)
            for j, (src, dst, device) in enumerate(moves)
        ]
        for copy in copies:
            copy.start()
        for copy in copies:
            copy.wait_recv()
        if k == 0:
            for copy in at_copies:
                copy.start()
        above, below, left, right = f > 0, f < n_f - 1, t > 0, t < 3

        def valid(flag, values):
            return jnp.where(flag, values.astype(F32), 0.0)

        pd[0:3, 8 : 8 + grid_cols, :] = valid(above, rn[k, 0]).reshape(3, grid_cols, chans)
        pd[3 + grid_rows : 6 + grid_rows, 8 : 8 + grid_cols, :] = valid(below, rn[k, 1]).reshape(
            3, grid_cols, chans
        )
        flags = (
            left,
            right,
            jnp.logical_and(below, right),
            jnp.logical_and(below, left),
            jnp.logical_and(above, right),
            jnp.logical_and(above, left),
        )
        starts = (0, 96, 192, 208, 224, 240, 256)
        came = jnp.concatenate(
            [valid(flags[j], rw[k, starts[j] : starts[j + 1]]) for j in range(6)], axis=0
        ).astype(BF)
        strips = jnp.dot(place_ref[...], came, preferred_element_type=F32)
        count = (grid_rows + 6) * 8
        pd[:, 0:8, :] = strips[:count].reshape(grid_rows + 6, 8, chans)
        pd[:, wide - 8 : wide, :] = strips[count:].reshape(grid_rows + 6, 8, chans)

        @pl.loop(0, grid_rows + 6)
        def _(r):
            line = pd[r]
            for b in range(7):
                sh[b, r] = line[5 + b : 5 + b + grid_cols].reshape(grid_cols // 8, 8, chans)

        @pl.loop(0, (grid_rows // 4) * (chans // 128))
        def _(i):
            first = (i // (chans // 128)) * 4
            lanes = pl.ds(pl.multiple_of((i % (chans // 128)) * 128, 128), 128)
            totals = [jnp.zeros((grid_cols // 8, 8, 128), F32) for _ in range(4)]
            for b in range(7):
                weights = [wb[k, a, b, :, lanes] for a in range(7)]
                for r in range(10):
                    values = sh[b, first + r, :, :, lanes]
                    for j in range(4):
                        if 0 <= r - j < 7:
                            totals[j] = totals[j] + values * weights[r - j]
            for j in range(4):
                cv[first + j, :, :, lanes] = totals[j]

        @pl.loop(0, grid_rows // 8)
        def _(i):
            span = pl.ds(pl.multiple_of(i * cells, cells), cells)
            total = cv[pl.ds(i * 8, 8)].reshape(cells, chans)
            center = total - jnp.mean(total, axis=-1, keepdims=True)
            spread = jnp.mean(center * center, axis=-1, keepdims=True)
            pnorm = (center * lax.rsqrt(spread + EPS) * sgain_ref[k : k + 1, :]).astype(BF)
            inner = jax.nn.gelu(
                jnp.dot(pnorm, one_ref[k], preferred_element_type=F32), approximate=True
            ).astype(BF)
            lowered = jnp.dot(inner, two_ref[k], preferred_element_type=F32)
            values = masked(span, st[k, span, :].astype(F32) + lowered)
            if k == 0:
                keep(1, i, span, values)
            else:
                out_ref[pl.ds(i * 8, 8)] = values.reshape(8, grid_cols, chans)

        for copy in copies:
            copy.wait_send()


def halo_matrices(grid_rows, grid_cols):
    pick = np.zeros((256, grid_rows * grid_cols), np.float32)
    place = np.zeros((2 * (grid_rows + 6) * 8, 256), np.float32)
    side = (grid_rows + 6) * 8
    for r in range(grid_rows):
        for j in range(3):
            pick[r * 3 + j, r * grid_cols + grid_cols - 3 + j] = 1
            pick[96 + r * 3 + j, r * grid_cols + j] = 1
            place[(3 + r) * 8 + 5 + j, r * 3 + j] = 1
            place[side + (3 + r) * 8 + j, 96 + r * 3 + j] = 1
    corner = 192
    for down in (0, 1):
        for right in (0, 1):
            for i in range(3):
                for j in range(3):
                    row = grid_rows - 3 + i if down else i
                    col = grid_cols - 3 + j if right else j
                    pick[corner + i * 3 + j, row * grid_cols + col] = 1
                    to_row = i if down else grid_rows + 3 + i
                    to = to_row * 8 + 5 + j if right else side + to_row * 8 + j
                    place[to, corner + i * 3 + j] = 1
            corner += 16
    return jnp.asarray(pick, BF), jnp.asarray(place, BF)


def atmosphere_kernel(
    xs, zs,
    tok_ref, gain_ref, up_ref, down_ref, wfi_ref, wfo_hbm,
    sea_hbm, mask_ref, map_ref, couple_hbm, taps_ref, sgain_ref, one_hbm, two_hbm, pick_hbm, place_hbm,
    atm_ref, out_ref,
    yb, gw, tk, nm, hd, fi, sb, rb, acc, at, ao, wn,
    y_send, y_recv, ring_send, ring_recv, tok_send, tok_recv, fi_send, fi_recv,
    rs_send, rs_recv, at_send, at_recv, fx_send, fx_recv, rim_send, rim_recv,
    mk, oh, wb, st, pd, sh, cv, pk, rw, rn, halo_send, halo_recv,
    wfo_ref, sea_ref, couple_ref, one_ref, two_ref, pick_ref, place_ref, load_sem,
    tok_hop, fi_hop, rs_hop, hop_send, hop_recv,
):
    f = lax.axis_index("fsdp")
    t = lax.axis_index("tile")
    n_f = 2 * xs * zs
    x, z, yl = f // (2 * zs), (f // 2) % zs, f % 2
    yh, c = t // 2, t % 2
    yp = f + 1 - 2 * yl
    x_right = (f + 2 * zs) % n_f
    x_left = (f - 2 * zs + n_f) % n_f
    z_right = x * 2 * zs + ((z + 1) % zs) * 2 + yl
    z_left = x * 2 * zs + ((z + zs - 1) % zs) * 2 + yl
    f_next, f_prev = (f + 1) % n_f, (f + n_f - 1) % n_f
    t_core = yh * 2 + (1 - c)
    t_far = (1 - yh) * 2 + c
    t_diag = (1 - yh) * 2 + (1 - c)
    rows = tok_ref.shape[0]
    quarter = rows // 4
    feat = tok_ref.shape[1]
    width = gw.shape[-1]
    d_model = 4 * feat

    barrier = pltpu.get_barrier_semaphore()
    for other in (x_right, x_left, z_right, z_left):
        pl.semaphore_signal(barrier, inc=1, device_id=(other, t), device_id_type=MESH)
    for other in (t_core, t_far, t_diag):
        pl.semaphore_signal(barrier, inc=1, device_id=(f, other), device_id_type=MESH)
    for other in (f_prev, f_next):
        for q in range(4):
            pl.semaphore_signal(barrier, inc=1, device_id=(other, q), device_id_type=MESH)
    tok_load = pltpu.make_async_copy(tok_ref, tk.at[t], load_sem.at[0])
    fi_load = pltpu.make_async_copy(wfi_ref, fi.at[t], load_sem.at[1])
    loads = [
        pltpu.make_async_copy(src, dst, load_sem.at[2 + j])
        for j, (src, dst) in enumerate((
            (wfo_hbm, wfo_ref), (sea_hbm, sea_ref), (couple_hbm, couple_ref), (one_hbm, one_ref),
            (two_hbm, two_ref), (pick_hbm, pick_ref), (place_hbm, place_ref),
        ))
    ]
    tok_load.start()
    pl.semaphore_wait(barrier, 15)

    def remote(src, dst, send, recv, device):
        return pltpu.make_async_remote_copy(
            src_ref=src, dst_ref=dst, send_sem=send, recv_sem=recv,
            device_id=device, device_id_type=MESH,
        )

    y_copies = [
        remote(ref, yb.at[w], y_send.at[w], y_recv.at[w], (yp, t))
        for w, ref in enumerate((up_ref, down_ref))
    ]
    for copy in y_copies:
        copy.start()
    y_at = yh * 2 + yl
    y_ways = []
    for way in (1, 3):
        y_to = (y_at + way) % 4
        y_ways.append((f - yl + y_to % 2, (y_to // 2) * 2 + c))

    def far_out(src, hop, sem):
        return [
            remote(src[h], hop.at[h], hop_send.at[sem + h], hop_recv.at[sem + h], y_ways[h])
            for h in (0, 1)
        ]

    def far_on(hop, dst, sem):
        copies = []
        for h in (0, 1):
            origin = (1 - y_ways[h][1] // 2) * 2 + c
            copies.append(
                remote(
                    hop.at[h], dst(origin, h), hop_send.at[sem + 2 + h], hop_recv.at[sem + 2 + h],
                    y_ways[h],
                )
            )
        return copies

    half_rows, half_feat = rows // 2, feat // 2
    tok_parts = [pl.ds(h * half_rows, half_rows) for h in (0, 1)]
    fi_parts = [pl.ds(h * half_feat, half_feat) for h in (0, 1)]
    tok_out = far_out([tok_ref.at[part] for part in tok_parts], tok_hop, 0)
    tok_on = far_on(tok_hop, lambda q, h: tk.at[q, tok_parts[h]], 0)
    fi_out = far_out([wfi_ref.at[part] for part in fi_parts], fi_hop, 4)
    fi_on = far_on(fi_hop, lambda q, h: fi.at[q, fi_parts[h]], 4)
    tok_near = remote(tok_ref, tk.at[t], tok_send.at[0], tok_recv.at[0], (f, t_core))
    fi_near = remote(wfi_ref, fi.at[t], fi_send.at[0], fi_recv.at[0], (f, t_core))
    tok_relay = remote(tk.at[t_far], tk.at[t_far], tok_send.at[1], tok_recv.at[1], (f, t_core))
    fi_relay = remote(fi.at[t_far], fi.at[t_far], fi_send.at[1], fi_recv.at[1], (f, t_core))

    def ring_round(w, stream, stage, s):
        on_x = (stream == 0) == (stage == 0)
        n = xs if on_x else zs
        here = x if on_x else z
        last = s == n // 2 - 1
        copies = [[], []]
        for k in (0, 1):
            piece = 2 * stream + k
            for way in (0, 1):
                if last and way != k:
                    continue
                chunk = (here - s + n) % n if way == 0 else (here + s) % n
                if stage == 0:
                    part = gw.at[w, piece, chunk, z] if on_x else gw.at[w, piece, x, chunk]
                else:
                    part = gw.at[w, piece, chunk] if on_x else gw.at[w, piece, :, chunk]
                if on_x:
                    target = x_right if way == 0 else x_left
                else:
                    target = z_right if way == 0 else z_left
                at_sem = ((((w * 2 + stream) * 2 + stage) * 4 + s) * 2 + way) * 2 + k
                copies[k].append(
                    remote(part, part, ring_send.at[at_sem], ring_recv.at[at_sem], (target, t))
                )
        return copies

    done = []

    def start(copies):
        for copy in copies:
            copy.start()
        done.extend(copies)
        return copies

    def arrive(copies):
        for copy in copies:
            copy.wait_recv()

    def begin(w, stream):
        new = ring_round(w, stream, 0, 0)
        start(new[0] + new[1])
        return new

    def advance(old, w, stream, stage, s):
        new = ring_round(w, stream, stage, s)
        for k in (0, 1):
            arrive(old[k])
            start(new[k])
        return new

    def assemble(w, ref):
        y_copies[w].wait_recv()
        for p in range(4):
            mine = ref[:, p * width : (p + 1) * width].astype(F32)
            other = yb[w, :, p * width : (p + 1) * width].astype(F32)
            first = jnp.where(yl == 0, mine, other)
            second = jnp.where(yl == 0, other, mine)
            gw[w, p, x, z] = jnp.concatenate([first, second], axis=0).astype(BF)

    for copy in tok_out:
        copy.start()
    tok_near.start()
    for copy in loads:
        copy.start()
    fi_load.start()
    assemble(0, up_ref)
    up_b = begin(0, 1)
    up_a = begin(0, 0)
    assemble(1, down_ref)
    down_b = begin(1, 1)
    down_a = begin(1, 0)
    up_a = advance(up_a, 0, 0, 0, 1)
    up_b = advance(up_b, 0, 1, 0, 1)
    down_b = advance(down_b, 1, 1, 0, 1)
    down_a = advance(down_a, 1, 0, 0, 1)
    up_b = advance(up_b, 0, 1, 0, 2)
    down_b = advance(down_b, 1, 1, 0, 2)
    up_b = advance(up_b, 0, 1, 0, 3)
    up_a = advance(up_a, 0, 0, 1, 0)
    down_b = advance(down_b, 1, 1, 0, 3)
    up_b = advance(up_b, 0, 1, 1, 0)
    arrive(tok_out)
    start(tok_on)
    down_a = advance(down_a, 1, 0, 1, 0)
    down_b = advance(down_b, 1, 1, 1, 0)
    up_a = advance(up_a, 0, 0, 1, 1)
    arrive(tok_on)
    start([tok_relay])
    start(fi_out)
    start([fi_near])
    down_a = advance(down_a, 1, 0, 1, 1)
    tok_load.wait()
    tok_near.wait_recv()
    tok_relay.wait_recv()
    step = min(32, quarter)

    @pl.loop(0, rows // step)
    def _(i):
        span = pl.ds(pl.multiple_of(i * step, step), step)
        values = [tk[q, span, :].astype(F32) for q in range(4)]
        mean = sum(jnp.sum(v, axis=-1, keepdims=True) for v in values) / d_model
        centers = [v - mean for v in values]
        spread = sum(jnp.sum(v * v, axis=-1, keepdims=True) for v in centers) / d_model
        inverse = lax.rsqrt(spread + EPS)
        for q in range(4):
            gain = gain_ref[q * feat : (q + 1) * feat][None, :]
            nm[span, q * feat : (q + 1) * feat] = (centers[q] * inverse * gain).astype(BF)

    up_b = advance(up_b, 0, 1, 1, 1)
    up_a = advance(up_a, 0, 0, 1, 2)
    down_b = advance(down_b, 1, 1, 1, 1)
    down_a = advance(down_a, 1, 0, 1, 2)
    ocean_prepare(f * rows - quarter, mask_ref, map_ref, taps_ref, mk, oh, wb)
    up_a = advance(up_a, 0, 0, 1, 3)
    down_a = advance(down_a, 1, 0, 1, 3)
    arrive(fi_out)
    start(fi_on)
    arrive(up_b[0] + up_b[1])
    arrive(up_a[0] + up_a[1])

    def up_block(half, block):
        span = pl.ds(pl.multiple_of(block * quarter, quarter), quarter)
        rhs = jnp.concatenate(
            [gw[0, half * 2 + k].reshape(d_model, width) for k in (0, 1)], axis=1
        )
        pre = jnp.dot(nm[span, :], rhs, preferred_element_type=F32)
        hd[half, span, :] = jax.nn.gelu(pre, approximate=True).astype(BF)

    for half in (0, 1):
        @pl.loop(0, 4)
        def _(block):
            up_block(half, block)

        if half == 0:
            arrive(fi_on)
            start([fi_relay])
    arrive(down_b[0] + down_b[1])
    arrive(down_a[0] + down_a[1])

    def partial(block, half):
        span = pl.ds(pl.multiple_of(block * quarter, quarter), quarter)
        lhs = jnp.concatenate([hd[0, span, :], hd[1, span, :]], axis=1)
        part = pl.ds(half * (xs // 2), xs // 2)
        rhs = jnp.concatenate(
            [gw[1, p, part].reshape(d_model // 2, width) for p in range(4)], axis=1
        )
        return nt_dot(lhs, rhs)

    def sums(k, half, target):
        return remote(
            sb.at[k, half], rb.at[k, half], rs_send.at[2 * k + half], rs_recv.at[2 * k + half],
            (f, target),
        )

    to_core = [sums(0, half, t_core) for half in (0, 1)]
    far_sums = far_out([sb.at[1, half] for half in (0, 1)], rs_hop, 8)
    far_sums_on = far_on(rs_hop, lambda q, half: rb.at[1, half], 8)
    to_core2 = [sums(2, half, t_core) for half in (0, 1)]

    for half in (0, 1):
        sb[0, half] = partial(t_diag, half).astype(BF)
        to_core[half].start()
    for half in (0, 1):
        acc[half] = partial(t_far, half)
        to_core[half].wait_recv()
        sb[1, half] = (acc[half] + rb[0, half].astype(F32)).astype(BF)
        far_sums[half].start()
    for half in (0, 1):
        sb[2, half] = partial(t_core, half).astype(BF)
        to_core2[half].start()
    for half in (0, 1):
        acc[half] = partial(t, half)
    arrive(far_sums)
    start(far_sums_on)
    mine = pl.ds(pl.multiple_of(t * quarter, quarter), quarter)
    for half in (0, 1):
        to_core2[half].wait_recv()
        far_sums_on[half].wait_recv()
        for k in (0, 1):
            q = 2 * half + k
            cols = slice(k * feat, (k + 1) * feat)
            delta = acc[half, :, cols] + rb[2, half, :, cols].astype(F32) + rb[1, half, :, cols].astype(F32)
            at[q] = (tk[q, mine, :].astype(F32) + delta).astype(BF)

    at_copies = []
    for k in range(1, 4):
        q = (t + k) % 4
        at_copies.append(remote(at.at[q], ao.at[t], at_send.at[k - 1], at_recv.at[k - 1], (f, q)))
    ao[t] = at[t]

    fi_load.wait()
    fi_near.wait_recv()
    fi_relay.wait_recv()
    for copy in loads:
        copy.wait()
    pre = jnp.dot(
        jnp.concatenate([at[q] for q in range(4)], axis=1),
        fi[...].reshape(d_model, fi.shape[-1]),
        preferred_element_type=F32,
    )
    flux_hidden = jax.nn.gelu(pre, approximate=True).astype(BF)
    wn[1 + t] = jnp.dot(flux_hidden, wfo_ref[...], preferred_element_type=F32).astype(BF)
    fx_copies = []
    for k in range(1, 4):
        fx_copies.append(
            remote(wn.at[1 + t], wn.at[1 + t], fx_send.at[k - 1], fx_recv.at[k - 1], (f, (t + k) % 4))
        )
        fx_copies[-1].start()

    def rim(slot, source, target):
        return [
            remote(wn.at[source], wn.at[slot], rim_send.at[q], rim_recv.at[slot // 5], (target, q))
            for q in range(4)
        ]

    low = rim(0, 4, f_next)
    high = rim(5, 1, f_prev)

    @pl.when(t == 3)
    def _():
        for copy in low:
            copy.start()

    @pl.when(t == 0)
    def _():
        for copy in high:
            copy.start()

    for copy in fx_copies:
        copy.wait_recv()
    low[0].wait_recv()
    high[0].wait_recv()
    ocean(
        f, t, n_f, f_prev, f_next, remote, wn, sea_ref, couple_ref, sgain_ref, one_ref, two_ref,
        pick_ref, place_ref, out_ref, mk, oh, wb, st, pd, sh, cv, pk, rw, rn, halo_send, halo_recv, at_copies,
    )
    for copy in at_copies:
        copy.wait_recv()
    for q in range(4):
        atm_ref[pl.ds(q * quarter, quarter), :] = ao[q]

    @pl.when(t == 3)
    def _():
        for copy in low:
            copy.wait_send()

    @pl.when(t == 0)
    def _():
        for copy in high:
            copy.wait_send()

    for copy in y_copies + done + tok_out + [tok_near] + at_copies + fx_copies + to_core + far_sums + to_core2:
        copy.wait_send()


def body(
    tokens,
    ln_gain,
    w_up,
    w_down,
    w_flux_in,
    w_flux_out,
    ocean_state,
    land_mask,
    column_map,
    w_couple,
    dw_kernel,
    ocean_gain,
    w_pw1,
    w_pw2,
):
    xs, zs = XS, ZS
    rows, feat = tokens.shape
    d_model = 4 * feat
    shard, hidden = w_up.shape
    width = hidden // 4
    fh, flx = w_flux_out.shape
    quarter = rows // 4
    grid_rows, grid_cols, chans = ocean_state.shape
    cells = grid_rows * grid_cols
    pick, place = halo_matrices(grid_rows, grid_cols)
    dma = pltpu.SemaphoreType.DMA
    vm = pl.BlockSpec(memory_space=pltpu.VMEM)
    hb = pl.BlockSpec(memory_space=pl.ANY)
    return pl.pallas_call(
        functools.partial(atmosphere_kernel, xs, zs),
        out_shape=(
            jax.ShapeDtypeStruct((rows, feat), BF),
            jax.ShapeDtypeStruct(ocean_state.shape, BF),
        ),
        in_specs=[hb, vm, vm, vm, hb, hb, hb, vm, vm, hb, vm, vm, hb, hb, hb, hb],
        out_specs=(vm, vm),
        scratch_shapes=[
            pltpu.VMEM((2, shard, hidden), BF),
            pltpu.VMEM((2, 4, xs, zs, 2 * shard, width), BF),
            pltpu.VMEM((4, rows, feat), BF),
            pltpu.VMEM((rows, d_model), BF),
            pltpu.VMEM((2, rows, hidden // 2), BF),
            pltpu.VMEM((4, feat, fh), BF),
            pltpu.VMEM((3, 2, quarter, d_model // 2), BF),
            pltpu.VMEM((3, 2, quarter, d_model // 2), BF),
            pltpu.VMEM((2, quarter, d_model // 2), F32),
            pltpu.VMEM((4, quarter, feat), BF),
            pltpu.VMEM((4, quarter, feat), BF),
            pltpu.VMEM((6, quarter, flx), BF),
            dma((2,)), dma((2,)), dma((128,)), dma((128,)),
            dma((3,)), dma((3,)), dma((3,)), dma((3,)),
            dma((6,)), dma((6,)), dma((3,)), dma((3,)),
            dma((3,)), dma((3,)), dma((4,)), dma((2,)),
            pltpu.VMEM((cells, 128), F32),
            pltpu.VMEM((cells, 6 * quarter), BF),
            pltpu.VMEM((2, 7, 7, 8, chans), F32),
            pltpu.VMEM((2, cells, chans), BF),
            pltpu.VMEM((grid_rows + 6, grid_cols + 16, chans), F32),
            pltpu.VMEM((7, grid_rows + 6, grid_cols // 8, 8, chans), F32),
            pltpu.VMEM((grid_rows, grid_cols // 8, 8, chans), F32),
            pltpu.VMEM((2, 256, chans), BF),
            pltpu.VMEM((2, 256, chans), BF),
            pltpu.VMEM((2, 2, 3 * grid_cols, chans), BF),
            dma((16,)), dma((16,)),
            pltpu.VMEM(w_flux_out.shape, BF),
            pltpu.VMEM(ocean_state.shape, BF),
            pltpu.VMEM(w_couple.shape, BF),
            pltpu.VMEM(w_pw1.shape, BF),
            pltpu.VMEM(w_pw2.shape, BF),
            pltpu.VMEM(pick.shape, BF),
            pltpu.VMEM(place.shape, BF),
            dma((9,)),
            pltpu.VMEM((2, rows // 2, feat), BF),
            pltpu.VMEM((2, feat // 2, fh), BF),
            pltpu.VMEM((2, quarter, d_model // 2), BF),
            dma((12,)), dma((12,)),
        ],
        compiler_params=pltpu.CompilerParams(
            collective_id=0, has_side_effects=True, vmem_limit_bytes=60 * 1024 * 1024
        ),
        name="coupled_step",
    )(
        tokens, ln_gain, w_up, w_down.T, w_flux_in, w_flux_out,
        ocean_state, land_mask, column_map, w_couple, dw_kernel.transpose(1, 2, 0, 3), ocean_gain, w_pw1, w_pw2,
        pick, place,
    )


def solution(mesh):
    placed = (
        P("fsdp", "tile"),
        P(),
        P("fsdp", "tile"),
        P("tile", "fsdp"),
        P("tile", None),
        P(),
        P("fsdp", "tile", None),
        P("fsdp", "tile"),
        P("fsdp", "tile"),
        P(),
        P(),
        P(),
        P(),
        P(),
    )
    return jax.shard_map(
        body,
        mesh=mesh,
        in_specs=placed,
        out_specs=(P("fsdp", "tile"), P("fsdp", "tile", None)),
        check_vma=False,
    )
```

```python
import functools

import jax
import jax.numpy as jnp
from jax import lax
from jax.experimental import pallas as pl
from jax.experimental.pallas import tpu as pltpu
from jax.sharding import PartitionSpec as P
import numpy as np

MESH = pl.DeviceIdType.MESH
BF = jnp.bfloat16
F32 = jnp.float32
EPS = 1e-06
XS = 4
ZS = 8


def nt_dot(lhs, rhs):
    return lax.dot_general(lhs, rhs, (((1,), (1,)), ((), ())), preferred_element_type=F32)


def ocean_prepare(first, mask_ref, map_ref, taps_ref, mk, oh, wb):
    grid_rows, grid_cols = map_ref.shape
    tiles = oh.shape[1] // 128

    @pl.loop(0, grid_rows)
    def _(r):
        square = (grid_cols, grid_cols)
        eye = (
            lax.broadcasted_iota(jnp.int32, square, 0) == lax.broadcasted_iota(jnp.int32, square, 1)
        ).astype(F32)
        ones = jnp.ones((grid_cols, 128), BF)

        def upright(line):
            return jnp.dot((eye * line).astype(BF), ones, preferred_element_type=F32)

        index = map_ref[pl.ds(r, 1), :] - first
        high = upright((index >> 5).astype(F32))
        low = upright((index & 31).astype(F32))
        index_up = high * 32.0 + low
        span = pl.ds(pl.multiple_of(r * grid_cols, grid_cols), grid_cols)
        mk[span, :] = upright(mask_ref[pl.ds(r, 1), :].astype(F32))
        lane = lax.broadcasted_iota(jnp.int32, (grid_cols, 128), 1).astype(F32)
        for k in range(tiles):
            oh[span, k * 128 : (k + 1) * 128] = jnp.where(
                index_up == lane + 128.0 * k, 1.0, 0.0
            ).astype(BF)

    for k in range(taps_ref.shape[2]):
        for a in range(7):
            for b in range(7):
                wb[k, a, b] = jnp.broadcast_to(taps_ref[a, b, k : k + 1, :], wb.shape[3:])


def ocean(
    f, t, n_f, f_prev, f_next, remote, wn, sea_ref, couple_ref, sgain_ref, one_ref, two_ref,
    pick_ref, place_ref, out_ref, mk, oh, wb, st, pd, sh, cv, pk, rw, rn, halo_send, halo_recv, at_copies,
):
    grid_rows, grid_cols, chans = sea_ref.shape
    cells = 8 * grid_cols
    wide = pd.shape[1]
    t_next, t_prev = (t + 1) % 4, (t + 3) % 4
    edge = 3 * grid_cols

    def masked(span, values):
        return (jnp.concatenate([mk[span, :]] * (chans // 128), axis=1) * values).astype(BF)

    def keep(k, i, span, values):
        st[k, span, :] = values
        pd[pl.ds(3 + i * 8, 8), 8 : 8 + grid_cols, :] = values.astype(F32).reshape(
            8, grid_cols, chans
        )

    @pl.loop(0, grid_rows // 8)
    def _(i):
        span = pl.ds(pl.multiple_of(i * cells, cells), cells)
        picked = jnp.dot(
            oh[span, :], wn[...].reshape(oh.shape[1], wn.shape[2]), preferred_element_type=F32
        ).astype(BF)
        forcing = jnp.dot(picked, couple_ref[...], preferred_element_type=F32)
        before = sea_ref[pl.ds(i * 8, 8)].reshape(cells, chans).astype(F32)
        keep(0, i, span, masked(span, before + forcing))

    for k in range(2):
        last = grid_rows * grid_cols - edge
        moves = [
            (st.at[k, pl.ds(last, edge)], rn.at[k, 0], (f_next, t)),
            (st.at[k, pl.ds(0, edge)], rn.at[k, 1], (f_prev, t)),
            (pk.at[k, pl.ds(0, 96)], rw.at[k, pl.ds(0, 96)], (f, t_next)),
            (pk.at[k, pl.ds(96, 96)], rw.at[k, pl.ds(96, 96)], (f, t_prev)),
        ]
        corner = 192
        for fd in (f_prev, f_next):
            for td in (t_prev, t_next):
                part = pl.ds(corner, 16)
                moves.append((pk.at[k, part], rw.at[k, part], (fd, td)))
                corner += 16
        copies = [
            remote(src, dst, halo_send.at[k * 8 + j], halo_recv.at[k * 8 + j], device)
            for j, (src, dst, device) in enumerate(moves)
        ]
        for copy in copies[:2]:
            copy.start()
        pk[k] = jnp.dot(pick_ref[...], st[k], preferred_element_type=F32).astype(BF)
        for copy in copies[4:] + copies[2:4]:
            copy.start()
        for copy in copies:
            copy.wait_recv()
        if k == 0:
            for copy in at_copies:
                copy.start()
        above, below, left, right = f > 0, f < n_f - 1, t > 0, t < 3

        def valid(flag, values):
            return jnp.where(flag, values.astype(F32), 0.0)

        pd[0:3, 8 : 8 + grid_cols, :] = valid(above, rn[k, 0]).reshape(3, grid_cols, chans)
        pd[3 + grid_rows : 6 + grid_rows, 8 : 8 + grid_cols, :] = valid(below, rn[k, 1]).reshape(
            3, grid_cols, chans
        )
        flags = (
            left,
            right,
            jnp.logical_and(below, right),
            jnp.logical_and(below, left),
            jnp.logical_and(above, right),
            jnp.logical_and(above, left),
        )
        starts = (0, 96, 192, 208, 224, 240, 256)
        came = jnp.concatenate(
            [valid(flags[j], rw[k, starts[j] : starts[j + 1]]) for j in range(6)], axis=0
        ).astype(BF)
        strips = jnp.dot(place_ref[...], came, preferred_element_type=F32)
        count = (grid_rows + 6) * 8
        pd[:, 0:8, :] = strips[:count].reshape(grid_rows + 6, 8, chans)
        pd[:, wide - 8 : wide, :] = strips[count:].reshape(grid_rows + 6, 8, chans)

        @pl.loop(0, grid_rows + 6)
        def _(r):
            line = pd[r]
            for b in range(7):
                sh[b, r] = line[5 + b : 5 + b + grid_cols].reshape(grid_cols // 8, 8, chans)

        @pl.loop(0, (grid_rows // 4) * (chans // 128))
        def _(i):
            first = (i // (chans // 128)) * 4
            lanes = pl.ds(pl.multiple_of((i % (chans // 128)) * 128, 128), 128)
            totals = [jnp.zeros((grid_cols // 8, 8, 128), F32) for _ in range(4)]
            for b in range(7):
                weights = [wb[k, a, b, :, lanes] for a in range(7)]
                for r in range(10):
                    values = sh[b, first + r, :, :, lanes]
                    for j in range(4):
                        if 0 <= r - j < 7:
                            totals[j] = totals[j] + values * weights[r - j]
            for j in range(4):
                cv[first + j, :, :, lanes] = totals[j]

        @pl.loop(0, grid_rows // 8)
        def _(i):
            span = pl.ds(pl.multiple_of(i * cells, cells), cells)
            total = cv[pl.ds(i * 8, 8)].reshape(cells, chans)
            center = total - jnp.mean(total, axis=-1, keepdims=True)
            spread = jnp.mean(center * center, axis=-1, keepdims=True)
            pnorm = (center * lax.rsqrt(spread + EPS) * sgain_ref[k : k + 1, :]).astype(BF)
            inner = jax.nn.gelu(
                jnp.dot(pnorm, one_ref[k], preferred_element_type=F32), approximate=True
            ).astype(BF)
            lowered = jnp.dot(inner, two_ref[k], preferred_element_type=F32)
            values = masked(span, st[k, span, :].astype(F32) + lowered)
            if k == 0:
                keep(1, i, span, values)
            else:
                out_ref[pl.ds(i * 8, 8)] = values.reshape(8, grid_cols, chans)

        for copy in copies:
            copy.wait_send()


def halo_matrices(grid_rows, grid_cols):
    pick = np.zeros((256, grid_rows * grid_cols), np.float32)
    place = np.zeros((2 * (grid_rows + 6) * 8, 256), np.float32)
    side = (grid_rows + 6) * 8
    for r in range(grid_rows):
        for j in range(3):
            pick[r * 3 + j, r * grid_cols + grid_cols - 3 + j] = 1
            pick[96 + r * 3 + j, r * grid_cols + j] = 1
            place[(3 + r) * 8 + 5 + j, r * 3 + j] = 1
            place[side + (3 + r) * 8 + j, 96 + r * 3 + j] = 1
    corner = 192
    for down in (0, 1):
        for right in (0, 1):
            for i in range(3):
                for j in range(3):
                    row = grid_rows - 3 + i if down else i
                    col = grid_cols - 3 + j if right else j
                    pick[corner + i * 3 + j, row * grid_cols + col] = 1
                    to_row = i if down else grid_rows + 3 + i
                    to = to_row * 8 + 5 + j if right else side + to_row * 8 + j
                    place[to, corner + i * 3 + j] = 1
            corner += 16
    return jnp.asarray(pick, BF), jnp.asarray(place, BF)


def atmosphere_kernel(
    xs, zs,
    tok_ref, gain_ref, up_ref, down_ref, wfi_ref, wfo_hbm,
    sea_hbm, mask_ref, map_ref, couple_hbm, taps_ref, sgain_ref, one_hbm, two_hbm, pick_hbm, place_hbm,
    atm_ref, out_ref,
    yb, gw, tk, nm, hd, fi, sb, rb, acc, at, ao, wn,
    y_send, y_recv, ring_send, ring_recv, tok_send, tok_recv, fi_send, fi_recv,
    rs_send, rs_recv, at_send, at_recv, fx_send, fx_recv, rim_send, rim_recv,
    mk, oh, wb, st, pd, sh, cv, pk, rw, rn, halo_send, halo_recv,
    wfo_ref, sea_ref, couple_ref, one_ref, two_ref, pick_ref, place_ref, load_sem,
    tok_hop, fi_hop, rs_hop, hop_send, hop_recv,
):
    f = lax.axis_index("fsdp")
    t = lax.axis_index("tile")
    n_f = 2 * xs * zs
    x, z, yl = f // (2 * zs), (f // 2) % zs, f % 2
    yh, c = t // 2, t % 2
    yp = f + 1 - 2 * yl
    x_right = (f + 2 * zs) % n_f
    x_left = (f - 2 * zs + n_f) % n_f
    z_right = x * 2 * zs + ((z + 1) % zs) * 2 + yl
    z_left = x * 2 * zs + ((z + zs - 1) % zs) * 2 + yl
    f_next, f_prev = (f + 1) % n_f, (f + n_f - 1) % n_f
    t_core = yh * 2 + (1 - c)
    t_far = (1 - yh) * 2 + c
    t_diag = (1 - yh) * 2 + (1 - c)
    rows = tok_ref.shape[0]
    quarter = rows // 4
    feat = tok_ref.shape[1]
    width = gw.shape[-1]
    d_model = 4 * feat

    barrier = pltpu.get_barrier_semaphore()
    for other in (x_right, x_left, z_right, z_left):
        pl.semaphore_signal(barrier, inc=1, device_id=(other, t), device_id_type=MESH)
    for other in (t_core, t_far, t_diag):
        pl.semaphore_signal(barrier, inc=1, device_id=(f, other), device_id_type=MESH)
    for other in (f_prev, f_next):
        for q in range(4):
            pl.semaphore_signal(barrier, inc=1, device_id=(other, q), device_id_type=MESH)
    tok_load = pltpu.make_async_copy(tok_ref, tk.at[t], load_sem.at[0])
    fi_load = pltpu.make_async_copy(wfi_ref, fi.at[t], load_sem.at[1])
    loads = [
        pltpu.make_async_copy(src, dst, load_sem.at[2 + j])
        for j, (src, dst) in enumerate((
            (wfo_hbm, wfo_ref), (sea_hbm, sea_ref), (couple_hbm, couple_ref), (one_hbm, one_ref),
            (two_hbm, two_ref), (pick_hbm, pick_ref), (place_hbm, place_ref),
        ))
    ]
    tok_load.start()
    pl.semaphore_wait(barrier, 15)

    def remote(src, dst, send, recv, device):
        return pltpu.make_async_remote_copy(
            src_ref=src, dst_ref=dst, send_sem=send, recv_sem=recv,
            device_id=device, device_id_type=MESH,
        )

    y_copies = [
        remote(ref, yb.at[w], y_send.at[w], y_recv.at[w], (yp, t))
        for w, ref in enumerate((up_ref, down_ref))
    ]
    for copy in y_copies:
        copy.start()
    y_at = yh * 2 + yl
    y_ways = []
    for way in (1, 3):
        y_to = (y_at + way) % 4
        y_ways.append((f - yl + y_to % 2, (y_to // 2) * 2 + c))

    def far_out(src, hop, sem):
        return [
            remote(src[h], hop.at[h], hop_send.at[sem + h], hop_recv.at[sem + h], y_ways[h])
            for h in (0, 1)
        ]

    def far_on(hop, dst, sem):
        copies = []
        for h in (0, 1):
            origin = (1 - y_ways[h][1] // 2) * 2 + c
            copies.append(
                remote(
                    hop.at[h], dst(origin, h), hop_send.at[sem + 2 + h], hop_recv.at[sem + 2 + h],
                    y_ways[h],
                )
            )
        return copies

    half_rows, half_feat = rows // 2, feat // 2
    tok_parts = [pl.ds(h * half_rows, half_rows) for h in (0, 1)]
    fi_parts = [pl.ds(h * half_feat, half_feat) for h in (0, 1)]
    tok_out = far_out([tok_ref.at[part] for part in tok_parts], tok_hop, 0)
    tok_on = far_on(tok_hop, lambda q, h: tk.at[q, tok_parts[h]], 0)
    fi_out = far_out([wfi_ref.at[part] for part in fi_parts], fi_hop, 4)
    fi_on = far_on(fi_hop, lambda q, h: fi.at[q, fi_parts[h]], 4)
    tok_near = remote(tok_ref, tk.at[t], tok_send.at[0], tok_recv.at[0], (f, t_core))
    fi_near = remote(wfi_ref, fi.at[t], fi_send.at[0], fi_recv.at[0], (f, t_core))
    tok_relay = remote(tk.at[t_far], tk.at[t_far], tok_send.at[1], tok_recv.at[1], (f, t_core))
    fi_relay = remote(fi.at[t_far], fi.at[t_far], fi_send.at[1], fi_recv.at[1], (f, t_core))

    def ring_round(w, stream, stage, s):
        on_x = (stream == 0) == (stage == 0)
        n = xs if on_x else zs
        here = x if on_x else z
        last = s == n // 2 - 1
        copies = [[], []]
        for k in (0, 1):
            piece = 2 * stream + k
            for way in (0, 1):
                if last and way != k:
                    continue
                chunk = (here - s + n) % n if way == 0 else (here + s) % n
                if stage == 0:
                    part = gw.at[w, piece, chunk, z] if on_x else gw.at[w, piece, x, chunk]
                else:
                    part = gw.at[w, piece, chunk] if on_x else gw.at[w, piece, :, chunk]
                if on_x:
                    target = x_right if way == 0 else x_left
                else:
                    target = z_right if way == 0 else z_left
                at_sem = ((((w * 2 + stream) * 2 + stage) * 4 + s) * 2 + way) * 2 + k
                copies[k].append(
                    remote(part, part, ring_send.at[at_sem], ring_recv.at[at_sem], (target, t))
                )
        return copies

    done = []

    def start(copies):
        for copy in copies:
            copy.start()
        done.extend(copies)
        return copies

    def arrive(copies):
        for copy in copies:
            copy.wait_recv()

    def begin(w, stream):
        new = ring_round(w, stream, 0, 0)
        start(new[0] + new[1])
        return new

    def advance(old, w, stream, stage, s):
        new = ring_round(w, stream, stage, s)
        for k in (0, 1):
            arrive(old[k])
            start(new[k])
        return new

    def assemble(w, ref):
        y_copies[w].wait_recv()
        for p in range(4):
            mine = ref[:, p * width : (p + 1) * width].astype(F32)
            other = yb[w, :, p * width : (p + 1) * width].astype(F32)
            first = jnp.where(yl == 0, mine, other)
            second = jnp.where(yl == 0, other, mine)
            gw[w, p, x, z] = jnp.concatenate([first, second], axis=0).astype(BF)

    for copy in tok_out:
        copy.start()
    tok_near.start()
    for copy in loads:
        copy.start()
    fi_load.start()
    assemble(0, up_ref)
    up_b = begin(0, 1)
    up_a = begin(0, 0)
    assemble(1, down_ref)
    down_b = begin(1, 1)
    down_a = begin(1, 0)
    up_a = advance(up_a, 0, 0, 0, 1)
    up_b = advance(up_b, 0, 1, 0, 1)
    down_b = advance(down_b, 1, 1, 0, 1)
    down_a = advance(down_a, 1, 0, 0, 1)
    up_b = advance(up_b, 0, 1, 0, 2)
    down_b = advance(down_b, 1, 1, 0, 2)
    up_b = advance(up_b, 0, 1, 0, 3)
    up_a = advance(up_a, 0, 0, 1, 0)
    down_b = advance(down_b, 1, 1, 0, 3)
    up_b = advance(up_b, 0, 1, 1, 0)
    arrive(tok_out)
    start(tok_on)
    down_a = advance(down_a, 1, 0, 1, 0)
    down_b = advance(down_b, 1, 1, 1, 0)
    up_a = advance(up_a, 0, 0, 1, 1)
    arrive(tok_on)
    start([tok_relay])
    start(fi_out)
    start([fi_near])
    down_a = advance(down_a, 1, 0, 1, 1)
    tok_load.wait()
    tok_near.wait_recv()
    tok_relay.wait_recv()
    step = min(32, quarter)

    @pl.loop(0, rows // step)
    def _(i):
        span = pl.ds(pl.multiple_of(i * step, step), step)
        values = [tk[q, span, :].astype(F32) for q in range(4)]
        mean = sum(jnp.sum(v, axis=-1, keepdims=True) for v in values) / d_model
        centers = [v - mean for v in values]
        spread = sum(jnp.sum(v * v, axis=-1, keepdims=True) for v in centers) / d_model
        inverse = lax.rsqrt(spread + EPS)
        for q in range(4):
            gain = gain_ref[q * feat : (q + 1) * feat][None, :]
            nm[span, q * feat : (q + 1) * feat] = (centers[q] * inverse * gain).astype(BF)

    up_b = advance(up_b, 0, 1, 1, 1)
    up_a = advance(up_a, 0, 0, 1, 2)
    down_b = advance(down_b, 1, 1, 1, 1)
    down_a = advance(down_a, 1, 0, 1, 2)
    ocean_prepare(f * rows - quarter, mask_ref, map_ref, taps_ref, mk, oh, wb)
    up_a = advance(up_a, 0, 0, 1, 3)
    down_a = advance(down_a, 1, 0, 1, 3)
    arrive(fi_out)
    start(fi_on)
    arrive(up_b[0] + up_b[1])
    arrive(up_a[0] + up_a[1])

    def up_block(half, block):
        span = pl.ds(pl.multiple_of(block * quarter, quarter), quarter)
        rhs = jnp.concatenate(
            [gw[0, half * 2 + k].reshape(d_model, width) for k in (0, 1)], axis=1
        )
        pre = jnp.dot(nm[span, :], rhs, preferred_element_type=F32)
        hd[half, span, :] = jax.nn.gelu(pre, approximate=True).astype(BF)

    for half in (0, 1):
        @pl.loop(0, 4)
        def _(block):
            up_block(half, block)

        if half == 0:
            arrive(fi_on)
            start([fi_relay])
    arrive(down_b[0] + down_b[1])
    arrive(down_a[0] + down_a[1])

    def partial(block, half):
        span = pl.ds(pl.multiple_of(block * quarter, quarter), quarter)
        lhs = jnp.concatenate([hd[0, span, :], hd[1, span, :]], axis=1)
        part = pl.ds(half * (xs // 2), xs // 2)
        rhs = jnp.concatenate(
            [gw[1, p, part].reshape(d_model // 2, width) for p in range(4)], axis=1
        )
        return nt_dot(lhs, rhs)

    def sums(k, half, target):
        return remote(
            sb.at[k, half], rb.at[k, half], rs_send.at[2 * k + half], rs_recv.at[2 * k + half],
            (f, target),
        )

    to_core = [sums(0, half, t_core) for half in (0, 1)]
    strip = quarter // 2
    strips = [pl.ds(h * strip, strip) for h in (0, 1)]
    far_sums = [
        far_out([sb.at[1, half, part] for part in strips], rs_hop.at[half], 8 + 4 * half)
        for half in (0, 1)
    ]
    far_sums_on = [
        far_on(
            rs_hop.at[half], lambda q, h, half=half: rb.at[1, half, strips[h]], 8 + 4 * half
        )
        for half in (0, 1)
    ]
    to_core2 = [sums(2, half, t_core) for half in (0, 1)]

    for half in (0, 1):
        sb[0, half] = partial(t_diag, half).astype(BF)
        to_core[half].start()
        acc[half] = partial(t_far, half)
        to_core[half].wait_recv()
        sb[1, half] = (acc[half] + rb[0, half].astype(F32)).astype(BF)
        start(far_sums[half])
    for half in (0, 1):
        sb[2, half] = partial(t_core, half).astype(BF)
        to_core2[half].start()
    for half in (0, 1):
        acc[half] = partial(t, half)
    for half in (0, 1):
        arrive(far_sums[half])
        start(far_sums_on[half])
    mine = pl.ds(pl.multiple_of(t * quarter, quarter), quarter)
    for half in (0, 1):
        to_core2[half].wait_recv()
        arrive(far_sums_on[half])
        for k in (0, 1):
            q = 2 * half + k
            cols = slice(k * feat, (k + 1) * feat)
            delta = acc[half, :, cols] + rb[2, half, :, cols].astype(F32) + rb[1, half, :, cols].astype(F32)
            at[q] = (tk[q, mine, :].astype(F32) + delta).astype(BF)

    at_copies = []
    for k in range(1, 4):
        q = (t + k) % 4
        at_copies.append(remote(at.at[q], ao.at[t], at_send.at[k - 1], at_recv.at[k - 1], (f, q)))
    ao[t] = at[t]

    fi_load.wait()
    fi_near.wait_recv()
    fi_relay.wait_recv()
    for copy in loads:
        copy.wait()
    pre = jnp.dot(
        jnp.concatenate([at[q] for q in range(4)], axis=1),
        fi[...].reshape(d_model, fi.shape[-1]),
        preferred_element_type=F32,
    )
    flux_hidden = jax.nn.gelu(pre, approximate=True).astype(BF)
    wn[1 + t] = jnp.dot(flux_hidden, wfo_ref[...], preferred_element_type=F32).astype(BF)
    fx_copies = []
    for k in range(1, 4):
        fx_copies.append(
            remote(wn.at[1 + t], wn.at[1 + t], fx_send.at[k - 1], fx_recv.at[k - 1], (f, (t + k) % 4))
        )
        fx_copies[-1].start()

    def rim(slot, source, target):
        return [
            remote(wn.at[source], wn.at[slot], rim_send.at[q], rim_recv.at[slot // 5], (target, q))
            for q in range(4)
        ]

    low = rim(0, 4, f_next)
    high = rim(5, 1, f_prev)

    @pl.when(t == 3)
    def _():
        for copy in low:
            copy.start()

    @pl.when(t == 0)
    def _():
        for copy in high:
            copy.start()

    for copy in fx_copies:
        copy.wait_recv()
    low[0].wait_recv()
    high[0].wait_recv()
    ocean(
        f, t, n_f, f_prev, f_next, remote, wn, sea_ref, couple_ref, sgain_ref, one_ref, two_ref,
        pick_ref, place_ref, out_ref, mk, oh, wb, st, pd, sh, cv, pk, rw, rn, halo_send, halo_recv, at_copies,
    )
    for copy in at_copies:
        copy.wait_recv()
    for q in range(4):
        atm_ref[pl.ds(q * quarter, quarter), :] = ao[q]

    @pl.when(t == 3)
    def _():
        for copy in low:
            copy.wait_send()

    @pl.when(t == 0)
    def _():
        for copy in high:
            copy.wait_send()

    for copy in y_copies + done + tok_out + [tok_near] + at_copies + fx_copies + to_core + to_core2:
        copy.wait_send()


def body(
    tokens,
    ln_gain,
    w_up,
    w_down,
    w_flux_in,
    w_flux_out,
    ocean_state,
    land_mask,
    column_map,
    w_couple,
    dw_kernel,
    ocean_gain,
    w_pw1,
    w_pw2,
):
    xs, zs = XS, ZS
    rows, feat = tokens.shape
    d_model = 4 * feat
    shard, hidden = w_up.shape
    width = hidden // 4
    fh, flx = w_flux_out.shape
    quarter = rows // 4
    grid_rows, grid_cols, chans = ocean_state.shape
    cells = grid_rows * grid_cols
    pick, place = halo_matrices(grid_rows, grid_cols)
    dma = pltpu.SemaphoreType.DMA
    vm = pl.BlockSpec(memory_space=pltpu.VMEM)
    hb = pl.BlockSpec(memory_space=pl.ANY)
    return pl.pallas_call(
        functools.partial(atmosphere_kernel, xs, zs),
        out_shape=(
            jax.ShapeDtypeStruct((rows, feat), BF),
            jax.ShapeDtypeStruct(ocean_state.shape, BF),
        ),
        in_specs=[hb, vm, vm, vm, hb, hb, hb, vm, vm, hb, vm, vm, hb, hb, hb, hb],
        out_specs=(vm, vm),
        scratch_shapes=[
            pltpu.VMEM((2, shard, hidden), BF),
            pltpu.VMEM((2, 4, xs, zs, 2 * shard, width), BF),
            pltpu.VMEM((4, rows, feat), BF),
            pltpu.VMEM((rows, d_model), BF),
            pltpu.VMEM((2, rows, hidden // 2), BF),
            pltpu.VMEM((4, feat, fh), BF),
            pltpu.VMEM((3, 2, quarter, d_model // 2), BF),
            pltpu.VMEM((3, 2, quarter, d_model // 2), BF),
            pltpu.VMEM((2, quarter, d_model // 2), F32),
            pltpu.VMEM((4, quarter, feat), BF),
            pltpu.VMEM((4, quarter, feat), BF),
            pltpu.VMEM((6, quarter, flx), BF),
            dma((2,)), dma((2,)), dma((128,)), dma((128,)),
            dma((3,)), dma((3,)), dma((3,)), dma((3,)),
            dma((6,)), dma((6,)), dma((3,)), dma((3,)),
            dma((3,)), dma((3,)), dma((4,)), dma((2,)),
            pltpu.VMEM((cells, 128), F32),
            pltpu.VMEM((cells, 6 * quarter), BF),
            pltpu.VMEM((2, 7, 7, 8, chans), F32),
            pltpu.VMEM((2, cells, chans), BF),
            pltpu.VMEM((grid_rows + 6, grid_cols + 16, chans), F32),
            pltpu.VMEM((7, grid_rows + 6, grid_cols // 8, 8, chans), F32),
            pltpu.VMEM((grid_rows, grid_cols // 8, 8, chans), F32),
            pltpu.VMEM((2, 256, chans), BF),
            pltpu.VMEM((2, 256, chans), BF),
            pltpu.VMEM((2, 2, 3 * grid_cols, chans), BF),
            dma((16,)), dma((16,)),
            pltpu.VMEM(w_flux_out.shape, BF),
            pltpu.VMEM(ocean_state.shape, BF),
            pltpu.VMEM(w_couple.shape, BF),
            pltpu.VMEM(w_pw1.shape, BF),
            pltpu.VMEM(w_pw2.shape, BF),
            pltpu.VMEM(pick.shape, BF),
            pltpu.VMEM(place.shape, BF),
            dma((9,)),
            pltpu.VMEM((2, rows // 2, feat), BF),
            pltpu.VMEM((2, feat // 2, fh), BF),
            pltpu.VMEM((2, 2, quarter // 2, d_model // 2), BF),
            dma((16,)), dma((16,)),
        ],
        compiler_params=pltpu.CompilerParams(
            collective_id=0, has_side_effects=True, vmem_limit_bytes=60 * 1024 * 1024
        ),
        name="coupled_step",
    )(
        tokens, ln_gain, w_up, w_down.T, w_flux_in, w_flux_out,
        ocean_state, land_mask, column_map, w_couple, dw_kernel.transpose(1, 2, 0, 3), ocean_gain, w_pw1, w_pw2,
        pick, place,
    )


def solution(mesh):
    placed = (
        P("fsdp", "tile"),
        P(),
        P("fsdp", "tile"),
        P("tile", "fsdp"),
        P("tile", None),
        P(),
        P("fsdp", "tile", None),
        P("fsdp", "tile"),
        P("fsdp", "tile"),
        P(),
        P(),
        P(),
        P(),
        P(),
    )
    return jax.shard_map(
        body,
        mesh=mesh,
        in_specs=placed,
        out_specs=(P("fsdp", "tile"), P("fsdp", "tile", None)),
        check_vma=False,
    )
```

```python
import functools

import jax
import jax.numpy as jnp
from jax import lax
from jax.experimental import pallas as pl
from jax.experimental.pallas import tpu as pltpu
from jax.sharding import PartitionSpec as P
import numpy as np

MESH = pl.DeviceIdType.MESH
BF = jnp.bfloat16
F32 = jnp.float32
EPS = 1e-06
XS = 4
ZS = 8


def nt_dot(lhs, rhs):
    return lax.dot_general(lhs, rhs, (((1,), (1,)), ((), ())), preferred_element_type=F32)


def ocean_prepare(first, mask_ref, map_ref, taps_ref, mk, oh, wb):
    grid_rows, grid_cols = map_ref.shape
    tiles = oh.shape[1] // 128

    @pl.loop(0, grid_rows)
    def _(r):
        square = (grid_cols, grid_cols)
        eye = (
            lax.broadcasted_iota(jnp.int32, square, 0) == lax.broadcasted_iota(jnp.int32, square, 1)
        ).astype(F32)
        ones = jnp.ones((grid_cols, 128), BF)

        def upright(line):
            return jnp.dot((eye * line).astype(BF), ones, preferred_element_type=F32)

        index = map_ref[pl.ds(r, 1), :] - first
        high = upright((index >> 5).astype(F32))
        low = upright((index & 31).astype(F32))
        index_up = high * 32.0 + low
        span = pl.ds(pl.multiple_of(r * grid_cols, grid_cols), grid_cols)
        mk[span, :] = upright(mask_ref[pl.ds(r, 1), :].astype(F32))
        lane = lax.broadcasted_iota(jnp.int32, (grid_cols, 128), 1).astype(F32)
        for k in range(tiles):
            oh[span, k * 128 : (k + 1) * 128] = jnp.where(
                index_up == lane + 128.0 * k, 1.0, 0.0
            ).astype(BF)

    for k in range(taps_ref.shape[2]):
        for a in range(7):
            for b in range(7):
                wb[k, a, b] = jnp.broadcast_to(taps_ref[a, b, k : k + 1, :], wb.shape[3:])


def ocean(
    f, t, n_f, f_prev, f_next, remote, wn, sea_ref, couple_ref, sgain_ref, one_ref, two_ref,
    pick_ref, place_ref, out_ref, mk, oh, wb, st, pd, sh, cv, pk, rw, rn, halo_send, halo_recv, at_copies,
):
    grid_rows, grid_cols, chans = sea_ref.shape
    cells = 8 * grid_cols
    wide = pd.shape[1]
    t_next, t_prev = (t + 1) % 4, (t + 3) % 4
    edge = 3 * grid_cols

    def masked(span, values):
        return (jnp.concatenate([mk[span, :]] * (chans // 128), axis=1) * values).astype(BF)

    def keep(k, i, span, values):
        st[k, span, :] = values
        pd[pl.ds(3 + i * 8, 8), 8 : 8 + grid_cols, :] = values.astype(F32).reshape(
            8, grid_cols, chans
        )

    @pl.loop(0, grid_rows // 8)
    def _(i):
        span = pl.ds(pl.multiple_of(i * cells, cells), cells)
        picked = jnp.dot(
            oh[span, :], wn[...].reshape(oh.shape[1], wn.shape[2]), preferred_element_type=F32
        ).astype(BF)
        forcing = jnp.dot(picked, couple_ref[...], preferred_element_type=F32)
        before = sea_ref[pl.ds(i * 8, 8)].reshape(cells, chans).astype(F32)
        keep(0, i, span, masked(span, before + forcing))

    halves = chans // 128

    def correlate(k, quad, half, spans):
        first = quad * 4
        lanes = pl.ds(pl.multiple_of(half * 128, 128), 128)
        totals = [[jnp.zeros((hi - lo, 8, 128), F32) for lo, hi in spans] for _ in range(4)]
        for b in range(7):
            weights = [wb[k, a, b, :, lanes] for a in range(7)]
            for r in range(10):
                for n, (lo, hi) in enumerate(spans):
                    values = sh[b, first + r, lo:hi, :, lanes]
                    for j in range(4):
                        if 0 <= r - j < 7:
                            totals[j][n] = totals[j][n] + values * weights[r - j]
        for j in range(4):
            for n, (lo, hi) in enumerate(spans):
                cv[first + j, lo:hi, :, lanes] = totals[j][n]

    for k in range(2):
        last = grid_rows * grid_cols - edge
        moves = [
            (st.at[k, pl.ds(last, edge)], rn.at[k, 0], (f_next, t)),
            (st.at[k, pl.ds(0, edge)], rn.at[k, 1], (f_prev, t)),
            (pk.at[k, pl.ds(0, 96)], rw.at[k, pl.ds(0, 96)], (f, t_next)),
            (pk.at[k, pl.ds(96, 96)], rw.at[k, pl.ds(96, 96)], (f, t_prev)),
        ]
        corner = 192
        for fd in (f_prev, f_next):
            for td in (t_prev, t_next):
                part = pl.ds(corner, 16)
                moves.append((pk.at[k, part], rw.at[k, part], (fd, td)))
                corner += 16
        copies = [
            remote(src, dst, halo_send.at[k * 8 + j], halo_recv.at[k * 8 + j], device)
            for j, (src, dst, device) in enumerate(moves)
        ]
        for copy in copies[:2]:
            copy.start()
        pk[k] = jnp.dot(pick_ref[...], st[k], preferred_element_type=F32).astype(BF)
        for copy in copies[4:] + copies[2:4]:
            copy.start()

        @pl.loop(3, grid_rows + 3)
        def _(r):
            line = pd[r, 8 : 8 + grid_cols, :]
            for b in range(7):
                sh[b, r, 1 : grid_cols // 8 - 1] = line[5 + b : 5 + b + grid_cols - 16].reshape(
                    grid_cols // 8 - 2, 8, chans
                )

        @pl.loop(0, (grid_rows // 4 - 2) * halves)
        def _(i):
            correlate(k, 1 + i // halves, i % halves, ((1, grid_cols // 8 - 1),))

        for copy in copies:
            copy.wait_recv()
        if k == 0:
            for copy in at_copies:
                copy.start()
        above, below, left, right = f > 0, f < n_f - 1, t > 0, t < 3

        def valid(flag, values):
            return jnp.where(flag, values.astype(F32), 0.0)

        pd[0:3, 8 : 8 + grid_cols, :] = valid(above, rn[k, 0]).reshape(3, grid_cols, chans)
        pd[3 + grid_rows : 6 + grid_rows, 8 : 8 + grid_cols, :] = valid(below, rn[k, 1]).reshape(
            3, grid_cols, chans
        )
        flags = (
            left,
            right,
            jnp.logical_and(below, right),
            jnp.logical_and(below, left),
            jnp.logical_and(above, right),
            jnp.logical_and(above, left),
        )
        starts = (0, 96, 192, 208, 224, 240, 256)
        came = jnp.concatenate(
            [valid(flags[j], rw[k, starts[j] : starts[j + 1]]) for j in range(6)], axis=0
        ).astype(BF)
        strips = jnp.dot(place_ref[...], came, preferred_element_type=F32)
        count = (grid_rows + 6) * 8
        pd[:, 0:8, :] = strips[:count].reshape(grid_rows + 6, 8, chans)
        pd[:, wide - 8 : wide, :] = strips[count:].reshape(grid_rows + 6, 8, chans)

        @pl.loop(0, grid_rows + 6)
        def _(r):
            line = pd[r]
            for b in range(7):
                sh[b, r] = line[5 + b : 5 + b + grid_cols].reshape(grid_cols // 8, 8, chans)

        last_quad = grid_rows // 4 - 1
        tiles = grid_cols // 8

        @pl.loop(0, halves)
        def _(i):
            correlate(k, 0, i, ((0, tiles),))
            correlate(k, last_quad, i, ((0, tiles),))

        @pl.loop(0, (last_quad - 1) * halves)
        def _(i):
            correlate(k, 1 + i // halves, i % halves, ((0, 1), (tiles - 1, tiles)))

        @pl.loop(0, grid_rows // 8)
        def _(i):
            span = pl.ds(pl.multiple_of(i * cells, cells), cells)
            total = cv[pl.ds(i * 8, 8)].reshape(cells, chans)
            center = total - jnp.mean(total, axis=-1, keepdims=True)
            spread = jnp.mean(center * center, axis=-1, keepdims=True)
            pnorm = (center * lax.rsqrt(spread + EPS) * sgain_ref[k : k + 1, :]).astype(BF)
            inner = jax.nn.gelu(
                jnp.dot(pnorm, one_ref[k], preferred_element_type=F32), approximate=True
            ).astype(BF)
            lowered = jnp.dot(inner, two_ref[k], preferred_element_type=F32)
            values = masked(span, st[k, span, :].astype(F32) + lowered)
            if k == 0:
                keep(1, i, span, values)
            else:
                out_ref[pl.ds(i * 8, 8)] = values.reshape(8, grid_cols, chans)

        for copy in copies:
            copy.wait_send()


def halo_matrices(grid_rows, grid_cols):
    pick = np.zeros((256, grid_rows * grid_cols), np.float32)
    place = np.zeros((2 * (grid_rows + 6) * 8, 256), np.float32)
    side = (grid_rows + 6) * 8
    for r in range(grid_rows):
        for j in range(3):
            pick[r * 3 + j, r * grid_cols + grid_cols - 3 + j] = 1
            pick[96 + r * 3 + j, r * grid_cols + j] = 1
            place[(3 + r) * 8 + 5 + j, r * 3 + j] = 1
            place[side + (3 + r) * 8 + j, 96 + r * 3 + j] = 1
    corner = 192
    for down in (0, 1):
        for right in (0, 1):
            for i in range(3):
                for j in range(3):
                    row = grid_rows - 3 + i if down else i
                    col = grid_cols - 3 + j if right else j
                    pick[corner + i * 3 + j, row * grid_cols + col] = 1
                    to_row = i if down else grid_rows + 3 + i
                    to = to_row * 8 + 5 + j if right else side + to_row * 8 + j
                    place[to, corner + i * 3 + j] = 1
            corner += 16
    return jnp.asarray(pick, BF), jnp.asarray(place, BF)


def atmosphere_kernel(
    xs, zs,
    tok_ref, gain_ref, up_ref, down_ref, wfi_ref, wfo_hbm,
    sea_hbm, mask_ref, map_ref, couple_hbm, taps_ref, sgain_ref, one_hbm, two_hbm, pick_hbm, place_hbm,
    atm_ref, out_ref,
    yb, gw, tk, nm, hd, fi, sb, rb, acc, at, ao, wn,
    y_send, y_recv, ring_send, ring_recv, tok_send, tok_recv, fi_send, fi_recv,
    rs_send, rs_recv, at_send, at_recv, fx_send, fx_recv, rim_send, rim_recv,
    mk, oh, wb, st, pd, sh, cv, pk, rw, rn, halo_send, halo_recv,
    wfo_ref, sea_ref, couple_ref, one_ref, two_ref, pick_ref, place_ref, load_sem,
    tok_hop, fi_hop, rs_hop, hop_send, hop_recv,
):
    f = lax.axis_index("fsdp")
    t = lax.axis_index("tile")
    n_f = 2 * xs * zs
    x, z, yl = f // (2 * zs), (f // 2) % zs, f % 2
    yh, c = t // 2, t % 2
    yp = f + 1 - 2 * yl
    x_right = (f + 2 * zs) % n_f
    x_left = (f - 2 * zs + n_f) % n_f
    z_right = x * 2 * zs + ((z + 1) % zs) * 2 + yl
    z_left = x * 2 * zs + ((z + zs - 1) % zs) * 2 + yl
    f_next, f_prev = (f + 1) % n_f, (f + n_f - 1) % n_f
    t_core = yh * 2 + (1 - c)
    t_far = (1 - yh) * 2 + c
    t_diag = (1 - yh) * 2 + (1 - c)
    rows = tok_ref.shape[0]
    quarter = rows // 4
    feat = tok_ref.shape[1]
    width = gw.shape[-1]
    d_model = 4 * feat

    barrier = pltpu.get_barrier_semaphore()
    for other in (x_right, x_left, z_right, z_left):
        pl.semaphore_signal(barrier, inc=1, device_id=(other, t), device_id_type=MESH)
    for other in (t_core, t_far, t_diag):
        pl.semaphore_signal(barrier, inc=1, device_id=(f, other), device_id_type=MESH)
    for other in (f_prev, f_next):
        for q in range(4):
            pl.semaphore_signal(barrier, inc=1, device_id=(other, q), device_id_type=MESH)
    tok_load = pltpu.make_async_copy(tok_ref, tk.at[t], load_sem.at[0])
    fi_load = pltpu.make_async_copy(wfi_ref, fi.at[t], load_sem.at[1])
    loads = [
        pltpu.make_async_copy(src, dst, load_sem.at[2 + j])
        for j, (src, dst) in enumerate((
            (wfo_hbm, wfo_ref), (sea_hbm, sea_ref), (couple_hbm, couple_ref), (one_hbm, one_ref),
            (two_hbm, two_ref), (pick_hbm, pick_ref), (place_hbm, place_ref),
        ))
    ]
    tok_load.start()
    pl.semaphore_wait(barrier, 15)

    def remote(src, dst, send, recv, device):
        return pltpu.make_async_remote_copy(
            src_ref=src, dst_ref=dst, send_sem=send, recv_sem=recv,
            device_id=device, device_id_type=MESH,
        )

    y_copies = [
        remote(ref, yb.at[w], y_send.at[w], y_recv.at[w], (yp, t))
        for w, ref in enumerate((up_ref, down_ref))
    ]
    for copy in y_copies:
        copy.start()
    y_at = yh * 2 + yl
    y_ways = []
    for way in (1, 3):
        y_to = (y_at + way) % 4
        y_ways.append((f - yl + y_to % 2, (y_to // 2) * 2 + c))

    def far_out(src, hop, sem):
        return [
            remote(src[h], hop.at[h], hop_send.at[sem + h], hop_recv.at[sem + h], y_ways[h])
            for h in (0, 1)
        ]

    def far_on(hop, dst, sem):
        copies = []
        for h in (0, 1):
            origin = (1 - y_ways[h][1] // 2) * 2 + c
            copies.append(
                remote(
                    hop.at[h], dst(origin, h), hop_send.at[sem + 2 + h], hop_recv.at[sem + 2 + h],
                    y_ways[h],
                )
            )
        return copies

    half_rows, half_feat = rows // 2, feat // 2
    tok_parts = [pl.ds(h * half_rows, half_rows) for h in (0, 1)]
    fi_parts = [pl.ds(h * half_feat, half_feat) for h in (0, 1)]
    tok_out = far_out([tok_ref.at[part] for part in tok_parts], tok_hop, 0)
    tok_on = far_on(tok_hop, lambda q, h: tk.at[q, tok_parts[h]], 0)
    fi_out = far_out([wfi_ref.at[part] for part in fi_parts], fi_hop, 4)
    fi_on = far_on(fi_hop, lambda q, h: fi.at[q, fi_parts[h]], 4)
    tok_near = remote(tok_ref, tk.at[t], tok_send.at[0], tok_recv.at[0], (f, t_core))
    fi_near = remote(wfi_ref, fi.at[t], fi_send.at[0], fi_recv.at[0], (f, t_core))
    tok_relay = remote(tk.at[t_far], tk.at[t_far], tok_send.at[1], tok_recv.at[1], (f, t_core))
    fi_relay = remote(fi.at[t_far], fi.at[t_far], fi_send.at[1], fi_recv.at[1], (f, t_core))

    def ring_round(w, stream, stage, s):
        on_x = (stream == 0) == (stage == 0)
        n = xs if on_x else zs
        here = x if on_x else z
        last = s == n // 2 - 1
        copies = [[], []]
        for k in (0, 1):
            piece = 2 * stream + k
            for way in (0, 1):
                if last and way != k:
                    continue
                chunk = (here - s + n) % n if way == 0 else (here + s) % n
                if stage == 0:
                    part = gw.at[w, piece, chunk, z] if on_x else gw.at[w, piece, x, chunk]
                else:
                    part = gw.at[w, piece, chunk] if on_x else gw.at[w, piece, :, chunk]
                if on_x:
                    target = x_right if way == 0 else x_left
                else:
                    target = z_right if way == 0 else z_left
                at_sem = ((((w * 2 + stream) * 2 + stage) * 4 + s) * 2 + way) * 2 + k
                copies[k].append(
                    remote(part, part, ring_send.at[at_sem], ring_recv.at[at_sem], (target, t))
                )
        return copies

    done = []

    def start(copies):
        for copy in copies:
            copy.start()
        done.extend(copies)
        return copies

    def arrive(copies):
        for copy in copies:
            copy.wait_recv()

    def begin(w, stream):
        new = ring_round(w, stream, 0, 0)
        start(new[0] + new[1])
        return new

    def advance(old, w, stream, stage, s):
        new = ring_round(w, stream, stage, s)
        for k in (0, 1):
            arrive(old[k])
            start(new[k])
        return new

    def assemble(w, ref):
        y_copies[w].wait_recv()
        for p in range(4):
            mine = ref[:, p * width : (p + 1) * width].astype(F32)
            other = yb[w, :, p * width : (p + 1) * width].astype(F32)
            first = jnp.where(yl == 0, mine, other)
            second = jnp.where(yl == 0, other, mine)
            gw[w, p, x, z] = jnp.concatenate([first, second], axis=0).astype(BF)

    for copy in tok_out:
        copy.start()
    tok_near.start()
    for copy in loads:
        copy.start()
    fi_load.start()
    assemble(0, up_ref)
    up_b = begin(0, 1)
    up_a = begin(0, 0)
    assemble(1, down_ref)
    down_b = begin(1, 1)
    down_a = begin(1, 0)
    up_a = advance(up_a, 0, 0, 0, 1)
    up_b = advance(up_b, 0, 1, 0, 1)
    down_b = advance(down_b, 1, 1, 0, 1)
    down_a = advance(down_a, 1, 0, 0, 1)
    up_b = advance(up_b, 0, 1, 0, 2)
    down_b = advance(down_b, 1, 1, 0, 2)
    up_b = advance(up_b, 0, 1, 0, 3)
    up_a = advance(up_a, 0, 0, 1, 0)
    down_b = advance(down_b, 1, 1, 0, 3)
    up_b = advance(up_b, 0, 1, 1, 0)
    arrive(tok_out)
    start(tok_on)
    down_a = advance(down_a, 1, 0, 1, 0)
    down_b = advance(down_b, 1, 1, 1, 0)
    up_a = advance(up_a, 0, 0, 1, 1)
    arrive(tok_on)
    start([tok_relay])
    start(fi_out)
    start([fi_near])
    down_a = advance(down_a, 1, 0, 1, 1)
    tok_load.wait()
    tok_near.wait_recv()
    tok_relay.wait_recv()
    step = min(32, quarter)

    @pl.loop(0, rows // step)
    def _(i):
        span = pl.ds(pl.multiple_of(i * step, step), step)
        values = [tk[q, span, :].astype(F32) for q in range(4)]
        mean = sum(jnp.sum(v, axis=-1, keepdims=True) for v in values) / d_model
        centers = [v - mean for v in values]
        spread = sum(jnp.sum(v * v, axis=-1, keepdims=True) for v in centers) / d_model
        inverse = lax.rsqrt(spread + EPS)
        for q in range(4):
            gain = gain_ref[q * feat : (q + 1) * feat][None, :]
            nm[span, q * feat : (q + 1) * feat] = (centers[q] * inverse * gain).astype(BF)

    up_b = advance(up_b, 0, 1, 1, 1)
    up_a = advance(up_a, 0, 0, 1, 2)
    down_b = advance(down_b, 1, 1, 1, 1)
    down_a = advance(down_a, 1, 0, 1, 2)
    ocean_prepare(f * rows - quarter, mask_ref, map_ref, taps_ref, mk, oh, wb)
    up_a = advance(up_a, 0, 0, 1, 3)
    down_a = advance(down_a, 1, 0, 1, 3)
    arrive(fi_out)
    start(fi_on)
    arrive(up_b[0] + up_b[1])
    arrive(up_a[0] + up_a[1])

    def up_block(half, block):
        span = pl.ds(pl.multiple_of(block * quarter, quarter), quarter)
        rhs = jnp.concatenate(
            [gw[0, half * 2 + k].reshape(d_model, width) for k in (0, 1)], axis=1
        )
        pre = jnp.dot(nm[span, :], rhs, preferred_element_type=F32)
        hd[half, span, :] = jax.nn.gelu(pre, approximate=True).astype(BF)

    for half in (0, 1):
        @pl.loop(0, 4)
        def _(block):
            up_block(half, block)

        if half == 0:
            arrive(fi_on)
            start([fi_relay])
    arrive(down_b[0] + down_b[1])
    arrive(down_a[0] + down_a[1])

    def partial(block, half):
        span = pl.ds(pl.multiple_of(block * quarter, quarter), quarter)
        lhs = jnp.concatenate([hd[0, span, :], hd[1, span, :]], axis=1)
        part = pl.ds(half * (xs // 2), xs // 2)
        rhs = jnp.concatenate(
            [gw[1, p, part].reshape(d_model // 2, width) for p in range(4)], axis=1
        )
        return nt_dot(lhs, rhs)

    def sums(k, half, target):
        return remote(
            sb.at[k, half], rb.at[k, half], rs_send.at[2 * k + half], rs_recv.at[2 * k + half],
            (f, target),
        )

    to_core = [sums(0, half, t_core) for half in (0, 1)]
    strip = quarter // 2
    strips = [pl.ds(h * strip, strip) for h in (0, 1)]
    far_sums = [
        far_out([sb.at[1, half, part] for part in strips], rs_hop.at[half], 8 + 4 * half)
        for half in (0, 1)
    ]
    far_sums_on = [
        far_on(
            rs_hop.at[half], lambda q, h, half=half: rb.at[1, half, strips[h]], 8 + 4 * half
        )
        for half in (0, 1)
    ]
    to_core2 = [sums(2, half, t_core) for half in (0, 1)]

    for half in (0, 1):
        sb[0, half] = partial(t_diag, half).astype(BF)
        to_core[half].start()
        acc[half] = partial(t_far, half)
        to_core[half].wait_recv()
        sb[1, half] = (acc[half] + rb[0, half].astype(F32)).astype(BF)
        start(far_sums[half])
    for half in (0, 1):
        sb[2, half] = partial(t_core, half).astype(BF)
        to_core2[half].start()
    for half in (0, 1):
        acc[half] = partial(t, half)
    for half in (0, 1):
        arrive(far_sums[half])
        start(far_sums_on[half])
    mine = pl.ds(pl.multiple_of(t * quarter, quarter), quarter)
    for half in (0, 1):
        to_core2[half].wait_recv()
        arrive(far_sums_on[half])
        for k in (0, 1):
            q = 2 * half + k
            cols = slice(k * feat, (k + 1) * feat)
            delta = acc[half, :, cols] + rb[2, half, :, cols].astype(F32) + rb[1, half, :, cols].astype(F32)
            at[q] = (tk[q, mine, :].astype(F32) + delta).astype(BF)

    at_copies = []
    for k in range(1, 4):
        q = (t + k) % 4
        at_copies.append(remote(at.at[q], ao.at[t], at_send.at[k - 1], at_recv.at[k - 1], (f, q)))
    ao[t] = at[t]

    fi_load.wait()
    fi_near.wait_recv()
    fi_relay.wait_recv()
    for copy in loads:
        copy.wait()
    pre = jnp.dot(
        jnp.concatenate([at[q] for q in range(4)], axis=1),
        fi[...].reshape(d_model, fi.shape[-1]),
        preferred_element_type=F32,
    )
    flux_hidden = jax.nn.gelu(pre, approximate=True).astype(BF)
    wn[1 + t] = jnp.dot(flux_hidden, wfo_ref[...], preferred_element_type=F32).astype(BF)
    fx_copies = []
    for k in range(1, 4):
        fx_copies.append(
            remote(wn.at[1 + t], wn.at[1 + t], fx_send.at[k - 1], fx_recv.at[k - 1], (f, (t + k) % 4))
        )
        fx_copies[-1].start()

    def rim(slot, source, target):
        return [
            remote(wn.at[source], wn.at[slot], rim_send.at[q], rim_recv.at[slot // 5], (target, q))
            for q in range(4)
        ]

    low = rim(0, 4, f_next)
    high = rim(5, 1, f_prev)

    @pl.when(t == 3)
    def _():
        for copy in low:
            copy.start()

    @pl.when(t == 0)
    def _():
        for copy in high:
            copy.start()

    for copy in fx_copies:
        copy.wait_recv()
    low[0].wait_recv()
    high[0].wait_recv()
    ocean(
        f, t, n_f, f_prev, f_next, remote, wn, sea_ref, couple_ref, sgain_ref, one_ref, two_ref,
        pick_ref, place_ref, out_ref, mk, oh, wb, st, pd, sh, cv, pk, rw, rn, halo_send, halo_recv, at_copies,
    )
    for copy in at_copies:
        copy.wait_recv()
    for q in range(4):
        atm_ref[pl.ds(q * quarter, quarter), :] = ao[q]

    @pl.when(t == 3)
    def _():
        for copy in low:
            copy.wait_send()

    @pl.when(t == 0)
    def _():
        for copy in high:
            copy.wait_send()

    for copy in y_copies + done + tok_out + [tok_near] + at_copies + fx_copies + to_core + to_core2:
        copy.wait_send()


def body(
    tokens,
    ln_gain,
    w_up,
    w_down,
    w_flux_in,
    w_flux_out,
    ocean_state,
    land_mask,
    column_map,
    w_couple,
    dw_kernel,
    ocean_gain,
    w_pw1,
    w_pw2,
):
    xs, zs = XS, ZS
    rows, feat = tokens.shape
    d_model = 4 * feat
    shard, hidden = w_up.shape
    width = hidden // 4
    fh, flx = w_flux_out.shape
    quarter = rows // 4
    grid_rows, grid_cols, chans = ocean_state.shape
    cells = grid_rows * grid_cols
    pick, place = halo_matrices(grid_rows, grid_cols)
    dma = pltpu.SemaphoreType.DMA
    vm = pl.BlockSpec(memory_space=pltpu.VMEM)
    hb = pl.BlockSpec(memory_space=pl.ANY)
    return pl.pallas_call(
        functools.partial(atmosphere_kernel, xs, zs),
        out_shape=(
            jax.ShapeDtypeStruct((rows, feat), BF),
            jax.ShapeDtypeStruct(ocean_state.shape, BF),
        ),
        in_specs=[hb, vm, vm, vm, hb, hb, hb, vm, vm, hb, vm, vm, hb, hb, hb, hb],
        out_specs=(vm, vm),
        scratch_shapes=[
            pltpu.VMEM((2, shard, hidden), BF),
            pltpu.VMEM((2, 4, xs, zs, 2 * shard, width), BF),
            pltpu.VMEM((4, rows, feat), BF),
            pltpu.VMEM((rows, d_model), BF),
            pltpu.VMEM((2, rows, hidden // 2), BF),
            pltpu.VMEM((4, feat, fh), BF),
            pltpu.VMEM((3, 2, quarter, d_model // 2), BF),
            pltpu.VMEM((3, 2, quarter, d_model // 2), BF),
            pltpu.VMEM((2, quarter, d_model // 2), F32),
            pltpu.VMEM((4, quarter, feat), BF),
            pltpu.VMEM((4, quarter, feat), BF),
            pltpu.VMEM((6, quarter, flx), BF),
            dma((2,)), dma((2,)), dma((128,)), dma((128,)),
            dma((3,)), dma((3,)), dma((3,)), dma((3,)),
            dma((6,)), dma((6,)), dma((3,)), dma((3,)),
            dma((3,)), dma((3,)), dma((4,)), dma((2,)),
            pltpu.VMEM((cells, 128), F32),
            pltpu.VMEM((cells, 6 * quarter), BF),
            pltpu.VMEM((2, 7, 7, 8, chans), F32),
            pltpu.VMEM((2, cells, chans), BF),
            pltpu.VMEM((grid_rows + 6, grid_cols + 16, chans), F32),
            pltpu.VMEM((7, grid_rows + 6, grid_cols // 8, 8, chans), F32),
            pltpu.VMEM((grid_rows, grid_cols // 8, 8, chans), F32),
            pltpu.VMEM((2, 256, chans), BF),
            pltpu.VMEM((2, 256, chans), BF),
            pltpu.VMEM((2, 2, 3 * grid_cols, chans), BF),
            dma((16,)), dma((16,)),
            pltpu.VMEM(w_flux_out.shape, BF),
            pltpu.VMEM(ocean_state.shape, BF),
            pltpu.VMEM(w_couple.shape, BF),
            pltpu.VMEM(w_pw1.shape, BF),
            pltpu.VMEM(w_pw2.shape, BF),
            pltpu.VMEM(pick.shape, BF),
            pltpu.VMEM(place.shape, BF),
            dma((9,)),
            pltpu.VMEM((2, rows // 2, feat), BF),
            pltpu.VMEM((2, feat // 2, fh), BF),
            pltpu.VMEM((2, 2, quarter // 2, d_model // 2), BF),
            dma((16,)), dma((16,)),
        ],
        compiler_params=pltpu.CompilerParams(
            collective_id=0, has_side_effects=True, vmem_limit_bytes=60 * 1024 * 1024
        ),
        name="coupled_step",
    )(
        tokens, ln_gain, w_up, w_down.T, w_flux_in, w_flux_out,
        ocean_state, land_mask, column_map, w_couple, dw_kernel.transpose(1, 2, 0, 3), ocean_gain, w_pw1, w_pw2,
        pick, place,
    )


def solution(mesh):
    placed = (
        P("fsdp", "tile"),
        P(),
        P("fsdp", "tile"),
        P("tile", "fsdp"),
        P("tile", None),
        P(),
        P("fsdp", "tile", None),
        P("fsdp", "tile"),
        P("fsdp", "tile"),
        P(),
        P(),
        P(),
        P(),
        P(),
    )
    return jax.shard_map(
        body,
        mesh=mesh,
        in_specs=placed,
        out_specs=(P("fsdp", "tile"), P("fsdp", "tile", None)),
        check_vma=False,
    )
```
